32 devices in a mesh: dp: 2 (over y), fsdp: 16 (over z, x, core).
Axes of the slice: x: 2, y: 2, z: 4, core: 2. Of those that a mesh axis runs over, the one named last changes fastest.
Arguments:
- tokens: bfloat16 [65536, 512], P(('dp', 'fsdp')), may hold values from -6 to 6
- routes: int32 [65536, 2], P(('dp', 'fsdp')), may hold values from 0 to 7, all different within a row
- lengths: int32 [64, 4], P(('dp', 'fsdp')), may hold values from 1 to 512, 1024 in all within a row
- ln1_gain: bfloat16 [512], P(('dp', 'fsdp')), may hold values from 0.5 to 1.5
- ln1_bias: bfloat16 [512], P(('dp', 'fsdp')), may hold values from -3 to 3
- w_query: bfloat16 [512, 512], P(('dp', 'fsdp')), may hold values from -0.25 to 0.25
- w_key: bfloat16 [512, 64], P(('dp', 'fsdp')), may hold values from -0.25 to 0.25
- w_value: bfloat16 [512, 64], P(('dp', 'fsdp')), may hold values from -0.25 to 0.25
- w_out: bfloat16 [512, 512], P(('dp', 'fsdp')), may hold values from -6 to 6
- w_router: bfloat16 [512, 8], P(('dp', 'fsdp')), may hold values from -0.1875 to 0.1875
- ln2_gain: bfloat16 [512], P(('dp', 'fsdp')), may hold values from 0.5 to 1.5
- ln2_bias: bfloat16 [512], P(('dp', 'fsdp')), may hold values from -3 to 3
- w_up: bfloat16 [512, 2048], P(('dp', 'fsdp')), may hold values from -0.25 to 0.25
- b_up: bfloat16 [2048], P(('dp', 'fsdp')), may hold values from -3 to 3
- w_down: bfloat16 [2048, 512], P(('dp', 'fsdp')), may hold values from -0.25 to 0.25
- b_down: bfloat16 [512], P(('dp', 'fsdp')), may hold values from -3 to 3
- cotangent: bfloat16 [65536, 512], P(('dp', 'fsdp')), may hold values from -6 to 6
Outputs:
- result: bfloat16 [65536, 512], P(('dp', 'fsdp'))
- grad_tokens: bfloat16 [65536, 512], P(('dp', 'fsdp'))
- grad_ln1_gain: float32 [512], P(('dp', 'fsdp'))
- grad_ln1_bias: float32 [512], P(('dp', 'fsdp'))
- grad_query: float32 [512, 512], P(('dp', 'fsdp'))
- grad_key: float32 [512, 64], P(('dp', 'fsdp'))
- grad_value: float32 [512, 64], P(('dp', 'fsdp'))
- grad_out: float32 [512, 512], P(('dp', 'fsdp'))
- grad_router: float32 [512, 8], P(('dp', 'fsdp'))
- grad_ln2_gain: float32 [512], P(('dp', 'fsdp'))
- grad_ln2_bias: float32 [512], P(('dp', 'fsdp'))
- grad_up: float32 [512, 2048], P(('dp', 'fsdp'))
- grad_up_bias: float32 [2048], P(('dp', 'fsdp'))
- grad_down: float32 [2048, 512], P(('dp', 'fsdp'))
- grad_down_bias: float32 [512], P(('dp', 'fsdp'))
- expert_load: float32 [8], replicated
The draws below stay inside these ranges and needn't reach their ends.
Inputs may be any that keep to these rules, and one draw needn't show every extreme that they name: `routes`: the two experts of a token differ; every expert is named by some token. Each row's lengths sum to 1024; in every row one document has exactly 512 tokens.
All inputs are finite; a program needn't handle non-finite values.
Results may differ from the reference program's by a relative error of at most 0.014.
Values may be sent and summed in bfloat16 or wider, within the bound.
No kernel may reach another device: no remote copies, remote signals or barrier semaphores. Data moves between devices by JAX's collectives and lax.ppermute only.
A program may use at most 192 MiB of HBM per device.

```python
import math
import jax
import jax.numpy as jnp
import numpy as np
from jax import lax

D = 512
FF = 2048
E = 8
HD = 64
TOP = 2
LEN = 1024
SEGS = 4
ROWS = 64
TOKENS = 65536


def steps_of(key, dims, pieces, least, high):
    level, own = 1.0, jax.random.fold_in(key, 6)
    for dim, parts in pieces:
        draws = jnp.exp(jax.random.uniform(jax.random.fold_in(own, dim), (parts,), jnp.float32, least / len(pieces), high / len(pieces)))
        level = level * jnp.repeat(draws, dims[dim] // parts).reshape([-1 if axis == dim else 1 for axis in range(len(dims))])
    return level


def distinct(rng, rows, count, top, lift):
    ranking = jax.random.permutation(jax.random.fold_in(rng, 1), count)
    boost = ranking
    for power in range(3):
        boost = boost * boost // count
    boost = boost * lift // count
    chance = jax.random.randint(jax.random.fold_in(rng, 2), (rows, count), 0, 4096) + boost
    holders = jax.random.permutation(jax.random.fold_in(rng, 3), rows)[jnp.arange(count) % rows]
    chance = jnp.where(jnp.arange(rows)[:, None] == holders[None, :], 1 << 14, chance)
    merit = chance * count + jnp.arange(count)
    return lax.top_k(merit.astype(jnp.int32), top)[1].astype(jnp.int32)


def length_profile(amount, total, limit, lean):
    weights = [(1 << 20) // math.isqrt(standing ** lean) + 1 for standing in range(2, amount + 1)]
    spare, given = total - limit - (amount - 1), [1] * (amount - 1)
    while spare > 0:
        free = [i for i in range(amount - 1) if given[i] < limit]
        pool, budget = sum([weights[i] for i in free]), spare
        for i in free:
            more = min(limit - given[i], max(1, budget * weights[i] // pool), spare)
            given[i] = given[i] + more
            spare = spare - more
    return np.array([limit] + given)


def uneven_parts(rng, count, total, limit, skew):
    if count == 2:
        one = jax.random.randint(rng, (), max(1, total - limit), min(limit, total - 1) + 1)
        return jnp.stack([one, total - one])
    sizes = jnp.asarray(length_profile(count, total, limit, skew), jnp.int32)
    pairs = (count - 1) // 2
    giver, taker = sizes[1:1 + 2 * pairs:2], sizes[2:2 + 2 * pairs:2]
    room = jnp.minimum(giver - 1, limit - taker)
    shifted = jax.random.randint(jax.random.fold_in(rng, 1), (pairs,), 0, 1 << 20) % (room + 1)
    sizes = sizes.at[1:1 + 2 * pairs:2].set(giver - shifted).at[2:2 + 2 * pairs:2].set(taker + shifted)
    return sizes[jax.random.permutation(jax.random.fold_in(rng, 2), count)]


def scatter_about(key, extent, width, limit, shards=(), held_as=jnp.bfloat16):
    values = jax.random.normal(key, extent, jnp.float32) * width
    if len(shards) > 0:
        values = steps_of(key, extent, shards, -0.22, 0.18) * values
    return jnp.clip(values, min=-limit, max=limit).astype(held_as)


def setup_inputs(seed: int = 0) -> dict:
    seeds = jax.random.split(jax.random.key(seed), 18)
    return {
        "tokens": scatter_about(seeds[0], (TOKENS, D), 1.0, 6.0, ((0, 32),)),
        "routes": distinct(seeds[1], TOKENS, E, TOP, 2048),
        "lengths": jax.vmap(lambda own: uneven_parts(own, SEGS, LEN, LEN // 2, 1))(jax.random.split(seeds[2], ROWS)).reshape((ROWS, SEGS)).astype(jnp.int32),
        "ln1_gain": jnp.clip(1.0 + 0.1 * jax.random.normal(seeds[3], (D,), jnp.float32), 0.5, 1.5).astype(jnp.bfloat16),
        "ln1_bias": scatter_about(seeds[4], (D,), 0.3, 3.0, ((0, 32),)),
        "w_query": scatter_about(seeds[5], (D, E * HD), D ** -0.5, 0.25, ((0, 32),)),
        "w_key": scatter_about(seeds[6], (D, HD), D ** -0.5, 0.25, ((0, 32),)),
        "w_value": scatter_about(seeds[7], (D, HD), D ** -0.5, 0.25, ((0, 32),)),
        "w_out": scatter_about(seeds[8], (E * HD, D), 1 ** -0.5, 6.0, ((0, 32),)),
        "w_router": scatter_about(seeds[9], (D, E), (2 * D) ** -0.5, 0.1875, ((0, 32),)),
        "ln2_gain": jnp.clip(1.0 + 0.1 * jax.random.normal(seeds[10], (D,), jnp.float32), 0.5, 1.5).astype(jnp.bfloat16),
        "ln2_bias": scatter_about(seeds[11], (D,), 0.3, 3.0, ((0, 32),)),
        "w_up": scatter_about(seeds[12], (D, FF), D ** -0.5, 0.25, ((0, 32),)),
        "b_up": scatter_about(seeds[13], (FF,), 0.5, 3.0, ((0, 32),)),
        "w_down": scatter_about(seeds[14], (FF, D), (FF // 4) ** -0.5, 0.25, ((0, 32),)),
        "b_down": scatter_about(seeds[15], (D,), 0.3, 3.0, ((0, 32),)),
        "cotangent": scatter_about(seeds[16], (TOKENS, D), 1.0, 6.0, ((0, 32),)),
    }


@jax.custom_vjp
def low(v):
    return lax.optimization_barrier(v.astype(jnp.bfloat16)).astype(jnp.float32)

@jax.custom_vjp
def low_back(v):
    return v

def low_keep(v):
    return (low(v), None)

def low_pass(kept, grad):
    return (grad,)

def back_keep(v):
    return (v, None)

def back_low(kept, grad):
    return (low(grad),)
low.defvjp(low_keep, low_pass)
low_back.defvjp(back_keep, back_low)

def matmul(left, right):
    return jnp.dot(left, right, precision=lax.Precision.HIGHEST, preferred_element_type=jnp.float32)

def layer_norm(value, gain, bias):
    center = value - lax.optimization_barrier(jnp.mean(value, -1, keepdims=True))
    spread = lax.optimization_barrier(jnp.mean(center * center, -1, keepdims=True))
    return center * lax.rsqrt(spread + 1e-05) * gain + bias

def segment_ids(lengths):
    ends = jnp.cumsum(lengths, -1).astype(jnp.int32)
    places = jnp.arange(LEN, dtype=jnp.int32)
    return lax.optimization_barrier(jnp.sum((places[None, :, None] >= ends[:, None, :]).astype(jnp.int32), -1)).astype(jnp.int32)

def attend_row(query, key_row, value_row, seg_row):
    scores = jnp.einsum('qeh,kh->eqk', query, key_row, precision=lax.Precision.HIGHEST) * HD ** (-0.5)
    scores = low_back(scores)
    same = seg_row[:, None] == seg_row[None, :]
    scores = jnp.where(same[None], scores, -1e+30)
    probs = low(jax.nn.softmax(scores, axis=-1))
    return low_back(jnp.einsum('eqk,kh->qeh', probs, value_row, precision=lax.Precision.HIGHEST))

def layer(params, inputs, route_rows, seg_rows):
    g_one, b_one, wq, wk, wv, wo, wr, g_two, b_two, wu, bu, wd, bd = params
    count_rows = seg_rows.shape[0]
    total = inputs.shape[0]
    hidden = low(layer_norm(inputs, g_one, b_one))
    query = low(low_back(matmul(hidden, wq)))
    keys = low(low_back(matmul(hidden, wk)))
    values = low(low_back(matmul(hidden, wv)))
    logits = low_back(matmul(hidden, wr))
    probs = jax.nn.softmax(logits, axis=-1)
    picked = lax.optimization_barrier(jnp.sum((route_rows[:, :, None] == jnp.arange(E, dtype=jnp.int32)[None, None, :]).astype(jnp.float32), 1))
    gates = probs * picked
    heads = jax.vmap(jax.checkpoint(attend_row))(query.reshape(count_rows, LEN, E, HD), keys.reshape(count_rows, LEN, HD), values.reshape(count_rows, LEN, HD), seg_rows)
    heads = heads.reshape(total, E, HD)
    mixed = low(low_back(heads * gates[:, :, None])).reshape(total, E * HD)
    after = inputs + low_back(matmul(mixed, wo))
    second = low(layer_norm(after, g_two, b_two))
    inner = low_back(matmul(second, wu) + bu)
    active = low(jax.nn.gelu(inner))
    return after + matmul(active, wd) + bd

def reference(tokens, routes, lengths, ln1_gain, ln1_bias, w_query, w_key, w_value, w_out, w_router, ln2_gain, ln2_bias, w_up, b_up, w_down, b_down, cotangent):
    params = tuple((p.astype(jnp.float32) for p in (ln1_gain, ln1_bias, w_query, w_key, w_value, w_out, w_router, ln2_gain, ln2_bias, w_up, b_up, w_down, b_down)))
    seg = segment_ids(lengths)
    group = math.gcd(ROWS, max(1, 4096 // LEN))
    steps_count = ROWS // group
    inputs = tokens.astype(jnp.float32).reshape(steps_count, group * LEN, D)
    route_groups = routes.reshape(steps_count, group * LEN, TOP)
    seg_groups = seg.reshape(steps_count, group, LEN)
    cot_groups = cotangent.astype(jnp.float32).reshape(steps_count, group * LEN, D)

    def advance(totals, item):
        xin, rin, sin, cin = item
        out, pull = jax.vjp(lambda p, v: layer(p, v, rin, sin), params, xin)
        grad_params, grad_in = pull(cin)
        totals = jax.tree.map(jnp.add, totals, grad_params)
        return (totals, (out.astype(jnp.bfloat16), grad_in.astype(jnp.bfloat16)))
    zeros = jax.tree.map(jnp.zeros_like, params)
    totals, (outs, grads_in) = lax.scan(advance, zeros, (inputs, route_groups, seg_groups, cot_groups))
    counts = lax.optimization_barrier(jnp.sum((routes[:, :, None] == jnp.arange(E, dtype=jnp.int32)[None, None, :]).astype(jnp.float32), (0, 1)))
    load = counts / TOKENS
    return (outs.reshape(TOKENS, D), grads_in.reshape(TOKENS, D), totals[0], totals[1], totals[2], totals[3], totals[4], totals[5], totals[6], totals[7], totals[8], totals[9], totals[10], totals[11], totals[12], load)
```

```python
import functools

import jax
import jax.numpy as jnp
from jax import lax
from jax.experimental import pallas as pl
from jax.experimental.pallas import tpu as pltpu
from jax.sharding import PartitionSpec as P

AXES = ("dp", "fsdp")
F32 = jnp.float32
BF = jnp.bfloat16
FAR = -1e30
LANES = 128
G1, B1, G2, B2, BD, BU, LOAD = 8, 9, 10, 11, 12, 13, 17
TILE = 256
VMEM = 56 * 1024 * 1024


def nn(left, right):
    return jnp.dot(left, right, preferred_element_type=F32)


def nt(left, right):
    return lax.dot_general(left, right, (((1,), (1,)), ((), ())), preferred_element_type=F32)


def iota(shape, dim):
    return lax.broadcasted_iota(jnp.int32, shape, dim)


def normed(value):
    center = value - jnp.mean(value, -1, keepdims=True)
    inv = lax.rsqrt(jnp.mean(center * center, -1, keepdims=True) + 1e-05)
    return center * inv, inv


def fetch(me, pieces, codes, block, dst, sem):
    for piece, own in zip(pieces, codes):
        for place, code in enumerate(own):
            at = pl.multiple_of(jnp.bitwise_xor(me, code) * block, block)
            pltpu.make_async_copy(piece.at[place], dst.at[pl.ds(at, block), :], sem).start()


def arrive(dst, sem):
    pltpu.make_async_copy(dst, dst, sem).wait()


def scatter(me, pieces, codes, block, src, sem):
    for piece, own in zip(pieces, codes):
        for place, code in enumerate(own):
            at = pl.multiple_of(jnp.bitwise_xor(me, code) * block, block)
            pltpu.make_async_copy(src.at[pl.ds(at, block), :], piece.at[place], sem).start()


def split3(value):
    high = value.astype(BF).astype(F32)
    rest = value - high
    mid = rest.astype(BF).astype(F32)
    return high, mid, rest - mid


def segment_of(lens, row, start, rows):
    place = iota((rows, LANES), 0) + start
    end = lens[row, 0]
    seg = (place >= end).astype(jnp.int32)
    for j in range(1, lens.shape[1]):
        end = end + lens[row, j]
        seg = seg + (place >= end).astype(jnp.int32)
    return seg


def pick(routes, rows, slot):
    return jnp.broadcast_to(routes[rows, slot : slot + 1], (TILE, LANES))


def chosen(wide, expert, half):
    out = jnp.zeros(expert.shape, F32)
    for j in range(wide.shape[1] // LANES):
        out = jnp.where(expert == 2 * j + half, wide[:, j * LANES : (j + 1) * LANES], out)
    return out


def forward_kernel(n_pieces, codes, block, experts, me, lens, tok, routes, *refs):
    pieces = refs[:n_pieces]
    hid_o, qx_o, kv_o, pr_o, o_o, u_o, x1_o, h2_o, vec_o, w, kx, vx, vec, sem = refs[n_pieces:]
    length, depth = tok.shape
    segs = lens.shape[1]
    row = pl.program_id(0)

    @pl.when(row == 0)
    def _():
        fetch(me[0], pieces, codes, block, w, sem)
        arrive(w, sem)
        vec[...] = w[:, 2 * depth + LANES :].astype(F32).T
        vec_o[...] = vec[0:32, :]

    lane = iota((TILE, LANES), 1)
    half = lane // 64
    low = lane < 64

    def first(c, _):
        rows = pl.ds(pl.multiple_of(c * TILE, TILE), TILE)
        unit, _ = normed(tok[rows, :].astype(F32))
        hid = (unit * vec[G1 : G1 + 1, :] + vec[B1 : B1 + 1, :]).astype(BF)
        hid_o[rows, :] = hid
        query = nn(hid, w[:, 0:depth])
        small = nn(hid, w[:, 2 * depth :])
        kv = small[:, :LANES].astype(BF)
        kv_o[rows, :] = kv
        kv = kv.astype(F32)
        swap = pltpu.roll(kv, 64, 1)
        seg = segment_of(lens, row, c * TILE, TILE)
        same = jnp.where(lane == seg, 1.0, 0.0)
        kx[rows, 0:LANES] = jnp.where(low, kv, swap).astype(BF)
        kx[rows, LANES:] = jnp.where(lane < segs, same, jnp.where(lane < 8, 1.0, 0.0)).astype(BF)
        vx[rows, 0:LANES] = jnp.where(low, swap, kv).astype(BF)
        vx[rows, LANES:] = jnp.ones((TILE, LANES), BF)
        logits = jnp.where(lane < experts, small[:, LANES:], FAR)
        raised = jnp.exp(logits - jnp.max(logits, -1, keepdims=True))
        pr_o[rows, :] = raised / jnp.sum(raised, -1, keepdims=True)
        apart = jnp.where(lane < segs, (1.0 - same) * FAR, 0.0)
        for slot in range(2):
            mine = chosen(query, pick(routes, rows, slot), half)
            qx_o[slot, rows, 0:LANES] = (mine * 0.125).astype(BF)
            qx_o[slot, rows, LANES:] = apart.astype(BF)
        return 0

    lax.fori_loop(0, length // TILE, first, 0)

    def second(c, _):
        rows = pl.ds(pl.multiple_of(c * TILE, TILE), TILE)
        probs = pr_o[rows, :]
        seen, gated, experts_of = [], [], []
        for slot in range(2):
            expert = pick(routes, rows, slot)
            scores = nt(qx_o[slot, rows, :], kx[...])
            top = jnp.max(scores, -1, keepdims=True)
            raised = jnp.exp(scores - top).astype(BF)
            both = nn(raised, vx[...])
            mass = both[:, LANES:]
            out = both[:, :LANES] / mass
            high, mid, rest = split3(top + jnp.log(mass))
            feats = qx_o[slot, rows, LANES:].astype(F32)
            feats = jnp.where(lane == 4, -high, jnp.where(lane == 5, -mid, jnp.where(lane == 6, -rest, feats)))
            qx_o[slot, rows, LANES:] = feats.astype(BF)
            gate = jnp.sum(jnp.where(lane == expert, probs, 0.0), -1, keepdims=True)
            seen.append(out)
            gated.append(out * gate)
            experts_of.append(expert)
        o_o[rows, :] = jnp.where(low, seen[0], seen[1])
        for j in range(depth // LANES):
            part = jnp.where(experts_of[0] == 2 * j + half, gated[0], jnp.where(experts_of[1] == 2 * j + half, gated[1], 0.0))
            u_o[rows, j * LANES : (j + 1) * LANES] = part.astype(BF)
        after = tok[rows, :].astype(F32) + nn(u_o[rows, :], w[:, depth : 2 * depth])
        x1_o[rows, :] = after
        unit, _ = normed(after)
        h2_o[rows, :] = (unit * vec[G2 : G2 + 1, :] + vec[B2 : B2 + 1, :]).astype(BF)
        return 0

    lax.fori_loop(0, length // TILE, second, 0)


def ffn_kernel(n_pieces, n_out, codes, out_codes, block, me, h2, dy, vec, *refs):
    pieces = refs[:n_pieces]
    act_o, dz_o, bias_o = refs[n_pieces : n_pieces + 3]
    grads = refs[n_pieces + 3 : n_pieces + 3 + n_out]
    w, ht, yt, up_acc, down_acc, out, sem, out_sem = refs[n_pieces + 3 + n_out :]
    sub, t = pl.program_id(0), pl.program_id(1)
    subs, tiles = pl.num_programs(0), pl.num_programs(1)
    span, depth = act_o.shape[0], h2.shape[1]
    width = act_o.shape[1]

    @pl.when((sub == 0) & (t == 0))
    def _():
        fetch(me[0], pieces, codes, block, w, sem)
        ht[depth:, :] = jnp.ones((16, ht.shape[1]), BF)
        arrive(w, sem)

    start = pl.multiple_of(t * span, span)

    @pl.when(sub == 0)
    def _():
        ht[0:depth, pl.ds(start, span)] = h2[pl.ds(start, span), :].T
        yt[:, pl.ds(start, span)] = dy[pl.ds(start, span), :].T

    here = pl.ds(pl.multiple_of(sub * width, width), width)
    there = pl.ds(pl.multiple_of((subs + sub) * width, width), width)
    bias = vec[pl.ds(BU + sub, 1), :]
    one = 0.7978845608028654
    two = one * 0.044715
    for c in range(span // TILE):
        rows = pl.ds(pl.multiple_of(start + c * TILE, TILE), TILE)
        own = slice(c * TILE, (c + 1) * TILE)
        z = nn(h2[rows, :], w[:, here]) + bias
        dact = nt(dy[rows, :], w[:, there])
        square = z * z
        tanh = jnp.tanh(z * (one + two * square))
        part = 0.5 * tanh + 0.5
        act = z * part
        slope = part + act * (1.0 - tanh) * (one + 3.0 * two * square)
        act_o[own, :] = act.astype(BF)
        dz_o[own, :] = (dact * slope).astype(BF)
    up = nn(ht[:, pl.ds(start, span)], dz_o[...])
    down = nn(yt[:, pl.ds(start, span)], act_o[...])

    @pl.when(t == 0)
    def _():
        up_acc[...] = up
        down_acc[...] = down

    @pl.when(t > 0)
    def _():
        up_acc[...] += up
        down_acc[...] += down

    @pl.when(t == tiles - 1)
    def _():
        out[:, here] = up_acc[0:depth, :].astype(BF)
        out[:, there] = down_acc[...].T.astype(BF)
        bias_o[pl.ds(sub, 1), :] = up_acc[depth : depth + 1, :]

    @pl.when((t == tiles - 1) & (sub == subs - 1))
    def _():
        scatter(me[0], grads, out_codes, block, out, out_sem)
        arrive(out, out_sem)


def backward_kernel(
    n_w, n_f, n_out, codes, f_codes, out_codes, block, experts,
    me, lens, dz, dy, x1, routes, hid, qx, kv, pr, o, u, vec, bias, *refs
):
    w_pieces = refs[:n_w]
    f_pieces = refs[n_w : n_w + n_f]
    dx1_o, dq_o, ds_o = refs[n_w + n_f : n_w + n_f + 3]
    grads = refs[n_w + n_f + 3 : n_w + n_f + 3 + n_out]
    (w, wu, kx, vx, dax, dk, dv, gq, gs, go, sums, loads, out, sem, f_sem, out_sem) = refs[n_w + n_f + 3 + n_out :]
    length, depth = dy.shape
    segs = lens.shape[1]
    row = pl.program_id(0)

    @pl.when(row == 0)
    def _():
        fetch(me[0], w_pieces, codes, block, w, sem)
        fetch(me[0], [piece.at[:, :, 0 : wu.shape[1]] for piece in f_pieces], f_codes, block, wu, f_sem)
        gq[...] = jnp.zeros_like(gq)
        gs[...] = jnp.zeros_like(gs)
        go[...] = jnp.zeros_like(go)
        sums[...] = jnp.zeros_like(sums)
        loads[...] = jnp.zeros_like(loads)
        arrive(w, sem)
        arrive(wu, f_sem)

    lane = iota((TILE, LANES), 1)
    half = lane // 64
    low = lane < 64
    dk[...] = jnp.zeros_like(dk)
    dv[...] = jnp.zeros_like(dv)

    def first(c, _):
        rows = pl.ds(pl.multiple_of(c * TILE, TILE), TILE)
        dh2 = nt(dz[rows, :], wu[...])
        unit, inv = normed(x1[rows, :])
        grad = dy[rows, :].astype(F32)
        sums[G2 : G2 + 1, :] += jnp.sum(dh2 * unit, 0, keepdims=True)
        sums[B2 : B2 + 1, :] += jnp.sum(dh2, 0, keepdims=True)
        sums[BD : BD + 1, :] += jnp.sum(grad, 0, keepdims=True)
        scaled = dh2 * vec[G2 : G2 + 1, :]
        one = jnp.mean(scaled, -1, keepdims=True)
        two = jnp.mean(scaled * unit, -1, keepdims=True)
        dx1 = grad + inv * (scaled - one - unit * two)
        dx1_o[rows, :] = dx1
        dx1 = dx1.astype(BF)
        go[...] += nn(u[rows, :].T, dx1)
        du = nt(dx1, w[:, depth : 2 * depth]).astype(BF).astype(F32)
        probs = pr[rows, :]
        heads = o[rows, :]
        swap = pltpu.roll(heads, 64, 1)
        dprobs = jnp.zeros((TILE, LANES), F32)
        for slot in range(2):
            expert = pick(routes, rows, slot)
            own = chosen(du, expert, half)
            here = lane == expert
            gate = jnp.sum(jnp.where(here, probs, 0.0), -1, keepdims=True)
            seen = jnp.where(low, heads, swap) if slot == 0 else jnp.where(low, swap, heads)
            dgate = jnp.sum(own * seen, -1, keepdims=True)
            da = (own * gate).astype(BF)
            high, mid, rest = split3(jnp.sum(da.astype(F32) * seen, -1, keepdims=True))
            dax[slot, rows, 0:LANES] = da
            feats = jnp.where(lane == 4, -high, jnp.where(lane == 5, -mid, jnp.where(lane == 6, -rest, 0.0)))
            dax[slot, rows, LANES:] = feats.astype(BF)
            dprobs = jnp.where(here, dgate, dprobs)
            loads[0:1, :] += jnp.sum(jnp.where(here, 1.0, 0.0), 0, keepdims=True)
        inner = jnp.sum(dprobs * probs, -1, keepdims=True)
        ds_o[rows, LANES:] = (probs * (dprobs - inner)).astype(BF)
        both = kv[rows, :].astype(F32)
        swap = pltpu.roll(both, 64, 1)
        seg = segment_of(lens, row, c * TILE, TILE)
        feats = jnp.where(lane < segs, jnp.where(lane == seg, 1.0, 0.0), jnp.where(lane < 8, 1.0, 0.0)).astype(BF)
        kx[rows, 0:LANES] = jnp.where(low, both, swap).astype(BF)
        kx[rows, LANES:] = feats
        vx[rows, 0:LANES] = jnp.where(low, swap, both).astype(BF)
        vx[rows, LANES:] = feats
        return 0

    lax.fori_loop(0, length // TILE, first, 0)

    def second(c, _):
        rows = pl.ds(pl.multiple_of(c * TILE, TILE), TILE)
        found = []
        for slot in range(2):
            probs = jnp.exp(nt(qx[slot, rows, :], kx[...]))
            away = nt(dax[slot, rows, :], vx[...])
            ds = (probs * away).astype(BF)
            found.append(nn(ds, kx[:, 0:LANES]) * 0.125)
            dk[...] += nn(qx[slot, rows, 0:LANES].T, ds)
            dv[...] += nn(dax[slot, rows, 0:LANES].T, probs.astype(BF))
        one, two = pick(routes, rows, 0), pick(routes, rows, 1)
        for j in range(depth // LANES):
            part = jnp.where(one == 2 * j + half, found[0], jnp.where(two == 2 * j + half, found[1], 0.0))
            dq_o[rows, j * LANES : (j + 1) * LANES] = part.astype(BF)
        return 0

    lax.fori_loop(0, length // TILE, second, 0)

    def third(c, _):
        rows = pl.ds(pl.multiple_of(c * TILE, TILE), TILE)
        both = jnp.concatenate([dk[0:64, rows] + dk[64:, rows], dv[0:64, rows] + dv[64:, rows]], 0)
        ds_o[rows, 0:LANES] = both.T.astype(BF)
        turned = jnp.concatenate([hid[rows, :].T, jnp.ones((16, TILE), BF)], 0)
        gq[...] += nn(turned, dq_o[rows, :])
        gs[...] += nn(turned, ds_o[rows, :])
        return 0

    lax.fori_loop(0, length // TILE, third, 0)

    @pl.when(row == pl.num_programs(0) - 1)
    def _():
        sums[BU : BU + 4, :] = bias[0:4, :]
        wq = w[:, 0:depth].astype(F32)
        ws = w[:, 2 * depth :].astype(F32)
        wide = iota((depth, LANES), 1)
        ws_own = jnp.where(wide < experts, ws[:, LANES:], 0.0)
        around = jnp.sum(gq[0:depth, :] * wq, -1, keepdims=True)
        around += jnp.sum(gs[0:depth, 0:LANES] * ws[:, 0:LANES] + gs[0:depth, LANES:] * ws_own, -1, keepdims=True)
        shift = jnp.sum(gq[depth : depth + 1, :] * wq, -1, keepdims=True)
        shift += jnp.sum(
            gs[depth : depth + 1, 0:LANES] * ws[:, 0:LANES] + gs[depth : depth + 1, LANES:] * ws_own, -1, keepdims=True
        )
        gain = ws[:, LANES + G1 : LANES + G1 + 1]
        lift = ws[:, LANES + B1 : LANES + B1 + 1]
        stretch = (around - lift * shift) / gain
        place = lax.rem(iota((depth, LANES), 0), block)
        load = jnp.sum(jnp.where(wide == place, loads[0:1, :], 0.0), -1, keepdims=True)
        columns = jnp.where(wide < experts, gs[0:depth, LANES:], sums[...].T)
        columns = jnp.where(wide == G1, stretch, columns)
        columns = jnp.where(wide == B1, shift, columns)
        columns = jnp.where(wide == LOAD, load, columns)
        out[:, 0:depth] = gq[0:depth, :].astype(BF)
        out[:, depth : 2 * depth] = go[...].astype(BF)
        out[:, 2 * depth : 2 * depth + LANES] = gs[0:depth, 0:LANES].astype(BF)
        out[:, 2 * depth + LANES :] = columns.astype(BF)
        scatter(me[0], grads, out_codes, block, out, out_sem)
        arrive(out, out_sem)


def last_kernel(
    n_w, n_f, codes, f_codes, block, me, act, x1, dx1, dq, ds, tok, vec, *refs
):
    w_pieces = refs[:n_w]
    f_pieces = refs[n_w : n_w + n_f]
    res_o, grad_o, w, wd, sem, f_sem = refs[n_w + n_f :]
    depth = tok.shape[1]

    @pl.when(pl.program_id(0) == 0)
    def _():
        fetch(me[0], w_pieces, codes, block, w, sem)
        fetch(me[0], [piece.at[:, :, wd.shape[1] :] for piece in f_pieces], f_codes, block, wd, f_sem)
        arrive(w, sem)
        lane = iota((depth, LANES), 1)
        own = w[:, 2 * depth + LANES :].astype(F32)
        w[:, 2 * depth + LANES :] = jnp.where(lane < G1, own, 0.0).astype(BF)
        arrive(wd, f_sem)

    out = x1[...] + vec[BD : BD + 1, :]
    for at in range(0, wd.shape[1], depth):
        out = out + nn(act[:, at : at + depth], wd[:, at : at + depth])
    res_o[...] = out.astype(BF)
    dh = nt(dq[...], w[:, 0:depth]) + nt(ds[...], w[:, 2 * depth :])
    unit, inv = normed(tok[...].astype(F32))
    scaled = dh * vec[G1 : G1 + 1, :]
    one = jnp.mean(scaled, -1, keepdims=True)
    two = jnp.mean(scaled * unit, -1, keepdims=True)
    grad_o[...] = (dx1[...] + inv * (scaled - one - unit * two)).astype(BF)


def xor_pairs(count, mask):
    return [(i, i ^ mask) for i in range(count)]


def hops(dp, fsdp):
    inner = fsdp.bit_length() - 1
    masks = [1 << bit for bit in range(inner - 1, 0, -1)]
    masks += [1 << (inner + bit) for bit in range(dp.bit_length() - 1)]
    if fsdp > 1:
        masks.append(1)
    return masks


def layout(masks):
    own = [0]
    for mask in masks[:-1]:
        own = own + [code ^ mask for code in own]
    if not masks:
        return [own]
    return [own, [code ^ masks[-1] for code in own]]


def gather(share, masks, count):
    held = share[None]
    for mask in masks[:-1]:
        held = jnp.concatenate([held, lax.ppermute(held, AXES, xor_pairs(count, mask))], 0)
    if not masks:
        return [held]
    return [held, lax.ppermute(held, AXES, xor_pairs(count, masks[-1]))]


def reduce(pieces, masks, count):
    if not masks:
        return pieces[0][0].astype(F32)
    keep, send = pieces
    for step, mask in enumerate(reversed(masks)):
        got = lax.ppermute(send, AXES, xor_pairs(count, mask))
        total = keep.astype(F32) + got.astype(F32)
        if step == len(masks) - 1:
            return total[0]
        half = total.shape[0] // 2
        keep, send = total[:half].astype(BF), total[half:].astype(BF)


def on_device(
    sizes, tokens, routes, lengths, ln1_gain, ln1_bias, w_query, w_key, w_value, w_out, w_router,
    ln2_gain, ln2_bias, w_up, b_up, w_down, b_down, cotangent
):
    dp, fsdp = sizes
    count = dp * fsdp
    total, depth = tokens.shape
    rows = lengths.shape[0]
    length = total // rows
    experts, head = w_router.shape[1], w_key.shape[1]
    share = w_query.shape[0]
    inner = w_up.shape[1]
    subs = inner // depth
    width = depth
    fast = share % 16 == 0
    me = (lax.axis_index(AXES) if fast else jnp.int32(0)).astype(jnp.int32).reshape(1)
    small = jnp.concatenate(
        [w_query, w_out, w_key, w_value, w_router]
        + [v[:, None] for v in (ln1_gain, ln1_bias, ln2_gain, ln2_bias, b_down)]
        + [b_up.reshape(subs, share).T],
        1,
    )
    first_width = 2 * depth + 2 * LANES
    small = jnp.pad(small, ((0, 0), (0, first_width - small.shape[1])))
    large = jnp.concatenate(
        [
            w_up.reshape(share, count, subs, share).transpose(0, 2, 1, 3).reshape(share, inner),
            w_down.reshape(subs, share, depth).transpose(1, 0, 2).reshape(share, inner),
        ],
        1,
    )
    if fast:
        masks = hops(dp, fsdp)
        block = share
        codes = layout(masks)
        w_pieces = gather(small, masks, count)
        f_pieces = gather(large, masks, count)
    else:
        masks = []
        block = depth
        codes = [[0]]
        w_pieces = [lax.all_gather(small, AXES, axis=0, tiled=True)[None]]
        f_pieces = [lax.all_gather(large, AXES, axis=0, tiled=True)[None]]
    n = len(w_pieces)
    blocks = len(codes[0])

    smem = pl.BlockSpec(memory_space=pltpu.SMEM)
    hbm = pl.BlockSpec(memory_space=pl.ANY)

    def whole(shape):
        return pl.BlockSpec(shape, lambda *_: (0,) * len(shape))

    def by_row(wide):
        return pl.BlockSpec((length, wide), lambda r: (r, 0))

    def shape(dims, dtype):
        return jax.ShapeDtypeStruct(dims, dtype)

    params = pltpu.CompilerParams(vmem_limit_bytes=VMEM)
    twice = pl.BlockSpec((2, length, 2 * LANES), lambda r: (0, r, 0))
    hid, qx, kv, pr, o, u, x1, h2, vec = pl.pallas_call(
        functools.partial(forward_kernel, n, codes, block, experts),
        grid=(rows,),
        in_specs=[smem, smem, by_row(depth), by_row(2)] + [hbm] * n,
        out_specs=[
            by_row(depth), twice, by_row(LANES), by_row(LANES), by_row(LANES), by_row(depth), by_row(depth), by_row(depth),
            whole((32, depth)),
        ],
        out_shape=[
            shape((total, depth), BF),
            shape((2, total, 2 * LANES), BF),
            shape((total, LANES), BF),
            shape((total, LANES), F32),
            shape((total, LANES), F32),
            shape((total, depth), BF),
            shape((total, depth), F32),
            shape((total, depth), BF),
            shape((32, depth), F32),
        ],
        scratch_shapes=[
            pltpu.VMEM((depth, first_width), BF),
            pltpu.VMEM((length, 2 * LANES), BF),
            pltpu.VMEM((length, 2 * LANES), BF),
            pltpu.VMEM((LANES, depth), F32),
            pltpu.SemaphoreType.DMA,
        ],
        compiler_params=params,
        name="attend",
    )(me, lengths, tokens, routes, *w_pieces)

    span = min(1024, total)
    act, dz, bias, *f_grads = pl.pallas_call(
        functools.partial(ffn_kernel, n, n, codes, codes, block),
        grid=(subs, total // span),
        in_specs=[smem, whole((total, depth)), whole((total, depth)), whole((32, depth))] + [hbm] * n,
        out_specs=[
            pl.BlockSpec((span, width), lambda s, t: (t, s)),
            pl.BlockSpec((span, width), lambda s, t: (t, s)),
            whole((8, depth)),
        ]
        + [hbm] * n,
        out_shape=[
            shape((total, inner), BF),
            shape((total, inner), BF),
            shape((8, depth), F32),
        ]
        + [shape((blocks, block, 2 * inner), BF)] * n,
        scratch_shapes=[
            pltpu.VMEM((depth, 2 * inner), BF),
            pltpu.VMEM((depth + 16, total), BF),
            pltpu.VMEM((depth, total), BF),
            pltpu.VMEM((depth + 16, width), F32),
            pltpu.VMEM((depth, width), F32),
            pltpu.VMEM((depth, 2 * inner), BF),
            pltpu.SemaphoreType.DMA,
            pltpu.SemaphoreType.DMA,
        ],
        compiler_params=params,
        name="feed",
    )(me, h2, cotangent, vec, *f_pieces)

    dx1, dq, ds, *w_grads = pl.pallas_call(
        functools.partial(backward_kernel, n, n, n, codes, codes, codes, block, experts),
        grid=(rows,),
        in_specs=[
            smem, smem, by_row(inner), by_row(depth), by_row(depth), by_row(2), by_row(depth), twice,
            by_row(LANES), by_row(LANES), by_row(LANES), by_row(depth), whole((32, depth)), whole((8, depth)),
        ]
        + [hbm] * (2 * n),
        out_specs=[by_row(depth), by_row(depth), by_row(2 * LANES)] + [hbm] * n,
        out_shape=[shape((total, depth), F32), shape((total, depth), BF), shape((total, 2 * LANES), BF)]
        + [shape((blocks, block, first_width), BF)] * n,
        scratch_shapes=[
            pltpu.VMEM((depth, first_width), BF),
            pltpu.VMEM((depth, inner), BF),
            pltpu.VMEM((length, 2 * LANES), BF),
            pltpu.VMEM((length, 2 * LANES), BF),
            pltpu.VMEM((2, length, 2 * LANES), BF),
            pltpu.VMEM((LANES, length), F32),
            pltpu.VMEM((LANES, length), F32),
            pltpu.VMEM((depth + 16, depth), F32),
            pltpu.VMEM((depth + 16, 2 * LANES), F32),
            pltpu.VMEM((depth, depth), F32),
            pltpu.VMEM((LANES, depth), F32),
            pltpu.VMEM((8, LANES), F32),
            pltpu.VMEM((depth, first_width), BF),
            pltpu.SemaphoreType.DMA,
            pltpu.SemaphoreType.DMA,
            pltpu.SemaphoreType.DMA,
        ],
        compiler_params=params,
        name="back",
    )(me, lengths, dz, cotangent, x1, routes, hid, qx, kv, pr, o, u, vec, bias, *w_pieces, *f_pieces)

    part = min(512, total)

    def by_part(wide):
        return pl.BlockSpec((part, wide), lambda t: (t, 0))

    result, grad_tokens = pl.pallas_call(
        functools.partial(last_kernel, n, n, codes, codes, block),
        grid=(total // part,),
        in_specs=[
            smem,
            by_part(inner), by_part(depth), by_part(depth), by_part(depth), by_part(2 * LANES), by_part(depth), whole((32, depth)),
        ]
        + [hbm] * (2 * n),
        out_specs=[by_part(depth), by_part(depth)],
        out_shape=[shape((total, depth), BF), shape((total, depth), BF)],
        scratch_shapes=[
            pltpu.VMEM((depth, first_width), BF),
            pltpu.VMEM((depth, inner), BF),
            pltpu.SemaphoreType.DMA,
            pltpu.SemaphoreType.DMA,
        ],
        compiler_params=params,
        name="close",
    )(me, act, x1, dx1, dq, ds, tokens, vec, *w_pieces, *f_pieces)

    if fast:
        own_f = reduce(f_grads, masks, count)
        own_w = reduce(w_grads, masks, count)
    else:
        own_f = lax.psum_scatter(f_grads[0][0].astype(F32), AXES, scatter_dimension=0, tiled=True)
        own_w = lax.psum_scatter(w_grads[0][0].astype(F32), AXES, scatter_dimension=0, tiled=True)
        load = lax.psum(w_grads[0][0][:experts, 2 * depth + LANES + LOAD].astype(F32), AXES)
    extra = own_w[:, 2 * depth + LANES :]
    if fast:
        load = extra[:experts, LOAD]
    grad_up = own_f[:, :inner].reshape(share, subs, count, share).transpose(0, 2, 1, 3).reshape(share, inner)
    grad_down = own_f[:, inner:].reshape(share, subs, depth).transpose(1, 0, 2).reshape(subs * share, depth)
    return (
        result,
        grad_tokens,
        extra[:, G1],
        extra[:, B1],
        own_w[:, 0:depth],
        own_w[:, 2 * depth : 2 * depth + head],
        own_w[:, 2 * depth + head : 2 * depth + 2 * head],
        own_w[:, depth : 2 * depth],
        extra[:, 0:experts],
        extra[:, G2],
        extra[:, B2],
        grad_up,
        extra[:, BU : BU + subs].T.reshape(subs * share),
        grad_down,
        extra[:, BD],
        load / (total * count),
    )


def solution(mesh):
    over = P(AXES)
    flat = P(AXES, None)
    sizes = (mesh.shape["dp"], mesh.shape["fsdp"])
    return jax.shard_map(
        functools.partial(on_device, sizes),
        mesh=mesh,
        in_specs=(
            flat, flat, flat, over, over, flat, flat, flat, flat, flat, over, over, flat, over, flat, over, flat,
        ),
        out_specs=(
            flat, flat, over, over, flat, flat, flat, flat, flat, over, over, flat, over, flat, over, P(),
        ),
        check_vma=False,
    )
```

```python
import functools

import jax
import jax.numpy as jnp
from jax import lax
from jax.experimental import pallas as pl
from jax.experimental.pallas import tpu as pltpu
from jax.sharding import PartitionSpec as P

AXES = ("dp", "fsdp")
F32 = jnp.float32
BF = jnp.bfloat16
FAR = -1e30
LANES = 128
G1, B1, G2, B2, BD, BU, LOAD = 8, 9, 10, 11, 12, 13, 17
TILE = 256
STEP = 512
VMEM = 56 * 1024 * 1024


def nn(left, right):
    return jnp.dot(left, right, preferred_element_type=F32)


def nt(left, right):
    return lax.dot_general(left, right, (((1,), (1,)), ((), ())), preferred_element_type=F32)


def iota(shape, dim):
    return lax.broadcasted_iota(jnp.int32, shape, dim)


def normed(value):
    center = value - jnp.mean(value, -1, keepdims=True)
    inv = lax.rsqrt(jnp.mean(center * center, -1, keepdims=True) + 1e-05)
    return center * inv, inv


def fetch(me, pieces, block, parts, sem):
    for piece, codes in pieces:
        for place, code in enumerate(codes):
            own = jnp.bitwise_xor(me, code) * block
            for start, wide, dst, row, column in parts:
                at = pl.multiple_of(own + row, 16)
                pltpu.make_async_copy(
                    piece.at[place, :, start : start + wide], dst.at[pl.ds(at, block), column : column + wide], sem
                ).start()


def arrive(dst, sem):
    pltpu.make_async_copy(dst, dst, sem).wait()


def scatter(me, pieces, block, src, start, sem):
    for piece, codes in pieces:
        wide = piece.shape[2]
        for place, code in enumerate(codes):
            at = pl.multiple_of(jnp.bitwise_xor(me, code) * block, 16)
            pltpu.make_async_copy(src.at[pl.ds(at, block), start : start + wide], piece.at[place], sem).start()


def ffn_parts(wu, wd, half, depth, up, down):
    parts = []
    if up:
        parts.append((0, 2 * depth, wu, 0, half * 2 * depth))
    if down:
        parts += [((2 + j) * depth, depth, wd, (2 * half + j) * depth, 0) for j in range(2)]
    return parts


def split3(value):
    high = value.astype(BF).astype(F32)
    rest = value - high
    mid = rest.astype(BF).astype(F32)
    return high, mid, rest - mid


def three(lane, value):
    high, mid, rest = split3(value)
    return jnp.where(lane == 4, -high, jnp.where(lane == 5, -mid, jnp.where(lane == 6, -rest, 0.0)))


def segment_of(lens, row, start, rows):
    place = iota((rows, LANES), 0) + start
    end = lens[row, 0]
    seg = (place >= end).astype(jnp.int32)
    for j in range(1, lens.shape[1]):
        end = end + lens[row, j]
        seg = seg + (place >= end).astype(jnp.int32)
    return seg


def pick(routes, rows, slot):
    return jnp.broadcast_to(routes[rows, slot : slot + 1], (TILE, LANES))


def chosen(wide, expert, half):
    out = jnp.zeros(expert.shape, F32)
    for j in range(wide.shape[1] // LANES):
        out = jnp.where(expert == 2 * j + half, wide[:, j * LANES : (j + 1) * LANES], out)
    return out


def project_kernel(codes, block, length, segs, experts, me, lens, tok, routes, *refs):
    n = len(codes)
    pieces = list(zip(refs[:n], codes))
    hid_o, qa_o, kx_o, vx_o, pr_o, vec_o, w, vec, sem = refs[n:]
    span, depth = tok.shape
    step = pl.program_id(0)
    row = lax.div(step * span, length)
    begin = lax.rem(step * span, length)

    @pl.when(step == 0)
    def _():
        fetch(me[0], pieces, block, [(0, depth, w, 0, 0), (2 * depth, 2 * LANES, w, 0, depth)], sem)
        arrive(w, sem)
        vec[...] = w[:, depth + LANES :].astype(F32).T
        vec_o[...] = vec[0:32, :]

    lane = iota((TILE, LANES), 1)
    half = lane // 64
    low = lane < 64
    for c in range(span // TILE):
        rows = slice(c * TILE, (c + 1) * TILE)
        unit, _ = normed(tok[rows, :].astype(F32))
        hid = (unit * vec[G1 : G1 + 1, :] + vec[B1 : B1 + 1, :]).astype(BF)
        hid_o[rows, :] = hid
        query = nn(hid, w[:, 0:depth])
        small = nn(hid, w[:, depth:])
        kv = small[:, :LANES].astype(BF).astype(F32)
        swap = pltpu.roll(kv, 64, 1)
        seg = segment_of(lens, row, begin + c * TILE, TILE)
        same = jnp.where(lane == seg, 1.0, 0.0)
        kx_o[rows, 0:LANES] = jnp.where(low, kv, swap).astype(BF)
        kx_o[rows, LANES:] = jnp.where(lane < segs, same, jnp.where(lane < 8, 1.0, 0.0)).astype(BF)
        vx_o[rows, 0:LANES] = jnp.where(low, swap, kv).astype(BF)
        vx_o[rows, LANES:] = jnp.ones((TILE, LANES), BF)
        logits = jnp.where(lane < experts, small[:, LANES:], FAR)
        raised = jnp.exp(logits - jnp.max(logits, -1, keepdims=True))
        pr_o[rows, :] = raised / jnp.sum(raised, -1, keepdims=True)
        for slot in range(2):
            qa_o[slot, rows, :] = (chosen(query, pick(routes, rows, slot), half) * 0.125).astype(BF)


def attend_kernel(segs, lens, routes, qa, kx, vx, pr, o_o, u_o, qf_o):
    span, depth = u_o.shape
    row, step = pl.program_id(0), pl.program_id(1)
    lane = iota((TILE, LANES), 1)
    half = lane // 64
    low = lane < 64
    for c in range(span // TILE):
        rows = slice(c * TILE, (c + 1) * TILE)
        seg = segment_of(lens, row, step * span + c * TILE, TILE)
        apart = jnp.where((lane < segs) & (lane != seg), FAR, 0.0)
        probs = pr[rows, :]
        seen, gated, experts_of = [], [], []
        for slot in range(2):
            expert = pick(routes, rows, slot)
            scores = nt(jnp.concatenate([qa[slot, rows, :], apart.astype(BF)], 1), kx[...])
            top = jnp.max(scores, -1, keepdims=True)
            raised = jnp.exp(scores - top).astype(BF)
            both = nn(raised, vx[...])
            mass = both[:, LANES:]
            out = both[:, :LANES] / mass
            qf_o[slot, rows, :] = (apart + three(lane, top + jnp.log(mass))).astype(BF)
            gate = jnp.sum(jnp.where(lane == expert, probs, 0.0), -1, keepdims=True)
            seen.append(out)
            gated.append(out * gate)
            experts_of.append(expert)
        o_o[rows, :] = jnp.where(low, seen[0], seen[1])
        for j in range(depth // LANES):
            part = jnp.where(experts_of[0] == 2 * j + half, gated[0], jnp.where(experts_of[1] == 2 * j + half, gated[1], 0.0))
            u_o[rows, j * LANES : (j + 1) * LANES] = part.astype(BF)


def mix_kernel(codes, block, me, tok, u, vec, *refs):
    n = len(codes)
    x1_o, h2_o, w, sem = refs[n:]
    span, depth = tok.shape

    @pl.when(pl.program_id(0) == 0)
    def _():
        fetch(me[0], list(zip(refs[:n], codes)), block, [(depth, depth, w, 0, 0)], sem)
        arrive(w, sem)

    for c in range(span // TILE):
        rows = slice(c * TILE, (c + 1) * TILE)
        after = tok[rows, :].astype(F32) + nn(u[rows, :], w[...])
        x1_o[rows, :] = after
        unit, _ = normed(after)
        h2_o[rows, :] = (unit * vec[G2 : G2 + 1, :] + vec[B2 : B2 + 1, :]).astype(BF)


def ffn_kernel(codes, block, me, h2, dy, vec, *refs):
    n = [len(own) for own in codes]
    total_pieces = sum(n)
    pieces = [list(zip(refs[: n[0]], codes[0])), list(zip(refs[n[0] : total_pieces], codes[1]))]
    act_o, dz_o, bias_o = refs[total_pieces : total_pieces + 3]
    at = total_pieces + 3
    grads = [list(zip(refs[at : at + n[0]], codes[0])), list(zip(refs[at + n[0] : at + total_pieces], codes[1]))]
    wu, wd, ht, yt, out, sem, out_sem = refs[at + total_pieces :]
    sub = pl.program_id(0)
    total, width = act_o.shape
    depth = h2.shape[1]
    wide = 256

    @pl.when(sub == 0)
    def _():
        for half in range(2):
            fetch(me[0], pieces[half], block, ffn_parts(wu, wd, half, depth, True, True), sem)
        for t in range(0, total, STEP):
            ht[0:depth, t : t + STEP] = h2[t : t + STEP, :].T
            yt[:, t : t + STEP] = dy[t : t + STEP, :].T
        ht[depth:, :] = jnp.ones((16, total), BF)
        arrive(wu, sem)
        arrive(wd, sem)

    one = 0.7978845608028654
    two = one * 0.044715
    up_at = lax.div(sub, 2) * 4 * depth + lax.rem(sub, 2) * depth
    for k in range(width // wide):
        here = pl.ds(pl.multiple_of(sub * width + k * wide, wide), wide)
        own = slice(k * wide, (k + 1) * wide)
        z = nn(h2[...], wu[:, here]) + vec[pl.ds(BU + sub, 1), own]
        dact = nt(dy[...], wd[here, :])
        square = z * z
        tanh = jnp.tanh(z * (one + two * square))
        part = 0.5 * tanh + 0.5
        act = z * part
        slope = part + act * (1.0 - tanh) * (one + 3.0 * two * square)
        act_o[:, own] = act.astype(BF)
        dz_o[:, own] = (dact * slope).astype(BF)
    for k in range(width // wide):
        own = slice(k * wide, (k + 1) * wide)
        up = nn(ht[...], dz_o[:, own])
        out[:, pl.ds(pl.multiple_of(up_at + k * wide, wide), wide)] = up[0:depth, :].astype(BF)
        bias_o[pl.ds(sub, 1), own] = up[depth : depth + 1, :]
    down = nn(yt[...], act_o[...])
    out[:, pl.ds(pl.multiple_of(up_at + 2 * depth, width), width)] = down.T.astype(BF)

    @pl.when(sub == 1)
    def _():
        scatter(me[0], grads[0], block, out, 0, out_sem)

    @pl.when(sub == 3)
    def _():
        scatter(me[0], grads[1], block, out, 4 * depth, out_sem)
        arrive(out, out_sem)


def turn_kernel(codes, f_codes, go_codes, block, me, dz, dy, x1, routes, pr, o, u, vec, *refs):
    n, n_f, n_go = len(codes), [len(own) for own in f_codes], len(go_codes)
    w_pieces = list(zip(refs[:n], codes))
    f_pieces = [list(zip(refs[n : n + n_f[0]], f_codes[0])), list(zip(refs[n + n_f[0] : n + sum(n_f)], f_codes[1]))]
    at = n + sum(n_f)
    dx1_o, da_o, df_o, ds_o, sums_o = refs[at : at + 5]
    go_pieces = list(zip(refs[at + 5 : at + 5 + n_go], go_codes))
    w, wu, go, sums, out, sem, f_sem, out_sem = refs[at + 5 + n_go :]
    span, depth = dy.shape
    step = pl.program_id(0)

    @pl.when(step == 0)
    def _():
        for half in range(2):
            fetch(me[0], f_pieces[half], block, ffn_parts(wu, None, half, depth, True, False), f_sem)
        fetch(me[0], w_pieces, block, [(depth, depth, w, 0, 0)], sem)
        go[...] = jnp.zeros_like(go)
        sums[...] = jnp.zeros_like(sums)
        arrive(wu, f_sem)
        arrive(w, sem)

    lane = iota((TILE, LANES), 1)
    half = lane // 64
    low = lane < 64
    for c in range(span // TILE):
        rows = slice(c * TILE, (c + 1) * TILE)
        dh2 = nt(dz[rows, :], wu[...])
        unit, inv = normed(x1[rows, :])
        grad = dy[rows, :].astype(F32)
        sums[G2 : G2 + 1, :] += jnp.sum(dh2 * unit, 0, keepdims=True)
        sums[B2 : B2 + 1, :] += jnp.sum(dh2, 0, keepdims=True)
        sums[BD : BD + 1, :] += jnp.sum(grad, 0, keepdims=True)
        scaled = dh2 * vec[G2 : G2 + 1, :]
        one = jnp.mean(scaled, -1, keepdims=True)
        two = jnp.mean(scaled * unit, -1, keepdims=True)
        dx1 = grad + inv * (scaled - one - unit * two)
        dx1_o[rows, :] = dx1
        dx1 = dx1.astype(BF)
        go[...] += nn(u[rows, :].T, dx1)
        du = nt(dx1, w[...]).astype(BF).astype(F32)
        probs = pr[rows, :]
        heads = o[rows, :]
        swap = pltpu.roll(heads, 64, 1)
        dprobs = jnp.zeros((TILE, LANES), F32)
        for slot in range(2):
            expert = pick(routes, rows, slot)
            own = chosen(du, expert, half)
            here = lane == expert
            gate = jnp.sum(jnp.where(here, probs, 0.0), -1, keepdims=True)
            seen = jnp.where(low, heads, swap) if slot == 0 else jnp.where(low, swap, heads)
            dgate = jnp.sum(own * seen, -1, keepdims=True)
            da = (own * gate).astype(BF)
            da_o[slot, rows, :] = da
            df_o[slot, rows, :] = three(lane, jnp.sum(da.astype(F32) * seen, -1, keepdims=True)).astype(BF)
            dprobs = jnp.where(here, dgate, dprobs)
            sums[LOAD : LOAD + 1, 0:LANES] += jnp.sum(jnp.where(here, 1.0, 0.0), 0, keepdims=True)
        inner = jnp.sum(dprobs * probs, -1, keepdims=True)
        ds_o[rows, :] = (probs * (dprobs - inner)).astype(BF)

    @pl.when(step == pl.num_programs(0) - 1)
    def _():
        sums_o[...] = sums[...]
        out[...] = go[...].astype(BF)
        scatter(me[0], go_pieces, block, out, 0, out_sem)
        arrive(out, out_sem)


def attend_back_kernel(routes, qa, qf, kx, vx, da, df, dq_o, kv_o, dk, dv, ds, ps):
    span, depth = dq_o.shape
    step = pl.program_id(1)
    lane = iota((TILE, LANES), 1)
    half = lane // 64

    for slot in range(2):
        own = slice(slot * span, (slot + 1) * span)
        probs = jnp.exp(nt(jnp.concatenate([qa[slot], qf[slot]], 1), kx[...]))
        ps[own, :] = probs.astype(BF)
        away = nt(jnp.concatenate([da[slot], df[slot]], 1), vx[...])
        ds[own, :] = (probs * away).astype(BF)
    dk_part = nn(jnp.concatenate([qa[0].T, qa[1].T], 1), ds[...])
    dv_part = nn(jnp.concatenate([da[0].T, da[1].T], 1), ps[...])
    found = nn(ds[...], kx[:, 0:LANES]) * 0.125
    for c in range(span // TILE):
        rows = slice(c * TILE, (c + 1) * TILE)
        others = slice(span + c * TILE, span + (c + 1) * TILE)
        one, two = pick(routes, rows, 0), pick(routes, rows, 1)
        for j in range(depth // LANES):
            part = jnp.where(one == 2 * j + half, found[rows, :], jnp.where(two == 2 * j + half, found[others, :], 0.0))
            dq_o[rows, j * LANES : (j + 1) * LANES] = part.astype(BF)

    @pl.when(step == 0)
    def _():
        dk[...] = dk_part
        dv[...] = dv_part

    @pl.when(step > 0)
    def _():
        dk[...] += dk_part
        dv[...] += dv_part

    @pl.when(step == pl.num_programs(1) - 1)
    def _():
        for c in range(kv_o.shape[0] // TILE):
            rows = slice(c * TILE, (c + 1) * TILE)
            both = jnp.concatenate([dk[0:64, rows] + dk[64:, rows], dv[0:64, rows] + dv[64:, rows]], 0)
            kv_o[rows, :] = both.T.astype(BF)


def sum_kernel(codes, out_codes, block, experts, me, hid, dq, kv, ds, sums, bias, *refs):
    n, n_out = len(codes), len(out_codes)
    pieces = list(zip(refs[:n], codes))
    grads = list(zip(refs[n : n + n_out], out_codes))
    w, gq, gs, all_sums, out, sem, out_sem = refs[n + n_out :]
    span, depth = hid.shape
    step = pl.program_id(0)

    @pl.when(step == 0)
    def _():
        fetch(me[0], pieces, block, [(0, depth, w, 0, 0), (2 * depth, 2 * LANES, w, 0, depth)], sem)
        gq[...] = jnp.zeros_like(gq)
        gs[...] = jnp.zeros_like(gs)

    turned = jnp.concatenate([hid[...].T, jnp.ones((16, span), BF)], 0)
    gq[...] += nn(turned, dq[...])
    gs[...] += nn(turned, jnp.concatenate([kv[...], ds[...]], 1))

    @pl.when(step == pl.num_programs(0) - 1)
    def _():
        arrive(w, sem)
        all_sums[...] = jnp.zeros_like(all_sums)
        all_sums[0:32, :] = sums[...]
        all_sums[BU : BU + 4, :] = bias[0:4, :]
        wq = w[:, 0:depth].astype(F32)
        ws = w[:, depth:].astype(F32)
        wide = iota((depth, LANES), 1)
        ws_own = jnp.where(wide < experts, ws[:, LANES:], 0.0)
        around = jnp.sum(gq[0:depth, :] * wq, -1, keepdims=True)
        around += jnp.sum(gs[0:depth, 0:LANES] * ws[:, 0:LANES] + gs[0:depth, LANES:] * ws_own, -1, keepdims=True)
        shift = jnp.sum(gq[depth : depth + 1, :] * wq, -1, keepdims=True)
        shift += jnp.sum(
            gs[depth : depth + 1, 0:LANES] * ws[:, 0:LANES] + gs[depth : depth + 1, LANES:] * ws_own, -1, keepdims=True
        )
        gain = ws[:, LANES + G1 : LANES + G1 + 1]
        lift = ws[:, LANES + B1 : LANES + B1 + 1]
        stretch = (around - lift * shift) / gain
        place = lax.rem(iota((depth, LANES), 0), block)
        load = jnp.sum(jnp.where(wide == place, sums[LOAD : LOAD + 1, 0:LANES], 0.0), -1, keepdims=True)
        columns = jnp.where(wide < experts, gs[0:depth, LANES:], all_sums[...].T)
        columns = jnp.where(wide == G1, stretch, columns)
        columns = jnp.where(wide == B1, shift, columns)
        columns = jnp.where(wide == LOAD, load, columns)
        out[:, 0:depth] = gq[0:depth, :].astype(BF)
        out[:, depth : depth + LANES] = gs[0:depth, 0:LANES].astype(BF)
        out[:, depth + LANES :] = columns.astype(BF)
        scatter(me[0], grads, block, out, 0, out_sem)
        arrive(out, out_sem)


def result_kernel(f_codes, block, me, act, x1, vec, *refs):
    n = [len(own) for own in f_codes]
    f_pieces = [list(zip(refs[: n[0]], f_codes[0])), list(zip(refs[n[0] : sum(n)], f_codes[1]))]
    res_o, wd, sem = refs[sum(n) :]
    depth = x1.shape[1]

    @pl.when(pl.program_id(0) == 0)
    def _():
        for half in range(2):
            fetch(me[0], f_pieces[half], block, ffn_parts(None, wd, half, depth, False, True), sem)
        arrive(wd, sem)

    res_o[...] = (x1[...] + vec[BD : BD + 1, :] + nn(act[...], wd[...])).astype(BF)


def close_kernel(codes, block, me, dx1, dq, kv, ds, tok, vec, *refs):
    n = len(codes)
    grad_o, w, sem = refs[n:]
    span, depth = tok.shape

    @pl.when(pl.program_id(0) == 0)
    def _():
        fetch(me[0], list(zip(refs[:n], codes)), block, [(0, depth, w, 0, 0), (2 * depth, 2 * LANES, w, 0, depth)], sem)
        arrive(w, sem)

    for c in range(span // TILE):
        rows = slice(c * TILE, (c + 1) * TILE)
        dh = nt(dq[rows, :], w[:, 0:depth]) + nt(jnp.concatenate([kv[rows, :], ds[rows, :]], 1), w[:, depth:])
        unit, inv = normed(tok[rows, :].astype(F32))
        scaled = dh * vec[G1 : G1 + 1, :]
        one = jnp.mean(scaled, -1, keepdims=True)
        two = jnp.mean(scaled * unit, -1, keepdims=True)
        grad_o[rows, :] = (dx1[rows, :] + inv * (scaled - one - unit * two)).astype(BF)


def xor_pairs(count, mask):
    return [(i, i ^ mask) for i in range(count)]


def hops(dp, fsdp):
    inner = fsdp.bit_length() - 1
    along = [1 << bit for bit in range(inner - 1, 1, -1)]
    across = [2] if inner > 1 else []
    rows = [1 << (inner + bit) for bit in range(dp.bit_length() - 1)]
    core = [1] if inner > 0 else []
    return along + across + rows + core, along + rows + across + core


def layout(masks):
    own = [0]
    for mask in masks[:-1]:
        own = own + [code ^ mask for code in own]
    if not masks:
        return [own]
    return [own, [code ^ masks[-1] for code in own]]


def after(value, *others):
    return lax.optimization_barrier((value, *others))[0]


def move(value, mask, count):
    return lax.ppermute(value, AXES, xor_pairs(count, mask))


def spread(held, mask, count):
    return jnp.concatenate([held, move(held, mask, count)], 0)


def joined(keep, got, dtype=BF):
    return (keep.astype(F32) + got.astype(F32)).astype(dtype)


def halves(value):
    half = value.shape[0] // 2
    return value[:half], value[half:]


def cost(micros):
    return pl.CostEstimate(flops=int(micros * 1.0e9), bytes_accessed=1024, transcendentals=0)


def on_device(
    sizes, tokens, routes, lengths, ln1_gain, ln1_bias, w_query, w_key, w_value, w_out, w_router,
    ln2_gain, ln2_bias, w_up, b_up, w_down, b_down, cotangent
):
    dp, fsdp = sizes
    count = dp * fsdp
    total, depth = tokens.shape
    rows = lengths.shape[0]
    length = total // rows
    experts, head = w_router.shape[1], w_key.shape[1]
    segs = lengths.shape[1]
    share = w_query.shape[0]
    inner = w_up.shape[1]
    subs = inner // depth
    fast = share % 16 == 0 and fsdp >= 8 and dp >= 2
    me = (lax.axis_index(AXES) if fast else jnp.int32(0)).astype(jnp.int32).reshape(1)
    small = jnp.concatenate(
        [w_query, w_out, w_key, w_value, w_router]
        + [v[:, None] for v in (ln1_gain, ln1_bias, ln2_gain, ln2_bias, b_down)]
        + [b_up.reshape(subs, share).T],
        1,
    )
    first_width = 2 * depth + 2 * LANES
    small = jnp.pad(small, ((0, 0), (0, first_width - small.shape[1])))
    ups = w_up.reshape(share, count, subs, share).transpose(0, 2, 1, 3).reshape(share, subs, depth)
    downs = w_down.reshape(subs, share, depth).transpose(1, 0, 2)
    large = [
        jnp.concatenate([ups[:, 2 * i : 2 * i + 2], downs[:, 2 * i : 2 * i + 2]], 1).reshape(share, 4 * depth)
        for i in range(2)
    ]
    stage = [lambda value: value] * 8
    if fast:
        orders = hops(dp, fsdp)
        block = share
        codes = layout(orders[0])
        f_codes = [layout(order) for order in orders]
        steps = len(orders[0])
        held = spread(small[None], orders[0][0], count)
        big = [after(half[None], held) for half in large]
        big_all = spread(jnp.concatenate(big, 2), orders[0][0], count)
        early = len([m for m in orders[0][:-1] if orders[0].index(m) == orders[1].index(m)])
        for mask in orders[0][1 : -2]:
            held = spread(held, mask, count)
        held = after(held, big_all)
        for mask in orders[0][1:early]:
            big_all = spread(big_all, mask, count)
        held = spread(held, orders[0][-2], count)
        w_pieces = [held, move(held, orders[0][-1], count)]
        big = [big_all[:, :, : 4 * depth], big_all[:, :, 4 * depth :]]
        w_pieces[0] = after(w_pieces[0], *big)
        pending = list(range(early, steps - 1))
    else:
        block = depth
        codes = [[0]]
        f_codes = [[[0]], [[0]]]
        w_pieces = [lax.all_gather(small, AXES, axis=0, tiled=True)[None]]
        f_pieces = [[lax.all_gather(half, AXES, axis=0, tiled=True)[None]] for half in large]
    n, n_f = len(codes), [len(own) for own in f_codes]
    blocks = len(codes[0])

    smem = pl.BlockSpec(memory_space=pltpu.SMEM)
    hbm = pl.BlockSpec(memory_space=pl.ANY)
    dma = pltpu.SemaphoreType.DMA

    def whole(dims):
        return pl.BlockSpec(dims, lambda *_: (0,) * len(dims))

    def shape(dims, dtype):
        return jax.ShapeDtypeStruct(dims, dtype)

    def call(kernel, name, micros, grid, ins, in_specs, outs, out_specs, scratch):
        return pl.pallas_call(
            kernel, grid=grid, in_specs=in_specs, out_specs=out_specs, out_shape=outs, scratch_shapes=scratch,
            compiler_params=pltpu.CompilerParams(vmem_limit_bytes=VMEM), cost_estimate=cost(micros), name=name,
        )(*ins)

    span = min(STEP, length)
    tiles = total // span
    per_row = length // span

    def tile(wide):
        return pl.BlockSpec((span, wide), lambda t: (t, 0))

    def pair(wide):
        return pl.BlockSpec((2, span, wide), lambda t: (0, t, 0))

    def row_tile(wide):
        return pl.BlockSpec((span, wide), lambda r, t: (r * per_row + t, 0))

    def row_pair(wide):
        return pl.BlockSpec((2, span, wide), lambda r, t: (0, r * per_row + t, 0))

    def by_row(wide):
        return pl.BlockSpec((length, wide), lambda r, t: (r, 0))

    hid, qa, kx, vx, pr, vec = call(
        functools.partial(project_kernel, codes, block, length, segs, experts), "project", 9.0, (tiles,),
        (me, lengths, tokens, routes, *w_pieces),
        [smem, smem, tile(depth), tile(2)] + [hbm] * n,
        [
            shape((total, depth), BF), shape((2, total, LANES), BF), shape((total, 2 * LANES), BF),
            shape((total, 2 * LANES), BF), shape((total, LANES), F32), shape((32, depth), F32),
        ],
        [tile(depth), pair(LANES), tile(2 * LANES), tile(2 * LANES), tile(LANES), whole((32, depth))],
        [pltpu.VMEM((depth, depth + 2 * LANES), BF), pltpu.VMEM((LANES, depth), F32), dma],
    )
    if fast:
        big = [spread(half, order[pending[0]], count) for half, order in zip(big, orders)]
        qa = after(qa, *big)
        big = [after(half, kx) for half in big]
    o, u, qf = call(
        functools.partial(attend_kernel, segs), "attend", 13.0, (rows, per_row),
        (lengths, routes, qa, kx, vx, pr),
        [smem, row_tile(2), row_pair(LANES), by_row(2 * LANES), by_row(2 * LANES), row_tile(LANES)],
        [shape((total, LANES), F32), shape((total, depth), BF), shape((2, total, LANES), BF)],
        [row_tile(LANES), row_tile(depth), row_pair(LANES)],
        [],
    )
    if fast:
        for at in pending[1:]:
            big = [spread(half, order[at], count) for half, order in zip(big, orders)]
        u = after(u, *big)
        big = [after(half, o) for half in big]
        f_pieces = [[half, move(half, orders[0][-1], count)] for half in big]
    x1, h2 = call(
        functools.partial(mix_kernel, codes, block), "mix", 5.0, (tiles,),
        (me, tokens, u, vec, *w_pieces),
        [smem, tile(depth), tile(depth), whole((32, depth))] + [hbm] * n,
        [shape((total, depth), F32), shape((total, depth), BF)],
        [tile(depth), tile(depth)],
        [pltpu.VMEM((depth, depth), BF), dma],
    )
    flat_f = [piece for half in f_pieces for piece in half]

    act, dz, bias, *f_grads = call(
        functools.partial(ffn_kernel, f_codes, block), "feed", 25.0, (subs,),
        (me, h2, cotangent, vec, *flat_f),
        [smem, whole((total, depth)), whole((total, depth)), whole((32, depth))] + [hbm] * sum(n_f),
        [shape((total, inner), BF), shape((total, inner), BF), shape((8, depth), F32)]
        + [shape((blocks, block, 4 * depth), BF)] * sum(n_f),
        [pl.BlockSpec((total, depth), lambda s: (0, s)), pl.BlockSpec((total, depth), lambda s: (0, s)), whole((8, depth))]
        + [hbm] * sum(n_f),
        [
            pltpu.VMEM((depth, inner), BF), pltpu.VMEM((inner, depth), BF), pltpu.VMEM((depth + 16, total), BF),
            pltpu.VMEM((depth, total), BF), pltpu.VMEM((depth, 2 * inner), BF), dma, dma,
        ],
    )
    f_grads = [f_grads[: n_f[0]], f_grads[n_f[0] :]]
    if fast:
        sent = [move(half[1], orders[0][-1], count) for half in f_grads]

    dx1, da, df, ds, sums, *go = call(
        functools.partial(turn_kernel, codes, f_codes, f_codes[0], block), "turn", 20.0, (tiles,),
        (me, dz, cotangent, x1, routes, pr, o, u, vec, *w_pieces, *flat_f),
        [smem, tile(inner), tile(depth), tile(depth), tile(2), tile(LANES), tile(LANES), tile(depth), whole((32, depth))]
        + [hbm] * (n + sum(n_f)),
        [
            shape((total, depth), F32), shape((2, total, LANES), BF), shape((2, total, LANES), BF),
            shape((total, LANES), BF), shape((32, depth), F32),
        ]
        + [shape((blocks, block, depth), BF)] * n_f[0],
        [tile(depth), pair(LANES), pair(LANES), tile(LANES), whole((32, depth))] + [hbm] * n_f[0],
        [
            pltpu.VMEM((depth, depth), BF), pltpu.VMEM((depth, inner), BF), pltpu.VMEM((depth, depth), F32),
            pltpu.VMEM((32, depth), F32), pltpu.VMEM((depth, depth), BF), dma, dma, dma,
        ],
    )
    if fast:
        got = move(go[1], orders[0][-1], count)
        acc = [joined(half[0], s) for half, s in zip(f_grads, sent)]
        acc[0] = jnp.concatenate([acc[0], joined(go[0], got)], 2)
        acc = [after(a, dx1) for a in acc]
        back_orders = [list(reversed(order[:-1])) for order in orders]
        split = [halves(a) for a in acc]
        acc = [joined(keep, move(send, order[0], count)) for (keep, send), order in zip(split, back_orders)]

    dq, kv = call(
        attend_back_kernel, "attend_back", 18.0, (rows, per_row),
        (routes, qa, qf, kx, vx, da, df),
        [row_tile(2), row_pair(LANES), row_pair(LANES), by_row(2 * LANES), by_row(2 * LANES), row_pair(LANES), row_pair(LANES)],
        [shape((total, depth), BF), shape((total, LANES), BF)],
        [row_tile(depth), by_row(LANES)],
        [
            pltpu.VMEM((LANES, length), F32), pltpu.VMEM((LANES, length), F32), pltpu.VMEM((2 * span, length), BF),
            pltpu.VMEM((2 * span, length), BF),
        ],
    )
    if fast:
        kv = after(kv, *acc)
        acc = [after(a, kv) for a in acc]
        split = [halves(a) for a in acc]
        acc = [joined(keep, move(send, order[1], count)) for (keep, send), order in zip(split, back_orders)]
    w_grads = call(
        functools.partial(sum_kernel, codes, codes, block, experts), "sums", 6.0, (tiles,),
        (me, hid, dq, kv, ds, sums, bias, *w_pieces),
        [smem, tile(depth), tile(depth), tile(LANES), tile(LANES), whole((32, depth)), whole((8, depth))] + [hbm] * n,
        [shape((blocks, block, depth + 2 * LANES), BF)] * n,
        [hbm] * n,
        [
            pltpu.VMEM((depth, depth + 2 * LANES), BF), pltpu.VMEM((depth + 16, depth), F32),
            pltpu.VMEM((depth + 16, 2 * LANES), F32), pltpu.VMEM((LANES, depth), F32),
            pltpu.VMEM((depth, depth + 2 * LANES), BF), dma, dma,
        ],
    )
    if fast:
        tail = joined(w_grads[0], move(w_grads[1], orders[0][-1], count))
        late = back_orders[0]
        tail_keep, tail_send = halves(tail)
        tail = joined(tail_keep, move(tail_send, late[0], count))
        tail_keep, tail_send = halves(tail)
    grad_tokens = call(
        functools.partial(close_kernel, codes, block), "close", 6.0, (tiles,),
        (me, dx1, dq, kv, ds, tokens, vec, *w_pieces),
        [smem, tile(depth), tile(depth), tile(LANES), tile(LANES), tile(depth), whole((32, depth))] + [hbm] * n,
        [shape((total, depth), BF)],
        [tile(depth)],
        [pltpu.VMEM((depth, depth + 2 * LANES), BF), dma],
    )[0]
    result = call(
        functools.partial(result_kernel, f_codes, block), "result", 6.0, (tiles,),
        (me, act, x1, vec, *flat_f),
        [smem, tile(inner), tile(depth), whole((32, depth))] + [hbm] * sum(n_f),
        [shape((total, depth), BF)],
        [tile(depth)],
        [pltpu.VMEM((inner, depth), BF), dma],
    )[0]

    if fast:
        for step in range(2, len(back_orders[0])):
            split = [halves(a) for a in acc]
            acc = [
                joined(keep, move(send, order[step], count), F32 if step == len(back_orders[0]) - 1 else BF)
                for (keep, send), order in zip(split, back_orders)
            ]
        for step in range(1, len(late)):
            tail = joined(tail_keep, move(tail_send, late[step], count), F32 if step == len(late) - 1 else BF)
            if step < len(late) - 1:
                tail_keep, tail_send = halves(tail)
        own_f = [acc[0][0, :, : 4 * depth], acc[1][0]]
        grad_out = acc[0][0, :, 4 * depth :]
        own_w = tail[0]
        load = own_w[:experts, depth + LANES + LOAD]
    else:
        def scattered(value):
            return lax.psum_scatter(value[0].astype(F32), AXES, scatter_dimension=0, tiled=True)

        own_f = [scattered(half[0]) for half in f_grads]
        grad_out = scattered(go[0])
        own_w = scattered(w_grads[0])
        load = lax.psum(w_grads[0][0][:experts, depth + LANES + LOAD].astype(F32), AXES)
    extra = own_w[:, depth + LANES :]
    grad_up = jnp.concatenate([half[:, : 2 * depth] for half in own_f], 1)
    grad_up = grad_up.reshape(share, subs, count, share).transpose(0, 2, 1, 3).reshape(share, inner)
    grad_down = jnp.concatenate([half[:, 2 * depth :] for half in own_f], 1)
    grad_down = grad_down.reshape(share, subs, depth).transpose(1, 0, 2).reshape(subs * share, depth)
    return (
        result,
        grad_tokens,
        extra[:, G1],
        extra[:, B1],
        own_w[:, 0:depth],
        own_w[:, depth : depth + head],
        own_w[:, depth + head : depth + 2 * head],
        grad_out,
        extra[:, 0:experts],
        extra[:, G2],
        extra[:, B2],
        grad_up,
        extra[:, BU : BU + subs].T.reshape(subs * share),
        grad_down,
        extra[:, BD],
        load / (total * count),
    )


def solution(mesh):
    over = P(AXES)
    flat = P(AXES, None)
    sizes = (mesh.shape["dp"], mesh.shape["fsdp"])
    return jax.shard_map(
        functools.partial(on_device, sizes),
        mesh=mesh,
        in_specs=(
            flat, flat, flat, over, over, flat, flat, flat, flat, flat, over, over, flat, over, flat, over, flat,
        ),
        out_specs=(
            flat, flat, over, over, flat, flat, flat, flat, flat, over, over, flat, over, flat, over, P(),
        ),
        check_vma=False,
    )
```

```python
import functools

import jax
import jax.numpy as jnp
from jax import lax
from jax.experimental import pallas as pl
from jax.experimental.pallas import tpu as pltpu
from jax.sharding import PartitionSpec as P

AXES = ("dp", "fsdp")
F32 = jnp.float32
BF = jnp.bfloat16
FAR = -1e30
LANES = 128
G1, B1, G2, B2, BD, BU, LOAD = 8, 9, 10, 11, 12, 13, 17
TILE = 256
STEP = 512
ROOM = {
    "project": 16, "attend": 20, "mix": 14, "feed": 32, "turn": 28, "gates": 16, "attend_back": 32, "sums": 18, "close": 18,
    "result": 22,
}


def nn(left, right):
    return jnp.dot(left, right, preferred_element_type=F32)


def nt(left, right):
    return lax.dot_general(left, right, (((1,), (1,)), ((), ())), preferred_element_type=F32)


def iota(shape, dim):
    return lax.broadcasted_iota(jnp.int32, shape, dim)


def normed(value):
    center = value - jnp.mean(value, -1, keepdims=True)
    inv = lax.rsqrt(jnp.mean(center * center, -1, keepdims=True) + 1e-05)
    return center * inv, inv


def fetch(core, pieces, parts, sem):
    for other, piece in enumerate(pieces):
        own = jnp.bitwise_xor(core, other)
        for start, wide, dst in parts:
            blocks, block, _ = piece.shape
            view = dst.reshape(blocks, len(pieces), block, wide)
            pltpu.make_async_copy(piece.at[:, :, start : start + wide], view.at[:, own], sem).start()


def arrive(dst, sem):
    pltpu.make_async_copy(dst, dst, sem).wait()


def scatter(core, pieces, src, sem):
    for other, piece in enumerate(pieces):
        own = jnp.bitwise_xor(core, other)
        blocks, block, wide = piece.shape
        view = src.reshape(blocks, len(pieces), block, wide)
        pltpu.make_async_copy(view.at[:, own], piece, sem).start()


def ffn_parts(wu, wd, half, depth, up, down):
    parts = []
    if up:
        parts.append((0, 2 * depth, wu.at[half]))
    if down:
        parts += [((2 + j) * depth, depth, wd.at[pl.ds((2 * half + j) * depth, depth), :]) for j in range(2)]
    return parts


def pack_kernel(wq, wo, wk, wv, wr, g1, b1, g2, b2, bd, bu, o):
    share, depth = wq.shape
    head, experts = wk.shape[1], wr.shape[1]
    same = iota((share, share), 0) == iota((share, share), 1)
    lane = iota((share, LANES), 1)

    def column(v):
        return jnp.sum(jnp.where(same, jnp.broadcast_to(v.astype(F32), (share, share)), 0.0), 1, keepdims=True)

    out = jnp.zeros((share, LANES), F32)
    for at, v in zip((G1, B1, G2, B2, BD), (g1, b1, g2, b2, bd)):
        out = jnp.where(lane == at, column(v[...].reshape(1, share)), out)
    flat = bu[...].reshape(1, bu.shape[0])
    for j in range(bu.shape[0] // share):
        out = jnp.where(lane == BU + j, column(flat[:, j * share : (j + 1) * share]), out)
    o[:, 0:depth] = wq[...]
    o[:, depth : depth + head] = wk[...]
    o[:, depth + head : depth + LANES] = wv[...]
    o[:, depth + LANES : depth + 2 * LANES] = out.astype(BF)
    o[:, depth + LANES : depth + LANES + experts] = wr[...]
    o[:, depth + 2 * LANES :] = wo[...]


def split3(value):
    high = value.astype(BF).astype(F32)
    rest = value - high
    mid = rest.astype(BF).astype(F32)
    return high, mid, rest - mid


def three(lane, value):
    high, mid, rest = split3(value)
    return jnp.where(lane == 4, -high, jnp.where(lane == 5, -mid, jnp.where(lane == 6, -rest, 0.0)))


def segment_of(lens, row, start, rows):
    place = iota((rows, LANES), 0) + start
    end = lens[row, 0]
    seg = (place >= end).astype(jnp.int32)
    for j in range(1, lens.shape[1]):
        end = end + lens[row, j]
        seg = seg + (place >= end).astype(jnp.int32)
    return seg


def pick(routes, rows, slot):
    return jnp.broadcast_to(routes[rows, slot : slot + 1], (TILE, LANES))


def chosen(wide, expert, half):
    out = jnp.zeros(expert.shape, F32)
    for j in range(wide.shape[1] // LANES):
        out = jnp.where(expert == 2 * j + half, wide[:, j * LANES : (j + 1) * LANES], out)
    return out


def project_kernel(n, length, segs, experts, me, lens, tok, routes, *refs):
    hid_o, qa_o, kx_o, vx_o, pr_o, vec_o, w, vec, sem = refs[n:]
    span, depth = tok.shape
    step = pl.program_id(0)
    row = lax.div(step * span, length)
    begin = lax.rem(step * span, length)

    @pl.when(step == 0)
    def _():
        fetch(me[0], refs[:n], [(0, depth + 2 * LANES, w)], sem)
        arrive(w, sem)
        vec[...] = w[:, depth + LANES :].astype(F32).T
        vec_o[...] = vec[0:32, :]

    lane = iota((TILE, LANES), 1)
    half = lane // 64
    low = lane < 64
    for c in range(span // TILE):
        rows = slice(c * TILE, (c + 1) * TILE)
        unit, _ = normed(tok[rows, :].astype(F32))
        hid = (unit * vec[G1 : G1 + 1, :] + vec[B1 : B1 + 1, :]).astype(BF)
        hid_o[rows, :] = hid
        query = nn(hid, w[:, 0:depth])
        small = nn(hid, w[:, depth:])
        kv = small[:, :LANES].astype(BF).astype(F32)
        swap = pltpu.roll(kv, 64, 1)
        seg = segment_of(lens, row, begin + c * TILE, TILE)
        same = jnp.where(lane == seg, 1.0, 0.0)
        kx_o[rows, 0:LANES] = jnp.where(low, kv, swap).astype(BF)
        kx_o[rows, LANES:] = jnp.where(lane < segs, same, jnp.where(lane < 8, 1.0, 0.0)).astype(BF)
        vx_o[rows, 0:LANES] = jnp.where(low, swap, kv).astype(BF)
        vx_o[rows, LANES:] = jnp.ones((TILE, LANES), BF)
        logits = jnp.where(lane < experts, small[:, LANES:], FAR)
        raised = jnp.exp(logits - jnp.max(logits, -1, keepdims=True))
        pr_o[rows, :] = raised / jnp.sum(raised, -1, keepdims=True)
        for slot in range(2):
            qa_o[slot, rows, :] = (chosen(query, pick(routes, rows, slot), half) * 0.125).astype(BF)


def attend_kernel(segs, lens, routes, qa, kx, vx, pr, o_o, u_o, qf_o):
    span, depth = u_o.shape
    row, step = pl.program_id(0), pl.program_id(1)
    lane = iota((TILE, LANES), 1)
    half = lane // 64
    low = lane < 64
    for c in range(span // TILE):
        rows = slice(c * TILE, (c + 1) * TILE)
        seg = segment_of(lens, row, step * span + c * TILE, TILE)
        apart = jnp.where((lane < segs) & (lane != seg), FAR, 0.0)
        probs = pr[rows, :]
        seen, gated, experts_of = [], [], []
        for slot in range(2):
            expert = pick(routes, rows, slot)
            scores = nt(jnp.concatenate([qa[slot, rows, :], apart.astype(BF)], 1), kx[...])
            top = jnp.max(scores, -1, keepdims=True)
            raised = jnp.exp(scores - top).astype(BF)
            both = nn(raised, vx[...])
            mass = both[:, LANES:]
            out = both[:, :LANES] / mass
            qf_o[slot, rows, :] = (apart + three(lane, top + jnp.log(mass))).astype(BF)
            gate = jnp.sum(jnp.where(lane == expert, probs, 0.0), -1, keepdims=True)
            seen.append(out)
            gated.append(out * gate)
            experts_of.append(expert)
        o_o[rows, :] = jnp.where(low, seen[0], seen[1])
        for j in range(depth // LANES):
            part = jnp.where(experts_of[0] == 2 * j + half, gated[0], jnp.where(experts_of[1] == 2 * j + half, gated[1], 0.0))
            u_o[rows, j * LANES : (j + 1) * LANES] = part.astype(BF)


def mix_kernel(n, me, tok, u, vec, *refs):
    x1_o, h2_o, w, sem = refs[n:]
    span, depth = tok.shape

    @pl.when(pl.program_id(0) == 0)
    def _():
        fetch(me[0], refs[:n], [(depth + 2 * LANES, depth, w)], sem)
        arrive(w, sem)

    for c in range(span // TILE):
        rows = slice(c * TILE, (c + 1) * TILE)
        after = tok[rows, :].astype(F32) + nn(u[rows, :], w[...])
        x1_o[rows, :] = after
        unit, _ = normed(after)
        h2_o[rows, :] = (unit * vec[G2 : G2 + 1, :] + vec[B2 : B2 + 1, :]).astype(BF)


def ffn_kernel(n, me, h2, dy, vec, *refs):
    pieces = [refs[:n], refs[n : 2 * n]]
    act_o, dz_o, bias_o = refs[2 * n : 2 * n + 3]
    grads = [refs[2 * n + 3 : 3 * n + 3], refs[3 * n + 3 : 4 * n + 3]]
    wu, wd, ht, yt, acts, dzs, out, sem, out_sem = refs[4 * n + 3 :]
    step = pl.program_id(0)
    steps = pl.num_programs(0) - 1
    total, wide = act_o.shape
    depth = h2.shape[1]
    per = depth // wide
    some = wu.shape[2]

    @pl.when(step == 0)
    def _():
        for half in range(2):
            fetch(me[0], pieces[half], ffn_parts(wu, wd, half, depth, True, True), sem.at[half])
        for t in range(0, total, STEP):
            ht[0:depth, t : t + STEP] = h2[t : t + STEP, :].T
            yt[:, t : t + STEP] = dy[t : t + STEP, :].T
        ht[depth:, :] = jnp.ones((16, total), BF)

    for half in range(2):
        @pl.when(step == half * steps // 2)
        def _():
            arrive(wu.at[half], sem.at[half])
            arrive(wd.at[pl.ds(half * some, some), :], sem.at[half])

    one = 0.7978845608028654
    two = one * 0.044715
    cur = lax.rem(step, 2)

    def place(t):
        sub = lax.div(t, per)
        return sub, lax.rem(t, per), lax.rem(sub, 2) * depth, lax.div(sub, 2)

    def grad_up(t, slot):
        sub, part, column, half = place(t)
        up = nn(ht[...], dzs[slot])
        out[half, :, pl.ds(pl.multiple_of(column + part * wide, wide), wide)] = up[0:depth, :].astype(BF)
        bias_o[pl.ds(sub, 1), pl.ds(pl.multiple_of(part * wide, wide), wide)] = up[depth : depth + 1, :]

    def grad_down(t, slot):
        _, part, column, half = place(t)
        rows = pl.ds(pl.multiple_of(part * wide, wide), wide)
        out[half, rows, pl.ds(pl.multiple_of(column + 2 * depth, depth), depth)] = nn(yt[...], acts[slot]).T.astype(BF)

    @pl.when(step < steps)
    def _():
        before = jnp.maximum(step - 1, 0)
        sub, part, column, which = place(step)
        here = pl.ds(pl.multiple_of(step * wide, wide), wide)
        across = pl.ds(pl.multiple_of(column + part * wide, wide), wide)
        bias = vec[pl.ds(BU + sub, 1), pl.ds(pl.multiple_of(part * wide, wide), wide)]
        count = total // TILE
        for c in range(count):
            rows = slice(c * TILE, (c + 1) * TILE)
            z = nn(h2[rows, :], wu[which, :, across]) + bias
            dact = nt(dy[rows, :], wd[here, :])
            if c == 0:
                grad_up(before, 1 - cur)
            if c == count // 2:
                grad_down(before, 1 - cur)
            square = z * z
            tanh = jnp.tanh(z * (one + two * square))
            half = 0.5 * tanh + 0.5
            act = z * half
            slope = half + act * (1.0 - tanh) * (one + 3.0 * two * square)
            act = act.astype(BF)
            dz = (dact * slope).astype(BF)
            act_o[rows, :] = act
            dz_o[rows, :] = dz
            acts[cur, rows, :] = act
            dzs[cur, rows, :] = dz

    @pl.when(step == steps // 2)
    def _():
        scatter(me[0], grads[0], out.at[0], out_sem)

    @pl.when(step == steps)
    def _():
        grad_up(steps - 1, 1 - cur)
        grad_down(steps - 1, 1 - cur)
        scatter(me[0], grads[1], out.at[1], out_sem)
        arrive(out, out_sem)


def turn_kernel(n, me, dz, dy, x1, vec, *refs):
    dx1_o, low_o, sums_o, wu, f_sem = refs[2 * n :]
    span, depth = dy.shape
    step = pl.program_id(0)

    @pl.when(step == 0)
    def _():
        for half in range(2):
            fetch(me[0], refs[half * n : half * n + n], ffn_parts(wu, None, half, depth, True, False), f_sem)
        sums_o[...] = jnp.zeros_like(sums_o)
        arrive(wu, f_sem)

    for c in range(span // TILE):
        rows = slice(c * TILE, (c + 1) * TILE)
        dh2 = nt(dz[rows, 0 : 2 * depth], wu[0]) + nt(dz[rows, 2 * depth :], wu[1])
        unit, inv = normed(x1[rows, :])
        grad = dy[rows, :].astype(F32)
        sums_o[G2 : G2 + 1, :] += jnp.sum(dh2 * unit, 0, keepdims=True)
        sums_o[B2 : B2 + 1, :] += jnp.sum(dh2, 0, keepdims=True)
        sums_o[BD : BD + 1, :] += jnp.sum(grad, 0, keepdims=True)
        scaled = dh2 * vec[G2 : G2 + 1, :]
        one = jnp.mean(scaled, -1, keepdims=True)
        two = jnp.mean(scaled * unit, -1, keepdims=True)
        dx1 = grad + inv * (scaled - one - unit * two)
        dx1_o[rows, :] = dx1
        low_o[rows, :] = dx1.astype(BF)


def gates_kernel(n, me, dx1, routes, pr, o, u, *refs):
    da_o, df_o, ds_o, load_o, go_o, w, go, sem = refs[n:]
    span, depth = dx1.shape
    step = pl.program_id(0)

    @pl.when(step == 0)
    def _():
        fetch(me[0], refs[:n], [(depth + 2 * LANES, depth, w)], sem)
        go[...] = jnp.zeros_like(go)
        load_o[...] = jnp.zeros_like(load_o)
        arrive(w, sem)

    lane = iota((TILE, LANES), 1)
    half = lane // 64
    low = lane < 64
    go[...] += nn(u[...].T, dx1[...])
    for c in range(span // TILE):
        rows = slice(c * TILE, (c + 1) * TILE)
        du = nt(dx1[rows, :], w[...]).astype(BF).astype(F32)
        probs = pr[rows, :]
        heads = o[rows, :]
        swap = pltpu.roll(heads, 64, 1)
        dprobs = jnp.zeros((TILE, LANES), F32)
        loads = jnp.zeros((TILE, LANES), F32)
        for slot in range(2):
            expert = pick(routes, rows, slot)
            own = chosen(du, expert, half)
            here = lane == expert
            gate = jnp.sum(jnp.where(here, probs, 0.0), -1, keepdims=True)
            seen = jnp.where(low, heads, swap) if slot == 0 else jnp.where(low, swap, heads)
            dgate = jnp.sum(own * seen, -1, keepdims=True)
            da = (own * gate).astype(BF)
            da_o[slot, rows, :] = da
            df_o[slot, rows, :] = three(lane, jnp.sum(da.astype(F32) * seen, -1, keepdims=True)).astype(BF)
            dprobs = jnp.where(here, dgate, dprobs)
            loads = jnp.where(here, 1.0, loads)
        load_o[0:1, :] += jnp.sum(loads, 0, keepdims=True)
        inner = jnp.sum(dprobs * probs, -1, keepdims=True)
        ds_o[rows, :] = (probs * (dprobs - inner)).astype(BF)

    @pl.when(step == pl.num_programs(0) - 1)
    def _():
        go_o[...] = go[...].astype(BF)


def attend_back_kernel(routes, qa, qf, kx, vx, da, df, dq_o, kv_o, dk, dv, ds, ps):
    span, depth = dq_o.shape
    step = pl.program_id(1)
    lane = iota((TILE, LANES), 1)
    half = lane // 64

    for slot in range(2):
        own = slice(slot * span, (slot + 1) * span)
        probs = jnp.exp(nt(jnp.concatenate([qa[slot], qf[slot]], 1), kx[...]))
        ps[own, :] = probs.astype(BF)
        away = nt(jnp.concatenate([da[slot], df[slot]], 1), vx[...])
        ds[own, :] = (probs * away).astype(BF)
    dk_part = nn(jnp.concatenate([qa[0].T, qa[1].T], 1), ds[...])
    dv_part = nn(jnp.concatenate([da[0].T, da[1].T], 1), ps[...])
    found = nn(ds[...], kx[:, 0:LANES]) * 0.125
    for c in range(span // TILE):
        rows = slice(c * TILE, (c + 1) * TILE)
        others = slice(span + c * TILE, span + (c + 1) * TILE)
        one, two = pick(routes, rows, 0), pick(routes, rows, 1)
        for j in range(depth // LANES):
            part = jnp.where(one == 2 * j + half, found[rows, :], jnp.where(two == 2 * j + half, found[others, :], 0.0))
            dq_o[rows, j * LANES : (j + 1) * LANES] = part.astype(BF)

    @pl.when(step == 0)
    def _():
        dk[...] = dk_part
        dv[...] = dv_part

    @pl.when(step > 0)
    def _():
        dk[...] += dk_part
        dv[...] += dv_part

    @pl.when(step == pl.num_programs(1) - 1)
    def _():
        for c in range(kv_o.shape[0] // TILE):
            rows = slice(c * TILE, (c + 1) * TILE)
            both = jnp.concatenate([dk[0:64, rows] + dk[64:, rows], dv[0:64, rows] + dv[64:, rows]], 0)
            kv_o[rows, :] = both.T.astype(BF)


def sum_kernel(n, block, experts, me, hid, dq, kv, ds, sums, bias, loads, go, *refs):
    w, gq, gs, all_sums, out, sem, out_sem = refs[2 * n :]
    span, depth = hid.shape
    step = pl.program_id(0)

    @pl.when(step == 0)
    def _():
        fetch(me[0], refs[:n], [(0, depth + 2 * LANES, w)], sem)
        gq[...] = jnp.zeros_like(gq)
        gs[...] = jnp.zeros_like(gs)

    turned = jnp.concatenate([hid[...].T, jnp.ones((16, span), BF)], 0)
    gq[...] += nn(turned, dq[...])
    gs[...] += nn(turned, jnp.concatenate([kv[...], ds[...]], 1))

    @pl.when(step == pl.num_programs(0) - 1)
    def _():
        arrive(w, sem)
        all_sums[...] = jnp.zeros_like(all_sums)
        all_sums[0:32, :] = sums[...]
        all_sums[BU : BU + 4, :] = bias[0:4, :]
        wq = w[:, 0:depth].astype(F32)
        ws = w[:, depth:].astype(F32)
        wide = iota((depth, LANES), 1)
        ws_own = jnp.where(wide < experts, ws[:, LANES:], 0.0)
        around = jnp.sum(gq[0:depth, :] * wq, -1, keepdims=True)
        around += jnp.sum(gs[0:depth, 0:LANES] * ws[:, 0:LANES] + gs[0:depth, LANES:] * ws_own, -1, keepdims=True)
        shift = jnp.sum(gq[depth : depth + 1, :] * wq, -1, keepdims=True)
        shift += jnp.sum(
            gs[depth : depth + 1, 0:LANES] * ws[:, 0:LANES] + gs[depth : depth + 1, LANES:] * ws_own, -1, keepdims=True
        )
        gain = ws[:, LANES + G1 : LANES + G1 + 1]
        lift = ws[:, LANES + B1 : LANES + B1 + 1]
        stretch = (around - lift * shift) / gain
        place = lax.rem(iota((depth, LANES), 0), block)
        load = jnp.sum(jnp.where(wide == place, loads[0:1, :], 0.0), -1, keepdims=True)
        columns = jnp.where(wide < experts, gs[0:depth, LANES:], all_sums[...].T)
        columns = jnp.where(wide == G1, stretch, columns)
        columns = jnp.where(wide == B1, shift, columns)
        columns = jnp.where(wide == LOAD, load, columns)
        out[:, 0:depth] = gq[0:depth, :].astype(BF)
        out[:, depth : 2 * depth] = go[...]
        out[:, 2 * depth : 2 * depth + LANES] = gs[0:depth, 0:LANES].astype(BF)
        out[:, 2 * depth + LANES :] = columns.astype(BF)
        scatter(me[0], refs[n : 2 * n], out, out_sem)
        arrive(out, out_sem)


def result_kernel(n, me, act, x1, vec, *refs):
    res_o, wd, sem = refs[2 * n :]
    depth = x1.shape[1]

    @pl.when(pl.program_id(0) == 0)
    def _():
        for half in range(2):
            fetch(me[0], refs[half * n : half * n + n], ffn_parts(None, wd, half, depth, False, True), sem)
        arrive(wd, sem)

    res_o[...] = (x1[...] + vec[BD : BD + 1, :] + nn(act[...], wd[...])).astype(BF)


def close_kernel(n, me, dx1, dq, kv, ds, tok, vec, *refs):
    grad_o, w, sem = refs[n:]
    span, depth = tok.shape

    @pl.when(pl.program_id(0) == 0)
    def _():
        fetch(me[0], refs[:n], [(0, depth + 2 * LANES, w)], sem)
        arrive(w, sem)

    for c in range(span // TILE):
        rows = slice(c * TILE, (c + 1) * TILE)
        dh = nt(dq[rows, :], w[:, 0:depth]) + nt(jnp.concatenate([kv[rows, :], ds[rows, :]], 1), w[:, depth:])
        unit, inv = normed(tok[rows, :].astype(F32))
        scaled = dh * vec[G1 : G1 + 1, :]
        one = jnp.mean(scaled, -1, keepdims=True)
        two = jnp.mean(scaled * unit, -1, keepdims=True)
        grad_o[rows, :] = (dx1[rows, :] + inv * (scaled - one - unit * two)).astype(BF)


def xor_pairs(count, mask):
    return [(i, i ^ mask) for i in range(count)]


def hops(dp, fsdp):
    inner = fsdp.bit_length() - 1
    along = [1 << bit for bit in range(inner - 1, 1, -1)]
    across = [2] if inner > 1 else []
    rows = [1 << (inner + bit) for bit in range(dp.bit_length() - 1)]
    core = [1] if inner > 0 else []
    return along + across + rows + core, along + rows + across + core


def after(value, *others):
    return lax.optimization_barrier((value, *others))[0]


def move(value, mask, count):
    return lax.ppermute(value, AXES, xor_pairs(count, mask))


def spread(held, have, mask, me, count):
    axis = len([other for other in have if other > mask])
    own = jnp.expand_dims(held, axis)
    got = jnp.expand_dims(move(held, mask, count), axis)
    high = jnp.bitwise_and(me, mask) != 0
    return jnp.where(high, jnp.concatenate([got, own], axis), jnp.concatenate([own, got], axis))


def parted(value, have, mask, me):
    axis = len([other for other in have if other > mask])
    bit = (jnp.bitwise_and(me, mask) != 0).astype(jnp.int32)
    return (
        lax.dynamic_index_in_dim(value, bit, axis, keepdims=False),
        lax.dynamic_index_in_dim(value, 1 - bit, axis, keepdims=False),
    )


def joined(keep, got, dtype=BF):
    return (keep.astype(F32) + got.astype(F32)).astype(dtype)


def shrink(value, have, mask, me, count, dtype=BF):
    keep, send = parted(value, have, mask, me)
    return joined(keep, move(send, mask, count), dtype)


def cost(micros):
    return pl.CostEstimate(flops=int(micros * 1.0e9), bytes_accessed=1024, transcendentals=0)


def on_device(
    sizes, tokens, routes, lengths, ln1_gain, ln1_bias, w_query, w_key, w_value, w_out, w_router,
    ln2_gain, ln2_bias, w_up, b_up, w_down, b_down, cotangent
):
    dp, fsdp = sizes
    count = dp * fsdp
    total, depth = tokens.shape
    rows = lengths.shape[0]
    length = total // rows
    experts, head = w_router.shape[1], w_key.shape[1]
    segs = lengths.shape[1]
    share = w_query.shape[0]
    inner = w_up.shape[1]
    subs = inner // depth
    fast = share % 16 == 0 and fsdp >= 8 and dp >= 2
    first_width = 2 * depth + 2 * LANES
    me = lax.axis_index(AXES).astype(jnp.int32)
    core = (jnp.bitwise_and(me, 1) if fast else jnp.int32(0)).reshape(1)
    packed = (w_query, w_out, w_key, w_value, w_router, ln1_gain, ln1_bias, ln2_gain, ln2_bias, b_down, b_up)
    small = pl.pallas_call(pack_kernel, out_shape=jax.ShapeDtypeStruct((share, first_width), BF), name="pack")(*packed)
    ups = w_up.reshape(share, count, subs, share).transpose(0, 2, 1, 3).reshape(share, subs, depth)
    downs = w_down.reshape(subs, share, depth).transpose(1, 0, 2)
    large = [
        jnp.concatenate([ups[:, 2 * i : 2 * i + 2], downs[:, 2 * i : 2 * i + 2]], 1).reshape(share, 4 * depth)
        for i in range(2)
    ]
    if fast:
        orders = hops(dp, fsdp)
        steps = len(orders[0])
        early = len([m for m in orders[0][:-1] if orders[0].index(m) == orders[1].index(m)])
        blocks, block, n = count // 2, share, 2
        dims = (2,) * (steps - 1)

        def grow(held, order, at):
            return spread(held, order[:at], order[at], me, count)

        def flat(value):
            return value.reshape(blocks, block, value.shape[-1])

        held = grow(small, orders[0], 0)
        big = after(jnp.concatenate(large, 1), held)
        for at in range(1, early):
            held = grow(held, orders[0], at)
        big = grow(big, orders[0], 0)
        for at in range(early, steps - 2):
            held = grow(held, orders[0], at)
        held = after(held, big)
        for at in range(1, early):
            big = grow(big, orders[0], at)
        held = flat(grow(held, orders[0], steps - 2))
        held = after(held, big)
        w_pieces = [held, move(held, orders[0][-1], count)]
        big = [after(half, w_pieces[1]) for half in (big[..., : 4 * depth], big[..., 4 * depth :])]
        pending = list(range(early, steps - 1))
    else:
        blocks, block, n = 1, depth, 1
        w_pieces = [lax.all_gather(small, AXES, axis=0, tiled=True)[None]]
        f_pieces = [[lax.all_gather(half, AXES, axis=0, tiled=True)[None]] for half in large]

    smem = pl.BlockSpec(memory_space=pltpu.SMEM)
    hbm = pl.BlockSpec(memory_space=pl.ANY)
    dma = pltpu.SemaphoreType.DMA

    def whole(dims):
        return pl.BlockSpec(dims, lambda *_: (0,) * len(dims))

    def shape(dims, dtype):
        return jax.ShapeDtypeStruct(dims, dtype)

    def keep_far(value):
        return pltpu.with_memory_space_constraint(value, pltpu.HBM)

    def far(dims, dtype):
        return pltpu.HBM(dims, dtype)

    def call(kernel, name, micros, grid, ins, in_specs, outs, out_specs, scratch):
        return pl.pallas_call(
            kernel, grid=grid, in_specs=in_specs, out_specs=out_specs, out_shape=outs, scratch_shapes=scratch,
            compiler_params=pltpu.CompilerParams(vmem_limit_bytes=ROOM[name] << 20), cost_estimate=cost(micros), name=name,
        )(*ins)

    span = min(STEP, length)
    tiles = total // span
    per_row = length // span

    def tile(wide):
        return pl.BlockSpec((span, wide), lambda t: (t, 0))

    def pair(wide):
        return pl.BlockSpec((2, span, wide), lambda t: (0, t, 0))

    def row_tile(wide):
        return pl.BlockSpec((span, wide), lambda r, t: (r * per_row + t, 0))

    def row_pair(wide):
        return pl.BlockSpec((2, span, wide), lambda r, t: (0, r * per_row + t, 0))

    def by_row(wide):
        return pl.BlockSpec((length, wide), lambda r, t: (r, 0))

    hid, qa, kx, vx, pr, vec = call(
        functools.partial(project_kernel, n, length, segs, experts), "project", 9.0, (tiles,),
        (core, lengths, tokens, routes, *w_pieces),
        [smem, smem, tile(depth), tile(2)] + [hbm] * n,
        [
            shape((total, depth), BF), shape((2, total, LANES), BF), shape((total, 2 * LANES), BF),
            shape((total, 2 * LANES), BF), shape((total, LANES), F32), shape((32, depth), F32),
        ],
        [tile(depth), pair(LANES), tile(2 * LANES), tile(2 * LANES), tile(LANES), whole((32, depth))],
        [pltpu.VMEM((depth, depth + 2 * LANES), BF), pltpu.VMEM((LANES, depth), F32), dma],
    )
    if fast:
        big = [grow(half, order, pending[0]) for half, order in zip(big, orders)]
        qa = after(qa, *big)
        big = [after(half, kx) for half in big]
    o, u, qf = call(
        functools.partial(attend_kernel, segs), "attend", 13.0, (rows, per_row),
        (lengths, routes, qa, kx, vx, pr),
        [smem, row_tile(2), row_pair(LANES), by_row(2 * LANES), by_row(2 * LANES), row_tile(LANES)],
        [shape((total, LANES), F32), shape((total, depth), BF), shape((2, total, LANES), BF)],
        [row_tile(LANES), row_tile(depth), row_pair(LANES)],
        [],
    )
    if fast:
        for at in pending[1:]:
            big = [grow(half, order, at) for half, order in zip(big, orders)]
        big = [flat(half) for half in big]
        u = after(u, *big)
        big = [after(half, o) for half in big]
        f_pieces = [[half, move(half, orders[0][-1], count)] for half in big]
    x1, h2 = call(
        functools.partial(mix_kernel, n), "mix", 5.0, (tiles,),
        (core, tokens, u, vec, *w_pieces),
        [smem, tile(depth), tile(depth), whole((32, depth))] + [hbm] * n,
        [far((total, depth), F32), shape((total, depth), BF)],
        [tile(depth), tile(depth)],
        [pltpu.VMEM((depth, depth), BF), dma],
    )
    flat_f = [piece for half in f_pieces for piece in half]

    wide = 256

    def once(dims):
        return pl.BlockSpec(dims, lambda *_: (0,) * len(dims), pipeline_mode=pl.Buffered(1))

    column = pl.BlockSpec((total, wide), lambda s: (0, jnp.minimum(s, inner // wide - 1)))
    act, dz, bias, *f_grads = call(
        functools.partial(ffn_kernel, n), "feed", 25.0, (inner // wide + 1,),
        (core, h2, cotangent, vec, *flat_f),
        [smem, once((total, depth)), once((total, depth)), whole((32, depth))] + [hbm] * 2 * n,
        [far((total, inner), BF), far((total, inner), BF), shape((8, depth), F32)]
        + [shape((blocks, block, 4 * depth), BF)] * 2 * n,
        [column, column, whole((8, depth))] + [hbm] * 2 * n,
        [
            pltpu.VMEM((2, depth, inner // 2), BF), pltpu.VMEM((inner, depth), BF), pltpu.VMEM((depth + 16, total), BF),
            pltpu.VMEM((depth, total), BF), pltpu.VMEM((2, total, wide), BF), pltpu.VMEM((2, total, wide), BF),
            pltpu.VMEM((2, depth, inner), BF), pltpu.SemaphoreType.DMA((2,)), dma,
        ],
    )
    f_grads = [f_grads[:n], f_grads[n:]]
    dx1, low, sums = call(
        functools.partial(turn_kernel, n), "turn", 12.0, (tiles,),
        (core, keep_far(dz), cotangent, keep_far(x1), vec, *flat_f),
        [smem, tile(inner), tile(depth), tile(depth), whole((32, depth))] + [hbm] * 2 * n,
        [shape((total, depth), F32), shape((total, depth), BF), shape((32, depth), F32)],
        [tile(depth), tile(depth), whole((32, depth))],
        [pltpu.VMEM((2, depth, inner // 2), BF), dma],
    )
    if fast:
        back_orders = [list(reversed(order[:-1])) for order in orders]

        def fall(value, order, at, dtype=BF):
            return shrink(value, order[at:], order[at], me, count, dtype)

        acc = [joined(half[0], move(half[1], orders[0][-1], count)).reshape(*dims, block, 4 * depth) for half in f_grads]
        low = after(low, *acc)
        acc = [after(a, dx1) for a in acc]
        acc = [fall(a, order, 0) for a, order in zip(acc, back_orders)]
    da, df, ds, loads, go = call(
        functools.partial(gates_kernel, n), "gates", 9.0, (tiles,),
        (core, low, routes, pr, o, u, *w_pieces),
        [smem, tile(depth), tile(2), tile(LANES), tile(LANES), tile(depth)] + [hbm] * n,
        [
            shape((2, total, LANES), BF), shape((2, total, LANES), BF), shape((total, LANES), BF), shape((8, LANES), F32),
            shape((depth, depth), BF),
        ],
        [pair(LANES), pair(LANES), tile(LANES), whole((8, LANES)), whole((depth, depth))],
        [pltpu.VMEM((depth, depth), BF), pltpu.VMEM((depth, depth), F32), dma],
    )
    if fast:
        da = after(da, *acc)
        acc = [after(a, ds) for a in acc]
        acc = [fall(a, order, 1) for a, order in zip(acc, back_orders)]

    dq, kv = call(
        attend_back_kernel, "attend_back", 18.0, (rows, per_row),
        (routes, qa, qf, kx, vx, da, df),
        [row_tile(2), row_pair(LANES), row_pair(LANES), by_row(2 * LANES), by_row(2 * LANES), row_pair(LANES), row_pair(LANES)],
        [shape((total, depth), BF), shape((total, LANES), BF)],
        [row_tile(depth), by_row(LANES)],
        [
            pltpu.VMEM((LANES, length), F32), pltpu.VMEM((LANES, length), F32), pltpu.VMEM((2 * span, length), BF),
            pltpu.VMEM((2 * span, length), BF),
        ],
    )
    if fast:
        kv = after(kv, *acc)
        late = back_orders[0]
        acc = jnp.concatenate([after(a, dq) for a in acc], -1)
        acc = fall(acc, late, 2, F32 if len(late) == 3 else BF)
    w_grads = call(
        functools.partial(sum_kernel, n, block, experts), "sums", 6.0, (tiles,),
        (core, hid, dq, kv, ds, sums, bias, loads, go, *w_pieces),
        [
            smem, tile(depth), tile(depth), tile(LANES), tile(LANES), whole((32, depth)), whole((8, depth)),
            whole((8, LANES)), whole((depth, depth)),
        ]
        + [hbm] * n,
        [shape((blocks, block, first_width), BF)] * n,
        [hbm] * n,
        [
            pltpu.VMEM((depth, depth + 2 * LANES), BF), pltpu.VMEM((depth + 16, depth), F32),
            pltpu.VMEM((depth + 16, 2 * LANES), F32), pltpu.VMEM((LANES, depth), F32),
            pltpu.VMEM((depth, first_width), BF), dma, dma,
        ],
    )
    closing = dx1
    if fast:
        tail = joined(w_grads[0], move(w_grads[1], orders[0][-1], count)).reshape(*dims, block, first_width)
        closing = after(dx1, tail, acc)
        for at in range(3, len(late)):
            acc = fall(after(acc, tail), late, at, F32 if at == len(late) - 1 else BF)
        tail = fall(tail, late, 0)
    grad_tokens = call(
        functools.partial(close_kernel, n), "close", 6.0, (tiles,),
        (core, closing, dq, kv, ds, tokens, vec, *w_pieces),
        [smem, tile(depth), tile(depth), tile(LANES), tile(LANES), tile(depth), whole((32, depth))] + [hbm] * n,
        [shape((total, depth), BF)],
        [tile(depth)],
        [pltpu.VMEM((depth, depth + 2 * LANES), BF), dma],
    )[0]
    closing = x1
    if fast:
        closing = after(x1, tail, acc)
        tail = after(tail, grad_tokens)
        tail = fall(tail, late, 1)
    result = call(
        functools.partial(result_kernel, n), "result", 6.0, (tiles,),
        (core, act, closing, vec, *flat_f),
        [smem, tile(inner), tile(depth), whole((32, depth))] + [hbm] * 2 * n,
        [shape((total, depth), BF)],
        [tile(depth)],
        [pltpu.VMEM((inner, depth), BF), dma],
    )[0]

    if fast:
        tail = after(tail, result)
        for at in range(2, len(late)):
            tail = fall(tail, late, at, F32 if at == len(late) - 1 else BF)
        own_f = [acc[:, : 4 * depth], acc[:, 4 * depth :]]
        grad_out = tail[:, depth : 2 * depth]
        own_w = tail
        load = own_w[:experts, 2 * depth + LANES + LOAD]
    else:
        def scattered(value):
            return lax.psum_scatter(value[0].astype(F32), AXES, scatter_dimension=0, tiled=True)

        own_f = [scattered(half[0]) for half in f_grads]
        own_w = scattered(w_grads[0])
        grad_out = own_w[:, depth : 2 * depth]
        load = lax.psum(w_grads[0][0][:experts, 2 * depth + LANES + LOAD].astype(F32), AXES)
    extra = own_w[:, 2 * depth + LANES :]
    grad_up = jnp.concatenate([half[:, : 2 * depth] for half in own_f], 1)
    grad_up = grad_up.reshape(share, subs, count, share).transpose(0, 2, 1, 3).reshape(share, inner)
    grad_down = jnp.concatenate([half[:, 2 * depth :] for half in own_f], 1)
    grad_down = grad_down.reshape(share, subs, depth).transpose(1, 0, 2).reshape(subs * share, depth)
    return (
        result,
        grad_tokens,
        extra[:, G1],
        extra[:, B1],
        own_w[:, 0:depth],
        own_w[:, 2 * depth : 2 * depth + head],
        own_w[:, 2 * depth + head : 2 * depth + 2 * head],
        grad_out,
        extra[:, 0:experts],
        extra[:, G2],
        extra[:, B2],
        grad_up,
        extra[:, BU : BU + subs].T.reshape(subs * share),
        grad_down,
        extra[:, BD],
        load / (total * count),
    )


def solution(mesh):
    over = P(AXES)
    flat = P(AXES, None)
    sizes = (mesh.shape["dp"], mesh.shape["fsdp"])
    return jax.shard_map(
        functools.partial(on_device, sizes),
        mesh=mesh,
        in_specs=(
            flat, flat, flat, over, over, flat, flat, flat, flat, flat, over, over, flat, over, flat, over, flat,
        ),
        out_specs=(
            flat, flat, over, over, flat, flat, flat, flat, flat, over, over, flat, over, flat, over, P(),
        ),
        check_vma=False,
    )
```

```python
import functools

import jax
import jax.numpy as jnp
from jax import lax
from jax.experimental import pallas as pl
from jax.experimental.pallas import tpu as pltpu
from jax.sharding import PartitionSpec as P

AXES = ("dp", "fsdp")
F32 = jnp.float32
BF = jnp.bfloat16
FAR = -1e30
LANES = 128
G1, B1, G2, B2, BD, BU, LOAD = 8, 9, 10, 11, 12, 13, 17
TILE = 256
STEP = 512
ROOM = {
    "project": 12, "attend": 14, "mix": 10, "feed": 29, "turn": 18, "gates": 12, "attend_back": 28, "sums": 14, "close": 14,
    "result": 18,
}


def nn(left, right):
    return jnp.dot(left, right, preferred_element_type=F32)


def nt(left, right):
    return lax.dot_general(left, right, (((1,), (1,)), ((), ())), preferred_element_type=F32)


def iota(shape, dim):
    return lax.broadcasted_iota(jnp.int32, shape, dim)


def normed(value):
    center = value - jnp.mean(value, -1, keepdims=True)
    inv = lax.rsqrt(jnp.mean(center * center, -1, keepdims=True) + 1e-05)
    return center * inv, inv


def fetch(core, pieces, parts, sem):
    for other, piece in enumerate(pieces):
        own = jnp.bitwise_xor(core, other)
        for start, wide, dst in parts:
            blocks, block, _ = piece.shape
            view = dst.reshape(blocks, len(pieces), block, wide)
            pltpu.make_async_copy(piece.at[:, :, start : start + wide], view.at[:, own], sem).start()


def arrive(dst, sem):
    pltpu.make_async_copy(dst, dst, sem).wait()


def scatter(core, pieces, src, sem):
    for other, piece in enumerate(pieces):
        own = jnp.bitwise_xor(core, other)
        blocks, block, wide = piece.shape
        view = src.reshape(blocks, len(pieces), block, wide)
        pltpu.make_async_copy(view.at[:, own], piece, sem).start()


def ffn_parts(wu, wd, half, depth, up, down):
    parts = []
    if up:
        parts.append((0, 2 * depth, wu.at[half]))
    if down:
        parts += [((2 + j) * depth, depth, wd.at[pl.ds((2 * half + j) * depth, depth), :]) for j in range(2)]
    return parts


def pack_kernel(wq, wo, wk, wv, wr, g1, b1, g2, b2, bd, bu, up, down, o, big_o):
    share, depth = wq.shape
    head, experts = wk.shape[1], wr.shape[0]
    same = iota((share, share), 0) == iota((share, share), 1)
    lane = iota((share, LANES), 1)

    def column(v):
        return jnp.sum(jnp.where(same, jnp.broadcast_to(v.astype(F32), (share, share)), 0.0), 1, keepdims=True)

    out = jnp.zeros((share, LANES), F32)
    for at, v in zip((G1, B1, G2, B2, BD), (g1, b1, g2, b2, bd)):
        out = jnp.where(lane == at, column(v[...].reshape(1, share)), out)
    flat = bu[...].reshape(1, bu.shape[0])
    for j in range(bu.shape[0] // share):
        out = jnp.where(lane == BU + j, column(flat[:, j * share : (j + 1) * share]), out)
    o[:, 0:depth] = wq[...]
    o[:, depth : depth + head] = wk[...]
    o[:, depth + head : depth + LANES] = wv[...]
    o[:, depth + LANES : depth + 2 * LANES] = out.astype(BF)
    o[:, depth + LANES : depth + LANES + experts] = nt(jnp.where(same, 1.0, 0.0).astype(BF), wr[...]).astype(BF)
    o[:, depth + 2 * LANES :] = wo[...]
    subs = bu.shape[0] // share
    wide = subs * LANES
    row, col = iota((wide, wide), 0), iota((wide, wide), 1)
    at = lax.div(lax.rem(row, subs * share), share) * LANES + lax.div(row, subs * share) * share + lax.rem(row, share)
    turn = jnp.where(at == col, 1.0, 0.0).astype(BF)
    for part in range(up.shape[1] // wide):
        moved = nn(up[:, part * wide : (part + 1) * wide], turn).astype(BF)
        for j in range(subs):
            place = (j // 2) * 4 * depth + (j % 2) * depth + part * LANES
            big_o[:, place : place + LANES] = moved[:, j * LANES : (j + 1) * LANES]
    for j in range(subs):
        place = (j // 2) * 4 * depth + (2 + j % 2) * depth
        big_o[:, place : place + depth] = down[j * share : (j + 1) * share, :]


def split3(value):
    high = value.astype(BF).astype(F32)
    rest = value - high
    mid = rest.astype(BF).astype(F32)
    return high, mid, rest - mid


def three(lane, value):
    high, mid, rest = split3(value)
    return jnp.where(lane == 4, -high, jnp.where(lane == 5, -mid, jnp.where(lane == 6, -rest, 0.0)))


def segment_of(lens, row, start, rows):
    place = iota((rows, LANES), 0) + start
    end = lens[row, 0]
    seg = (place >= end).astype(jnp.int32)
    for j in range(1, lens.shape[1]):
        end = end + lens[row, j]
        seg = seg + (place >= end).astype(jnp.int32)
    return seg


def pick(routes, rows, slot):
    return jnp.broadcast_to(routes[rows, slot : slot + 1], (TILE, LANES))


def chosen(wide, expert, half):
    out = jnp.zeros(expert.shape, F32)
    for j in range(wide.shape[1] // LANES):
        out = jnp.where(expert == 2 * j + half, wide[:, j * LANES : (j + 1) * LANES], out)
    return out


def project_kernel(n, length, segs, experts, me, lens, tok, routes, *refs):
    hid_o, qa_o, kx_o, vx_o, pr_o, vec_o, w, vec, sem = refs[n:]
    span, depth = tok.shape
    step = pl.program_id(0)
    row = lax.div(step * span, length)
    begin = lax.rem(step * span, length)

    @pl.when(step == 0)
    def _():
        fetch(me[0], refs[:n], [(0, depth + 2 * LANES, w)], sem)
        arrive(w, sem)
        vec[...] = w[:, depth + LANES :].astype(F32).T
        vec_o[...] = vec[0:32, :]

    lane = iota((TILE, LANES), 1)
    half = lane // 64
    low = lane < 64
    parts = [slice(c * TILE, (c + 1) * TILE) for c in range(span // TILE)]
    for rows in parts:
        unit, _ = normed(tok[rows, :].astype(F32))
        hid_o[rows, :] = (unit * vec[G1 : G1 + 1, :] + vec[B1 : B1 + 1, :]).astype(BF)
    products = [(nn(hid_o[rows, :], w[:, 0:depth]), nn(hid_o[rows, :], w[:, depth:])) for rows in parts]
    for c, rows in enumerate(parts):
        query, small = products[c]
        kv = small[:, :LANES].astype(BF).astype(F32)
        swap = pltpu.roll(kv, 64, 1)
        seg = segment_of(lens, row, begin + c * TILE, TILE)
        same = jnp.where(lane == seg, 1.0, 0.0)
        kx_o[rows, 0:LANES] = jnp.where(low, kv, swap).astype(BF)
        kx_o[rows, LANES:] = jnp.where(lane < segs, same, jnp.where(lane < 8, 1.0, 0.0)).astype(BF)
        vx_o[rows, 0:LANES] = jnp.where(low, swap, kv).astype(BF)
        vx_o[rows, LANES:] = jnp.ones((TILE, LANES), BF)
        logits = jnp.where(lane < experts, small[:, LANES:], FAR)
        raised = jnp.exp(logits - jnp.max(logits, -1, keepdims=True))
        pr_o[rows, :] = raised / jnp.sum(raised, -1, keepdims=True)
        for slot in range(2):
            qa_o[slot, rows, :] = (chosen(query, pick(routes, rows, slot), half) * 0.125).astype(BF)


def attend_kernel(segs, lens, routes, qa, kx, vx, pr, o_o, u_o, qf_o):
    span, depth = u_o.shape
    row, step = pl.program_id(0), pl.program_id(1)
    lane = iota((TILE, LANES), 1)
    half = lane // 64
    low = lane < 64
    for c in range(span // TILE):
        rows = slice(c * TILE, (c + 1) * TILE)
        seg = segment_of(lens, row, step * span + c * TILE, TILE)
        apart = jnp.where((lane < segs) & (lane != seg), FAR, 0.0)
        probs = pr[rows, :]
        seen, gated, experts_of = [], [], []
        for slot in range(2):
            expert = pick(routes, rows, slot)
            scores = nt(jnp.concatenate([qa[slot, rows, :], apart.astype(BF)], 1), kx[...])
            top = jnp.max(scores, -1, keepdims=True)
            raised = jnp.exp(scores - top).astype(BF)
            both = nn(raised, vx[...])
            mass = both[:, LANES:]
            out = both[:, :LANES] / mass
            qf_o[slot, rows, :] = (apart + three(lane, top + jnp.log(mass))).astype(BF)
            gate = jnp.sum(jnp.where(lane == expert, probs, 0.0), -1, keepdims=True)
            seen.append(out)
            gated.append(out * gate)
            experts_of.append(expert)
        o_o[rows, :] = jnp.where(low, seen[0], seen[1])
        for j in range(depth // LANES):
            part = jnp.where(experts_of[0] == 2 * j + half, gated[0], jnp.where(experts_of[1] == 2 * j + half, gated[1], 0.0))
            u_o[rows, j * LANES : (j + 1) * LANES] = part.astype(BF)


def mix_kernel(n, me, tok, u, vec, *refs):
    x1_o, h2_o, w, sem = refs[n:]
    span, depth = tok.shape

    @pl.when(pl.program_id(0) == 0)
    def _():
        fetch(me[0], refs[:n], [(depth + 2 * LANES, depth, w)], sem)
        arrive(w, sem)

    parts = [slice(c * TILE, (c + 1) * TILE) for c in range(span // TILE)]
    products = [nn(u[rows, :], w[...]) for rows in parts]
    for rows, product in zip(parts, products):
        after = tok[rows, :].astype(F32) + product
        x1_o[rows, :] = after
        unit, _ = normed(after)
        h2_o[rows, :] = (unit * vec[G2 : G2 + 1, :] + vec[B2 : B2 + 1, :]).astype(BF)


def ffn_kernel(n, me, h2, dy, vec, *refs):
    pieces = [refs[:n], refs[n : 2 * n]]
    act_o, dz_o, bias_o = refs[2 * n : 2 * n + 3]
    grads = [refs[2 * n + 3 : 3 * n + 3], refs[3 * n + 3 : 4 * n + 3]]
    wu, wd, ht, yt, acts, dzs, out, sem, out_sem = refs[4 * n + 3 :]
    step = pl.program_id(0)
    steps = pl.num_programs(0) - 1
    total, wide = act_o.shape
    depth = h2.shape[1]
    per = depth // wide
    some = wu.shape[2]

    @pl.when(step == 0)
    def _():
        for half in range(2):
            fetch(me[0], pieces[half], ffn_parts(wu, wd, half, depth, True, True), sem.at[half])
        for t in range(0, total, STEP):
            ht[0:depth, t : t + STEP] = h2[t : t + STEP, :].T
            yt[:, t : t + STEP] = dy[t : t + STEP, :].T
        ht[depth:, :] = jnp.ones((16, total), BF)

    for half in range(2):
        @pl.when(step == half * steps // 2)
        def _():
            arrive(wu.at[half], sem.at[half])
            arrive(wd.at[pl.ds(half * some, some), :], sem.at[half])

    one = 0.7978845608028654
    two = one * 0.044715
    cur = lax.rem(step, 2)

    def place(t):
        sub = lax.div(t, per)
        return sub, lax.rem(t, per), lax.rem(sub, 2) * depth, lax.div(sub, 2)

    def grad_up(t, slot):
        sub, part, column, half = place(t)
        up = nn(ht[...], dzs[slot])
        out[half, :, pl.ds(pl.multiple_of(column + part * wide, wide), wide)] = up[0:depth, :].astype(BF)
        bias_o[pl.ds(sub, 1), pl.ds(pl.multiple_of(part * wide, wide), wide)] = up[depth : depth + 1, :]

    def grad_down(t, slot):
        _, part, column, half = place(t)
        rows = pl.ds(pl.multiple_of(part * wide, wide), wide)
        out[half, rows, pl.ds(pl.multiple_of(column + 2 * depth, depth), depth)] = nn(yt[...], acts[slot]).T.astype(BF)

    @pl.when(step < steps)
    def _():
        before = jnp.maximum(step - 1, 0)
        sub, part, column, which = place(step)
        here = pl.ds(pl.multiple_of(step * wide, wide), wide)
        across = pl.ds(pl.multiple_of(column + part * wide, wide), wide)
        bias = vec[pl.ds(BU + sub, 1), pl.ds(pl.multiple_of(part * wide, wide), wide)]
        count = total // TILE
        for c in range(count):
            rows = slice(c * TILE, (c + 1) * TILE)
            z = nn(h2[rows, :], wu[which, :, across]) + bias
            dact = nt(dy[rows, :], wd[here, :])
            if c == 0:
                grad_up(before, 1 - cur)
            if c == count // 2:
                grad_down(before, 1 - cur)
            square = z * z
            tanh = jnp.tanh(z * (one + two * square))
            half = 0.5 * tanh + 0.5
            act = z * half
            slope = half + act * (1.0 - tanh) * (one + 3.0 * two * square)
            act = act.astype(BF)
            dz = (dact * slope).astype(BF)
            act_o[rows, :] = act
            dz_o[rows, :] = dz
            acts[cur, rows, :] = act
            dzs[cur, rows, :] = dz

    @pl.when(step == steps // 2)
    def _():
        scatter(me[0], grads[0], out.at[0], out_sem)

    @pl.when(step == steps)
    def _():
        grad_up(steps - 1, 1 - cur)
        grad_down(steps - 1, 1 - cur)
        scatter(me[0], grads[1], out.at[1], out_sem)
        arrive(out, out_sem)


def turn_kernel(n, again, me, dz, dy, x1, vec, *refs):
    if again:
        before, refs = refs[0], refs[3:]
    dx1_o, low_o, sums_o, wu, f_sem = refs[2 * n :]
    span, depth = dy.shape
    step = pl.program_id(0)

    @pl.when(step == 0)
    def _():
        for half in range(2):
            fetch(me[0], refs[half * n : half * n + n], ffn_parts(wu, None, half, depth, True, False), f_sem)
        sums_o[...] = before[...] if again else jnp.zeros_like(sums_o)
        arrive(wu, f_sem)

    parts = [slice(c * TILE, (c + 1) * TILE) for c in range(span // TILE)]
    products = [nt(dz[rows, 0 : 2 * depth], wu[0]) + nt(dz[rows, 2 * depth :], wu[1]) for rows in parts]
    for rows, dh2 in zip(parts, products):
        unit, inv = normed(x1[rows, :])
        grad = dy[rows, :].astype(F32)
        sums_o[G2 : G2 + 1, :] += jnp.sum(dh2 * unit, 0, keepdims=True)
        sums_o[B2 : B2 + 1, :] += jnp.sum(dh2, 0, keepdims=True)
        sums_o[BD : BD + 1, :] += jnp.sum(grad, 0, keepdims=True)
        scaled = dh2 * vec[G2 : G2 + 1, :]
        one = jnp.mean(scaled, -1, keepdims=True)
        two = jnp.mean(scaled * unit, -1, keepdims=True)
        dx1 = grad + inv * (scaled - one - unit * two)
        dx1_o[rows, :] = dx1
        low_o[rows, :] = dx1.astype(BF)


def gates_kernel(n, me, dx1, routes, pr, o, u, *refs):
    da_o, df_o, ds_o, load_o, go_o, w, go, sem = refs[n:]
    span, depth = dx1.shape
    step = pl.program_id(0)

    @pl.when(step == 0)
    def _():
        fetch(me[0], refs[:n], [(depth + 2 * LANES, depth, w)], sem)
        go[...] = jnp.zeros_like(go)
        load_o[...] = jnp.zeros_like(load_o)
        arrive(w, sem)

    lane = iota((TILE, LANES), 1)
    half = lane // 64
    low = lane < 64
    go[...] += nn(u[...].T, dx1[...])
    parts = [slice(c * TILE, (c + 1) * TILE) for c in range(span // TILE)]
    products = [nt(dx1[rows, :], w[...]) for rows in parts]
    for rows, product in zip(parts, products):
        du = product.astype(BF).astype(F32)
        probs = pr[rows, :]
        heads = o[rows, :]
        swap = pltpu.roll(heads, 64, 1)
        dprobs = jnp.zeros((TILE, LANES), F32)
        loads = jnp.zeros((TILE, LANES), F32)
        for slot in range(2):
            expert = pick(routes, rows, slot)
            own = chosen(du, expert, half)
            here = lane == expert
            gate = jnp.sum(jnp.where(here, probs, 0.0), -1, keepdims=True)
            seen = jnp.where(low, heads, swap) if slot == 0 else jnp.where(low, swap, heads)
            dgate = jnp.sum(own * seen, -1, keepdims=True)
            da = (own * gate).astype(BF)
            da_o[slot, rows, :] = da
            df_o[slot, rows, :] = three(lane, jnp.sum(da.astype(F32) * seen, -1, keepdims=True)).astype(BF)
            dprobs = jnp.where(here, dgate, dprobs)
            loads = jnp.where(here, 1.0, loads)
        load_o[0:1, :] += jnp.sum(loads, 0, keepdims=True)
        inner = jnp.sum(dprobs * probs, -1, keepdims=True)
        ds_o[rows, :] = (probs * (dprobs - inner)).astype(BF)

    @pl.when(step == pl.num_programs(0) - 1)
    def _():
        go_o[...] = go[...].astype(BF)


def attend_back_kernel(routes, qa, qf, kx, vx, da, df, *refs):
    dq_o, kv_o, dk, dv, ds, ps = refs[-6:]
    span, depth = dq_o.shape
    step = pl.program_id(0)
    lane = iota((TILE, LANES), 1)
    half = lane // 64

    for slot in range(2):
        own = slice(slot * span, (slot + 1) * span)
        probs = jnp.exp(nt(jnp.concatenate([qa[slot], qf[slot]], 1), kx[...]))
        ps[own, :] = probs.astype(BF)
        away = nt(jnp.concatenate([da[slot], df[slot]], 1), vx[...])
        ds[own, :] = (probs * away).astype(BF)
    dk_part = nn(jnp.concatenate([qa[0].T, qa[1].T], 1), ds[...])
    dv_part = nn(jnp.concatenate([da[0].T, da[1].T], 1), ps[...])
    found = nn(ds[...], kx[:, 0:LANES]) * 0.125
    for c in range(span // TILE):
        rows = slice(c * TILE, (c + 1) * TILE)
        others = slice(span + c * TILE, span + (c + 1) * TILE)
        one, two = pick(routes, rows, 0), pick(routes, rows, 1)
        for j in range(depth // LANES):
            part = jnp.where(one == 2 * j + half, found[rows, :], jnp.where(two == 2 * j + half, found[others, :], 0.0))
            dq_o[rows, j * LANES : (j + 1) * LANES] = part.astype(BF)

    @pl.when(step == 0)
    def _():
        dk[...] = dk_part
        dv[...] = dv_part

    @pl.when(step > 0)
    def _():
        dk[...] += dk_part
        dv[...] += dv_part

    @pl.when(step == pl.num_programs(0) - 1)
    def _():
        for c in range(kv_o.shape[0] // TILE):
            rows = slice(c * TILE, (c + 1) * TILE)
            both = jnp.concatenate([dk[0:64, rows] + dk[64:, rows], dv[0:64, rows] + dv[64:, rows]], 0)
            kv_o[rows, :] = both.T.astype(BF)


def sum_kernel(n, block, experts, me, hid, dq, kv, ds, sums, bias, loads, go, *refs):
    w, gq, gs, all_sums, out, sem, out_sem = refs[2 * n :]
    span, depth = hid.shape
    step = pl.program_id(0)

    @pl.when(step == 0)
    def _():
        fetch(me[0], refs[:n], [(0, depth + 2 * LANES, w)], sem)
        gq[...] = jnp.zeros_like(gq)
        gs[...] = jnp.zeros_like(gs)

    turned = jnp.concatenate([hid[...].T, jnp.ones((16, span), BF)], 0)
    gq[...] += nn(turned, dq[...])
    gs[...] += nn(turned, jnp.concatenate([kv[...], ds[...]], 1))

    @pl.when(step == pl.num_programs(0) - 1)
    def _():
        arrive(w, sem)
        all_sums[...] = jnp.zeros_like(all_sums)
        all_sums[0:32, :] = sums[...]
        all_sums[BU : BU + 4, :] = bias[0:4, :]
        wq = w[:, 0:depth].astype(F32)
        ws = w[:, depth:].astype(F32)
        wide = iota((depth, LANES), 1)
        ws_own = jnp.where(wide < experts, ws[:, LANES:], 0.0)
        around = jnp.sum(gq[0:depth, :] * wq, -1, keepdims=True)
        around += jnp.sum(gs[0:depth, 0:LANES] * ws[:, 0:LANES] + gs[0:depth, LANES:] * ws_own, -1, keepdims=True)
        shift = jnp.sum(gq[depth : depth + 1, :] * wq, -1, keepdims=True)
        shift += jnp.sum(
            gs[depth : depth + 1, 0:LANES] * ws[:, 0:LANES] + gs[depth : depth + 1, LANES:] * ws_own, -1, keepdims=True
        )
        gain = ws[:, LANES + G1 : LANES + G1 + 1]
        lift = ws[:, LANES + B1 : LANES + B1 + 1]
        stretch = (around - lift * shift) / gain
        place = lax.rem(iota((depth, LANES), 0), block)
        load = jnp.sum(jnp.where(wide == place, loads[0:1, :], 0.0), -1, keepdims=True)
        columns = jnp.where(wide < experts, gs[0:depth, LANES:], all_sums[...].T)
        columns = jnp.where(wide == G1, stretch, columns)
        columns = jnp.where(wide == B1, shift, columns)
        columns = jnp.where(wide == LOAD, load, columns)
        out[:, 0:depth] = gq[0:depth, :].astype(BF)
        out[:, depth : 2 * depth] = go[...]
        out[:, 2 * depth : 2 * depth + LANES] = gs[0:depth, 0:LANES].astype(BF)
        out[:, 2 * depth + LANES :] = columns.astype(BF)
        scatter(me[0], refs[n : 2 * n], out, out_sem)
        arrive(out, out_sem)


def result_kernel(n, me, act, x1, vec, *refs):
    res_o, wd, sem = refs[2 * n :]
    depth = x1.shape[1]

    @pl.when(pl.program_id(0) == 0)
    def _():
        for half in range(2):
            fetch(me[0], refs[half * n : half * n + n], ffn_parts(None, wd, half, depth, False, True), sem)
        arrive(wd, sem)

    res_o[...] = (x1[...] + vec[BD : BD + 1, :] + nn(act[...], wd[...])).astype(BF)


def close_kernel(n, me, dx1, dq, kv, ds, tok, vec, *refs):
    grad_o, w, sem = refs[n:]
    span, depth = tok.shape

    @pl.when(pl.program_id(0) == 0)
    def _():
        fetch(me[0], refs[:n], [(0, depth + 2 * LANES, w)], sem)
        arrive(w, sem)

    parts = [slice(c * TILE, (c + 1) * TILE) for c in range(span // TILE)]
    products = [
        nt(dq[rows, :], w[:, 0:depth]) + nt(jnp.concatenate([kv[rows, :], ds[rows, :]], 1), w[:, depth:]) for rows in parts
    ]
    for rows, dh in zip(parts, products):
        unit, inv = normed(tok[rows, :].astype(F32))
        scaled = dh * vec[G1 : G1 + 1, :]
        one = jnp.mean(scaled, -1, keepdims=True)
        two = jnp.mean(scaled * unit, -1, keepdims=True)
        grad_o[rows, :] = (dx1[rows, :] + inv * (scaled - one - unit * two)).astype(BF)


def finish_kernel(share_of, keep, got, gq, gk, gv, go, gr, g1, b1, g2, b2, bd, bu, load):
    share, depth = gq.shape
    head, experts = gk.shape[1], gr.shape[0]
    total = keep[...].astype(F32) + got[...].astype(F32)
    gq[...] = total[:, 0:depth]
    go[...] = total[:, depth : 2 * depth]
    gk[...] = total[:, 2 * depth : 2 * depth + head]
    gv[...] = total[:, 2 * depth + head : 2 * depth + 2 * head]
    turned = jnp.concatenate([total[:, 2 * depth + LANES :], jnp.zeros((LANES - share, LANES), F32)], 0).T
    gr[...] = turned[0:experts, 0:share]
    for at, out in zip((G1, B1, G2, B2, BD), (g1, b1, g2, b2, bd)):
        out[...] = turned[at : at + 1, 0:share].reshape(share)
    lines = [turned[BU + j : BU + j + 1, 0:share] for j in range(bu.shape[0] // share)]
    bu[...] = jnp.concatenate(lines, 1).reshape(bu.shape[0])
    load[...] = (turned[LOAD : LOAD + 1, 0:experts] * share_of).reshape(experts)


def xor_pairs(count, mask):
    return [(i, i ^ mask) for i in range(count)]


def hops(dp, fsdp):
    inner = fsdp.bit_length() - 1
    along = [1 << bit for bit in range(inner - 1, 1, -1)]
    across = [2] if inner > 1 else []
    rows = [1 << (inner + bit) for bit in range(dp.bit_length() - 1)]
    core = [1] if inner > 0 else []
    return along + across + rows + core, along + rows + across + core


def after(value, *others):
    return lax.optimization_barrier((value, *others))[0]


def move(value, mask, count):
    return lax.ppermute(value, AXES, xor_pairs(count, mask))


def spread(held, have, mask, me, count):
    axis = len([other for other in have if other > mask])
    own = jnp.expand_dims(held, axis)
    got = jnp.expand_dims(move(held, mask, count), axis)
    high = jnp.bitwise_and(me, mask) != 0
    return jnp.where(high, jnp.concatenate([got, own], axis), jnp.concatenate([own, got], axis))


def parted(value, have, mask, me):
    axis = len([other for other in have if other > mask])
    bit = (jnp.bitwise_and(me, mask) != 0).astype(jnp.int32)
    return (
        lax.dynamic_index_in_dim(value, bit, axis, keepdims=False),
        lax.dynamic_index_in_dim(value, 1 - bit, axis, keepdims=False),
    )


def joined(keep, got, dtype=BF):
    return (keep.astype(F32) + got.astype(F32)).astype(dtype)


def shrink(value, have, mask, me, count, dtype=BF):
    keep, send = parted(value, have, mask, me)
    return joined(keep, move(send, mask, count), dtype)


def cost(micros):
    return pl.CostEstimate(flops=int(micros * 1.0e9), bytes_accessed=1024, transcendentals=0)


def on_device(
    sizes, tokens, routes, lengths, ln1_gain, ln1_bias, w_query, w_key, w_value, w_out, w_router,
    ln2_gain, ln2_bias, w_up, b_up, w_down, b_down, cotangent
):
    dp, fsdp = sizes
    count = dp * fsdp
    total, depth = tokens.shape
    rows = lengths.shape[0]
    length = total // rows
    experts, head = w_router.shape[1], w_key.shape[1]
    segs = lengths.shape[1]
    share = w_query.shape[0]
    inner = w_up.shape[1]
    subs = inner // depth
    fast = share % 16 == 0 and fsdp >= 8 and dp >= 2
    first_width = 2 * depth + 2 * LANES
    me = lax.axis_index(AXES).astype(jnp.int32)
    core = (jnp.bitwise_and(me, 1) if fast else jnp.int32(0)).reshape(1)
    packed = (w_query, w_out, w_key, w_value, w_router.T, ln1_gain, ln1_bias, ln2_gain, ln2_bias, b_down, b_up, w_up, w_down)
    small, large = pl.pallas_call(
        pack_kernel,
        out_shape=[
            pltpu.VMEM((share, first_width), BF), pltpu.VMEM((share, 2 * inner), BF),
        ],
        name="pack",
    )(*packed)
    if fast:
        orders = hops(dp, fsdp)
        steps = len(orders[0])
        early = len([m for m in orders[0][:-1] if orders[0].index(m) == orders[1].index(m)])
        blocks, block, n = count // 2, share, 2
        dims = (2,) * (steps - 1)

        def grow(held, order, at):
            return spread(held, order[:at], order[at], me, count)

        def flat(value):
            return value.reshape(blocks, block, value.shape[-1])

        held = small
        for at in range(early):
            held = grow(held, orders[0], at)
        big = grow(large, orders[0], 0)
        parts = [held[..., : first_width // 2], held[..., first_width // 2 :]]
        for at in range(early, steps - 1):
            parts = [grow(part, order, at) for part, order in zip(parts, orders)]
            if at == early:
                for other in range(1, early):
                    big = grow(after(big, *parts), orders[0], other)
        held = flat(jnp.concatenate(parts, -1))
        w_pieces = [held, move(held, orders[0][-1], count)]
        big = [after(half, w_pieces[1]) for half in (big[..., : 4 * depth], big[..., 4 * depth :])]
        pending = list(range(early, steps - 1))
    else:
        blocks, block, n = 1, depth, 1
        w_pieces = [lax.all_gather(small, AXES, axis=0, tiled=True)[None]]
        large = lax.all_gather(large, AXES, axis=0, tiled=True)[None]
        f_pieces = [[large[..., : 4 * depth]], [large[..., 4 * depth :]]]

    smem = pl.BlockSpec(memory_space=pltpu.SMEM)
    hbm = pl.BlockSpec(memory_space=pl.ANY)
    dma = pltpu.SemaphoreType.DMA

    def whole(dims):
        return pl.BlockSpec(dims, lambda *_: (0,) * len(dims))

    def shape(dims, dtype):
        return jax.ShapeDtypeStruct(dims, dtype)

    def keep_far(value):
        return pltpu.with_memory_space_constraint(value, pltpu.HBM)

    def far(dims, dtype):
        return pltpu.HBM(dims, dtype)

    def call(kernel, name, micros, grid, ins, in_specs, outs, out_specs, scratch):
        return pl.pallas_call(
            kernel, grid=grid, in_specs=in_specs, out_specs=out_specs, out_shape=outs, scratch_shapes=scratch,
            compiler_params=pltpu.CompilerParams(vmem_limit_bytes=ROOM[name] << 20), cost_estimate=cost(micros), name=name,
        )(*ins)

    span = min(STEP, length)
    tiles = total // span
    per_row = length // span

    def tile(wide):
        return pl.BlockSpec((span, wide), lambda t: (t, 0))

    def pair(wide):
        return pl.BlockSpec((2, span, wide), lambda t: (0, t, 0))

    def row_tile(wide):
        return pl.BlockSpec((span, wide), lambda r, t: (r * per_row + t, 0))

    def row_pair(wide):
        return pl.BlockSpec((2, span, wide), lambda r, t: (0, r * per_row + t, 0))

    def by_row(wide):
        return pl.BlockSpec((length, wide), lambda r, t: (r, 0))

    hid, qa, kx, vx, pr, vec = call(
        functools.partial(project_kernel, n, length, segs, experts), "project", 9.0, (tiles,),
        (core, lengths, keep_far(tokens), routes, *w_pieces),
        [smem, smem, tile(depth), tile(2)] + [hbm] * n,
        [
            far((total, depth), BF), shape((2, total, LANES), BF), far((total, 2 * LANES), BF),
            far((total, 2 * LANES), BF), shape((total, LANES), F32), shape((32, depth), F32),
        ],
        [tile(depth), pair(LANES), tile(2 * LANES), tile(2 * LANES), tile(LANES), whole((32, depth))],
        [pltpu.VMEM((depth, depth + 2 * LANES), BF), pltpu.VMEM((LANES, depth), F32), dma],
    )
    if fast:
        big = [grow(half, order, pending[0]) for half, order in zip(big, orders)]
        qa = after(qa, *big)
        big = [after(half, kx) for half in big]
    o, u, qf = call(
        functools.partial(attend_kernel, segs), "attend", 13.0, (rows, per_row),
        (lengths, routes, qa, kx, vx, pr),
        [smem, row_tile(2), row_pair(LANES), by_row(2 * LANES), by_row(2 * LANES), row_tile(LANES)],
        [shape((total, LANES), F32), shape((total, depth), BF), far((2, total, LANES), BF)],
        [row_tile(LANES), row_tile(depth), row_pair(LANES)],
        [],
    )
    if fast:
        for at in pending[1:]:
            big = [grow(half, order, at) for half, order in zip(big, orders)]
        big = [flat(half) for half in big]
        u = after(u, *big)
        big = [after(half, o) for half in big]
        f_pieces = [[half, move(half, orders[0][-1], count)] for half in big]
    x1, h2 = call(
        functools.partial(mix_kernel, n), "mix", 5.0, (tiles,),
        (core, tokens, u, vec, *w_pieces),
        [smem, tile(depth), tile(depth), whole((32, depth))] + [hbm] * n,
        [far((total, depth), F32), shape((total, depth), BF)],
        [tile(depth), tile(depth)],
        [pltpu.VMEM((depth, depth), BF), dma],
    )
    flat_f = [piece for half in f_pieces for piece in half]

    wide = 256

    def once(dims):
        return pl.BlockSpec(dims, lambda *_: (0,) * len(dims), pipeline_mode=pl.Buffered(1))

    column = pl.BlockSpec((total, wide), lambda s: (0, jnp.minimum(s, inner // wide - 1)))
    act, dz, bias, *f_grads = call(
        functools.partial(ffn_kernel, n), "feed", 25.0, (inner // wide + 1,),
        (core, h2, cotangent, vec, *flat_f),
        [smem, once((total, depth)), once((total, depth)), whole((32, depth))] + [hbm] * 2 * n,
        [far((total, inner), BF), far((total, inner), BF), shape((8, depth), F32)]
        + [far((blocks, block, 4 * depth), BF)] * 2 * n,
        [column, column, whole((8, depth))] + [hbm] * 2 * n,
        [
            pltpu.VMEM((2, depth, inner // 2), BF), pltpu.VMEM((inner, depth), BF), pltpu.VMEM((depth + 16, total), BF),
            pltpu.VMEM((depth, total), BF), pltpu.VMEM((2, total, wide), BF), pltpu.VMEM((2, total, wide), BF),
            pltpu.VMEM((2, depth, inner), BF), pltpu.SemaphoreType.DMA((2,)), dma,
        ],
    )
    f_grads = [f_grads[:n], f_grads[n:]]
    def turn(begin, again):
        def part(wide):
            return pl.BlockSpec((span, wide), lambda t: (t + begin, 0))

        return pl.pallas_call(
            functools.partial(turn_kernel, n, len(again) > 0), grid=(tiles // 2,),
            in_specs=[smem, part(inner), part(depth), part(depth), whole((32, depth))]
            + ([whole((32, depth)), hbm, hbm] if again else []) + [hbm] * 2 * n,
            out_specs=[part(depth), part(depth), whole((32, depth))],
            out_shape=[shape((total, depth), F32), shape((total, depth), BF), shape((32, depth), F32)],
            scratch_shapes=[pltpu.VMEM((2, depth, inner // 2), BF), dma],
            input_output_aliases={6: 0, 7: 1} if again else {},
            compiler_params=pltpu.CompilerParams(vmem_limit_bytes=ROOM["turn"] << 20), cost_estimate=cost(6.0), name="turn",
        )(core, keep_far(dz), cotangent, keep_far(x1), vec, *again, *flat_f)

    dx1, low, sums = turn(0, ())
    if fast:
        back_orders = [list(reversed(order[:-1])) for order in orders]
        late = back_orders[0]

        def fall(value, order, at, dtype=BF):
            return shrink(value, order[at:], order[at], me, count, dtype)

        acc = [joined(half[0], move(half[1], orders[0][-1], count)).reshape(*dims, block, 4 * depth) for half in f_grads]
        sums = after(sums, *acc)
        acc = [after(a, dx1) for a in acc]
        acc = [fall(a, order, 0) for a, order in zip(acc, back_orders)]
    dx1, low, sums = turn(tiles // 2, (sums, dx1, low))
    da, df, ds, loads, go = call(
        functools.partial(gates_kernel, n), "gates", 9.0, (tiles,),
        (core, low, routes, pr, o, u, *w_pieces),
        [smem, tile(depth), tile(2), tile(LANES), tile(LANES), tile(depth)] + [hbm] * n,
        [
            shape((2, total, LANES), BF), shape((2, total, LANES), BF), shape((total, LANES), BF), shape((8, LANES), F32),
            shape((depth, depth), BF),
        ],
        [pair(LANES), pair(LANES), tile(LANES), whole((8, LANES)), whole((depth, depth))],
        [pltpu.VMEM((depth, depth), BF), pltpu.VMEM((depth, depth), F32), dma],
    )
    if fast:
        da = after(da, *acc)
        acc = [after(a, ds) for a in acc]
        acc = [fall(a, order, 1) for a, order in zip(acc, back_orders)]

    def back(row, again):
        def part(wide):
            return pl.BlockSpec((span, wide), lambda t: (row * per_row + t, 0))

        def both(wide):
            return pl.BlockSpec((2, span, wide), lambda t: (0, row * per_row + t, 0))

        def full(wide):
            return pl.BlockSpec((length, wide), lambda t: (row, 0))

        return pl.pallas_call(
            attend_back_kernel, grid=(per_row,),
            in_specs=[part(2), both(LANES), both(LANES), full(2 * LANES), full(2 * LANES), both(LANES), both(LANES)]
            + [hbm] * len(again),
            out_specs=[part(depth), full(LANES)],
            out_shape=[shape((total, depth), BF), shape((total, LANES), BF)],
            scratch_shapes=[
                pltpu.VMEM((LANES, length), F32), pltpu.VMEM((LANES, length), F32), pltpu.VMEM((2 * span, length), BF),
                pltpu.VMEM((2 * span, length), BF),
            ],
            input_output_aliases={7: 0, 8: 1} if again else {},
            compiler_params=pltpu.CompilerParams(vmem_limit_bytes=ROOM["attend_back"] << 20), cost_estimate=cost(8.0),
            name="attend_back",
        )(routes, qa, qf, kx, vx, da, df, *again)

    dq, kv = back(0, ())
    for row in range(1, rows):
        if fast and row == 1:
            dq = after(dq, *acc)
            acc = jnp.concatenate([after(a, kv) for a in acc], -1)
            acc = fall(acc, late, 2, F32 if len(late) == 3 else BF)
        dq, kv = back(row, (dq, kv))
    if fast:
        kv = after(kv, acc)
        for at in range(3, len(late)):
            acc = fall(after(acc, dq), late, at, F32 if at == len(late) - 1 else BF)
    w_grads = call(
        functools.partial(sum_kernel, n, block, experts), "sums", 6.0, (tiles,),
        (core, hid, dq, kv, ds, sums, bias, loads, go, *w_pieces),
        [
            smem, tile(depth), tile(depth), tile(LANES), tile(LANES), whole((32, depth)), whole((8, depth)),
            whole((8, LANES)), whole((depth, depth)),
        ]
        + [hbm] * n,
        [shape((blocks, block, first_width), BF)] * n,
        [hbm] * n,
        [
            pltpu.VMEM((depth, depth + 2 * LANES), BF), pltpu.VMEM((depth + 16, depth), F32),
            pltpu.VMEM((depth + 16, 2 * LANES), F32), pltpu.VMEM((LANES, depth), F32),
            pltpu.VMEM((depth, first_width), BF), dma, dma,
        ],
    )
    closing = dx1
    if fast:
        tail = joined(w_grads[0], move(w_grads[1], orders[0][-1], count)).reshape(*dims, block, first_width)
        closing = after(dx1, tail, acc)
        tails = [tail[..., : first_width // 2], tail[..., first_width // 2 :]]
        tails = [fall(part, order, 0) for part, order in zip(tails, back_orders)]
    grad_tokens = call(
        functools.partial(close_kernel, n), "close", 6.0, (tiles,),
        (core, closing, dq, kv, ds, tokens, vec, *w_pieces),
        [smem, tile(depth), tile(depth), tile(LANES), tile(LANES), tile(depth), whole((32, depth))] + [hbm] * n,
        [shape((total, depth), BF)],
        [tile(depth)],
        [pltpu.VMEM((depth, depth + 2 * LANES), BF), dma],
    )[0]
    closing = x1
    if fast:
        closing = after(x1, *tails)
        tails = [fall(after(part, grad_tokens), order, 1) for part, order in zip(tails, back_orders)]
    result = call(
        functools.partial(result_kernel, n), "result", 6.0, (tiles,),
        (core, act, closing, vec, *flat_f),
        [smem, tile(inner), tile(depth), whole((32, depth))] + [hbm] * 2 * n,
        [shape((total, depth), BF)],
        [tile(depth)],
        [pltpu.VMEM((inner, depth), BF), dma],
    )[0]

    def unpacked(halves):
        up = jnp.concatenate([half[:, : 2 * depth] for half in halves], 1)
        up = up.reshape(share, subs, count, share).transpose(0, 2, 1, 3).reshape(share, inner)
        down = jnp.concatenate([half[:, 2 * depth :] for half in halves], 1)
        return up, down.reshape(share, subs, depth).transpose(1, 0, 2).reshape(subs * share, depth)

    if fast:
        tail = after(jnp.concatenate(tails, -1), result)
        grad_up, grad_down = unpacked([acc[:, : 4 * depth], acc[:, 4 * depth :]])
        for at in range(2, len(late) - 1):
            tail = fall(tail, late, at)
        keep, send = parted(after(tail, grad_up, grad_down), late[-1:], late[-1], me)
        own = functools.partial(jax.ShapeDtypeStruct, dtype=F32)
        grad_query, grad_key, grad_value, grad_out, grad_router, *lines = pl.pallas_call(
            functools.partial(finish_kernel, 1.0 / (total * count)),
            out_shape=[own((share, depth)), own((share, head)), own((share, head)), own((share, depth)), own((experts, share))]
            + [own((share,))] * 5 + [own((subs * share,)), own((experts,))],
            name="finish",
        )(keep, move(send, late[-1], count))
        grad_router = grad_router.T
        grad_g1, grad_b1, grad_g2, grad_b2, grad_bd, grad_bu, load = lines
    else:
        def scattered(value):
            return lax.psum_scatter(value[0].astype(F32), AXES, scatter_dimension=0, tiled=True)

        grad_up, grad_down = unpacked([scattered(half[0]) for half in f_grads])
        own_w = scattered(w_grads[0])
        load = lax.psum(w_grads[0][0][:experts, 2 * depth + LANES + LOAD].astype(F32), AXES) / (total * count)
        extra = own_w[:, 2 * depth + LANES :]
        grad_query, grad_out = own_w[:, 0:depth], own_w[:, depth : 2 * depth]
        grad_key, grad_value = own_w[:, 2 * depth : 2 * depth + head], own_w[:, 2 * depth + head : 2 * depth + 2 * head]
        grad_router = extra[:, 0:experts]
        grad_g1, grad_b1, grad_g2, grad_b2, grad_bd = [extra[:, at] for at in (G1, B1, G2, B2, BD)]
        grad_bu = extra[:, BU : BU + subs].T.reshape(subs * share)
    return (
        result, grad_tokens, grad_g1, grad_b1, grad_query, grad_key, grad_value, grad_out, grad_router, grad_g2, grad_b2,
        grad_up, grad_bu, grad_down, grad_bd, load,
    )


def solution(mesh):
    over = P(AXES)
    flat = P(AXES, None)
    sizes = (mesh.shape["dp"], mesh.shape["fsdp"])
    return jax.shard_map(
        functools.partial(on_device, sizes),
        mesh=mesh,
        in_specs=(
            flat, flat, flat, over, over, flat, flat, flat, flat, flat, over, over, flat, over, flat, over, flat,
        ),
        out_specs=(
            flat, flat, over, over, flat, flat, flat, flat, flat, over, over, flat, over, flat, over, P(),
        ),
        check_vma=False,
    )
```

```python
import functools

import jax
import jax.numpy as jnp
from jax import lax
from jax.experimental import pallas as pl
from jax.experimental.pallas import tpu as pltpu
from jax.sharding import PartitionSpec as P

AXES = ("dp", "fsdp")
F32 = jnp.float32
BF = jnp.bfloat16
FAR = -1e30
LANES = 128
G1, B1, G2, B2, BD, BU, LOAD = 8, 9, 10, 11, 12, 13, 17
TILE = 256
STEP = 512
ROOM = {
    "project": 12, "attend": 14, "mix": 10, "feed": 25, "turn": 18, "gates": 12, "attend_back": 28, "sums": 14, "close": 14,
    "result": 18,
}


def nn(left, right):
    return jnp.dot(left, right, preferred_element_type=F32)


def nt(left, right):
    return lax.dot_general(left, right, (((1,), (1,)), ((), ())), preferred_element_type=F32)


def iota(shape, dim):
    return lax.broadcasted_iota(jnp.int32, shape, dim)


def normed(value):
    center = value - jnp.mean(value, -1, keepdims=True)
    inv = lax.rsqrt(jnp.mean(center * center, -1, keepdims=True) + 1e-05)
    return center * inv, inv


def fetch(core, pieces, parts, sem):
    for other, piece in enumerate(pieces):
        own = jnp.bitwise_xor(core, other)
        for start, wide, dst in parts:
            blocks, block, _ = piece.shape
            view = dst.reshape(blocks, len(pieces), block, wide)
            pltpu.make_async_copy(piece.at[:, :, start : start + wide], view.at[:, own], sem).start()


def arrive(dst, sem):
    pltpu.make_async_copy(dst, dst, sem).wait()


def scatter(core, pieces, src, sem):
    for other, piece in enumerate(pieces):
        own = jnp.bitwise_xor(core, other)
        blocks, block, wide = piece.shape
        view = src.reshape(blocks, len(pieces), block, wide)
        pltpu.make_async_copy(view.at[:, own], piece, sem).start()


def ffn_parts(wu, wd, half, depth, up, down):
    parts = []
    if up:
        parts.append((0, 2 * depth, wu.at[half]))
    if down:
        parts += [((2 + j) * depth, depth, wd.at[pl.ds((2 * half + j) * depth, depth), :]) for j in range(2)]
    return parts


def pack_kernel(wq, wo, wk, wv, wr, g1, b1, g2, b2, bd, bu, up, down, o, big_o):
    share, depth = wq.shape
    head, experts = wk.shape[1], wr.shape[0]
    same = iota((share, share), 0) == iota((share, share), 1)
    lane = iota((share, LANES), 1)

    def column(v):
        return jnp.sum(jnp.where(same, jnp.broadcast_to(v.astype(F32), (share, share)), 0.0), 1, keepdims=True)

    out = jnp.zeros((share, LANES), F32)
    for at, v in zip((G1, B1, G2, B2, BD), (g1, b1, g2, b2, bd)):
        out = jnp.where(lane == at, column(v[...].reshape(1, share)), out)
    flat = bu[...].reshape(1, bu.shape[0])
    for j in range(bu.shape[0] // share):
        out = jnp.where(lane == BU + j, column(flat[:, j * share : (j + 1) * share]), out)
    o[:, 0:depth] = wq[...]
    o[:, depth : depth + head] = wk[...]
    o[:, depth + head : depth + LANES] = wv[...]
    o[:, depth + LANES : depth + 2 * LANES] = out.astype(BF)
    o[:, depth + LANES : depth + LANES + experts] = nt(jnp.where(same, 1.0, 0.0).astype(BF), wr[...]).astype(BF)
    o[:, depth + 2 * LANES :] = wo[...]
    subs = bu.shape[0] // share
    wide = subs * LANES
    row, col = iota((wide, wide), 0), iota((wide, wide), 1)
    at = lax.div(lax.rem(row, subs * share), share) * LANES + lax.div(row, subs * share) * share + lax.rem(row, share)
    turn = jnp.where(at == col, 1.0, 0.0).astype(BF)
    for part in range(up.shape[1] // wide):
        moved = nn(up[:, part * wide : (part + 1) * wide], turn).astype(BF)
        for j in range(subs):
            place = (j // 2) * 4 * depth + (j % 2) * depth + part * LANES
            big_o[:, place : place + LANES] = moved[:, j * LANES : (j + 1) * LANES]
    for j in range(subs):
        place = (j // 2) * 4 * depth + (2 + j % 2) * depth
        big_o[:, place : place + depth] = down[j * share : (j + 1) * share, :]


def split3(value):
    high = value.astype(BF).astype(F32)
    rest = value - high
    mid = rest.astype(BF).astype(F32)
    return high, mid, rest - mid


def three(lane, value):
    high, mid, rest = split3(value)
    return jnp.where(lane == 4, -high, jnp.where(lane == 5, -mid, jnp.where(lane == 6, -rest, 0.0)))


def segment_of(lens, row, start, rows):
    place = iota((rows, LANES), 0) + start
    end = lens[row, 0]
    seg = (place >= end).astype(jnp.int32)
    for j in range(1, lens.shape[1]):
        end = end + lens[row, j]
        seg = seg + (place >= end).astype(jnp.int32)
    return seg


def pick(routes, rows, slot):
    return jnp.broadcast_to(routes[rows, slot : slot + 1], (TILE, LANES))


def chosen(wide, expert, half):
    out = jnp.zeros(expert.shape, F32)
    for j in range(wide.shape[1] // LANES):
        out = jnp.where(expert == 2 * j + half, wide[:, j * LANES : (j + 1) * LANES], out)
    return out


def project_kernel(n, length, segs, experts, me, lens, tok, routes, *refs):
    hid_o, qa_o, kx_o, vx_o, pr_o, vec_o, w, vec, sem = refs[n:]
    span, depth = tok.shape
    step = pl.program_id(0)
    row = lax.div(step * span, length)
    begin = lax.rem(step * span, length)

    @pl.when(step == 0)
    def _():
        fetch(me[0], refs[:n], [(0, depth + 2 * LANES, w)], sem)
        arrive(w, sem)
        vec[...] = w[:, depth + LANES :].astype(F32).T
        vec_o[...] = vec[0:32, :]

    lane = iota((TILE, LANES), 1)
    half = lane // 64
    low = lane < 64
    parts = [slice(c * TILE, (c + 1) * TILE) for c in range(span // TILE)]
    for rows in parts:
        unit, _ = normed(tok[rows, :].astype(F32))
        hid_o[rows, :] = (unit * vec[G1 : G1 + 1, :] + vec[B1 : B1 + 1, :]).astype(BF)
    products = [(nn(hid_o[rows, :], w[:, 0:depth]), nn(hid_o[rows, :], w[:, depth:])) for rows in parts]
    for c, rows in enumerate(parts):
        query, small = products[c]
        kv = small[:, :LANES].astype(BF).astype(F32)
        swap = pltpu.roll(kv, 64, 1)
        seg = segment_of(lens, row, begin + c * TILE, TILE)
        same = jnp.where(lane == seg, 1.0, 0.0)
        kx_o[rows, 0:LANES] = jnp.where(low, kv, swap).astype(BF)
        kx_o[rows, LANES:] = jnp.where(lane < segs, same, jnp.where(lane < 8, 1.0, 0.0)).astype(BF)
        vx_o[rows, 0:LANES] = jnp.where(low, swap, kv).astype(BF)
        vx_o[rows, LANES:] = jnp.ones((TILE, LANES), BF)
        logits = jnp.where(lane < experts, small[:, LANES:], FAR)
        raised = jnp.exp(logits - jnp.max(logits, -1, keepdims=True))
        pr_o[rows, :] = raised / jnp.sum(raised, -1, keepdims=True)
        for slot in range(2):
            qa_o[slot, rows, :] = (chosen(query, pick(routes, rows, slot), half) * 0.125).astype(BF)


def attend_kernel(segs, lens, routes, qa, kx, vx, pr, o_o, u_o, qf_o):
    span, depth = u_o.shape
    row, step = pl.program_id(0), pl.program_id(1)
    lane = iota((TILE, LANES), 1)
    half = lane // 64
    low = lane < 64
    for c in range(span // TILE):
        rows = slice(c * TILE, (c + 1) * TILE)
        seg = segment_of(lens, row, step * span + c * TILE, TILE)
        apart = jnp.where((lane < segs) & (lane != seg), FAR, 0.0)
        probs = pr[rows, :]
        seen, gated, experts_of = [], [], []
        for slot in range(2):
            expert = pick(routes, rows, slot)
            scores = nt(jnp.concatenate([qa[slot, rows, :], apart.astype(BF)], 1), kx[...])
            top = jnp.max(scores, -1, keepdims=True)
            raised = jnp.exp(scores - top).astype(BF)
            both = nn(raised, vx[...])
            mass = both[:, LANES:]
            out = both[:, :LANES] / mass
            qf_o[slot, rows, :] = (apart + three(lane, top + jnp.log(mass))).astype(BF)
            gate = jnp.sum(jnp.where(lane == expert, probs, 0.0), -1, keepdims=True)
            seen.append(out)
            gated.append(out * gate)
            experts_of.append(expert)
        o_o[rows, :] = jnp.where(low, seen[0], seen[1])
        for j in range(depth // LANES):
            part = jnp.where(experts_of[0] == 2 * j + half, gated[0], jnp.where(experts_of[1] == 2 * j + half, gated[1], 0.0))
            u_o[rows, j * LANES : (j + 1) * LANES] = part.astype(BF)


def mix_kernel(n, me, tok, u, vec, *refs):
    x1_o, h2_o, w, sem = refs[n:]
    span, depth = tok.shape

    @pl.when(pl.program_id(0) == 0)
    def _():
        fetch(me[0], refs[:n], [(depth + 2 * LANES, depth, w)], sem)
        arrive(w, sem)

    parts = [slice(c * TILE, (c + 1) * TILE) for c in range(span // TILE)]
    products = [nn(u[rows, :], w[...]) for rows in parts]
    for rows, product in zip(parts, products):
        after = tok[rows, :].astype(F32) + product
        x1_o[rows, :] = after
        unit, _ = normed(after)
        h2_o[rows, :] = (unit * vec[G2 : G2 + 1, :] + vec[B2 : B2 + 1, :]).astype(BF)


def ffn_kernel(n, me, h2, dy, vec, *refs):
    pieces = [refs[:n], refs[n : 2 * n]]
    act_o, dz_o, bias_o = refs[2 * n : 2 * n + 3]
    grads = [refs[2 * n + 3 : 3 * n + 3], refs[3 * n + 3 : 4 * n + 3]]
    wu, wd, ht, yt, acts, dzs, out, sem, out_sem = refs[4 * n + 3 :]
    step = pl.program_id(0)
    steps = pl.num_programs(0) - 1
    total, wide = act_o.shape
    depth = h2.shape[1]
    per = depth // wide
    some = wu.shape[2]

    @pl.when(step == 0)
    def _():
        for half in range(2):
            fetch(me[0], pieces[half], ffn_parts(wu, wd, half, depth, True, True), sem.at[half])
        for t in range(0, total, STEP):
            ht[0:depth, t : t + STEP] = h2[t : t + STEP, :].T
            yt[:, t : t + STEP] = dy[t : t + STEP, :].T
        ht[depth:, :] = jnp.ones((16, total), BF)

    for half in range(2):
        @pl.when(step == half * steps // 2)
        def _():
            arrive(wu.at[half], sem.at[half])
            arrive(wd.at[pl.ds(half * some, some), :], sem.at[half])

    one = 0.7978845608028654
    two = one * 0.044715
    cur = lax.rem(step, 2)

    def place(t):
        sub = lax.div(t, per)
        return sub, lax.rem(t, per), lax.rem(sub, 2) * depth, lax.div(sub, 2)

    def grad_up(t, slot):
        sub, part, column, half = place(t)
        up = nn(ht[...], dzs[slot])
        out[half, :, pl.ds(pl.multiple_of(column + part * wide, wide), wide)] = up[0:depth, :].astype(BF)
        bias_o[pl.ds(sub, 1), pl.ds(pl.multiple_of(part * wide, wide), wide)] = up[depth : depth + 1, :]

    def grad_down(t, slot):
        _, part, column, half = place(t)
        rows = pl.ds(pl.multiple_of(part * wide, wide), wide)
        out[half, rows, pl.ds(pl.multiple_of(column + 2 * depth, depth), depth)] = nn(yt[...], acts[slot]).T.astype(BF)

    @pl.when(step < steps)
    def _():
        before = jnp.maximum(step - 1, 0)
        sub, part, column, which = place(step)
        here = pl.ds(pl.multiple_of(step * wide, wide), wide)
        across = pl.ds(pl.multiple_of(column + part * wide, wide), wide)
        bias = vec[pl.ds(BU + sub, 1), pl.ds(pl.multiple_of(part * wide, wide), wide)]
        count = total // TILE
        for c in range(count):
            rows = slice(c * TILE, (c + 1) * TILE)
            z = nn(h2[rows, :], wu[which, :, across]) + bias
            dact = nt(dy[rows, :], wd[here, :])
            if c == 0:
                grad_up(before, 1 - cur)
            if c == count // 2:
                grad_down(before, 1 - cur)
            square = z * z
            tanh = jnp.tanh(z * (one + two * square))
            half = 0.5 * tanh + 0.5
            act = z * half
            slope = half + act * (1.0 - tanh) * (one + 3.0 * two * square)
            act = act.astype(BF)
            dz = (dact * slope).astype(BF)
            act_o[rows, :] = act
            dz_o[rows, :] = dz
            acts[cur, rows, :] = act
            dzs[cur, rows, :] = dz

    @pl.when(step == steps // 2)
    def _():
        scatter(me[0], grads[0], out.at[0], out_sem)

    @pl.when(step == steps)
    def _():
        grad_up(steps - 1, 1 - cur)
        grad_down(steps - 1, 1 - cur)
        scatter(me[0], grads[1], out.at[1], out_sem)
        arrive(out, out_sem)


def turn_kernel(n, again, me, dz, dy, x1, vec, *refs):
    if again:
        before, refs = refs[0], refs[3:]
    dx1_o, low_o, sums_o, wu, f_sem = refs[2 * n :]
    span, depth = dy.shape
    step = pl.program_id(0)

    @pl.when(step == 0)
    def _():
        for half in range(2):
            fetch(me[0], refs[half * n : half * n + n], ffn_parts(wu, None, half, depth, True, False), f_sem)
        sums_o[...] = before[...] if again else jnp.zeros_like(sums_o)
        arrive(wu, f_sem)

    parts = [slice(c * TILE, (c + 1) * TILE) for c in range(span // TILE)]
    products = [nt(dz[rows, 0 : 2 * depth], wu[0]) + nt(dz[rows, 2 * depth :], wu[1]) for rows in parts]
    for rows, dh2 in zip(parts, products):
        unit, inv = normed(x1[rows, :])
        grad = dy[rows, :].astype(F32)
        sums_o[G2 : G2 + 1, :] += jnp.sum(dh2 * unit, 0, keepdims=True)
        sums_o[B2 : B2 + 1, :] += jnp.sum(dh2, 0, keepdims=True)
        sums_o[BD : BD + 1, :] += jnp.sum(grad, 0, keepdims=True)
        scaled = dh2 * vec[G2 : G2 + 1, :]
        one = jnp.mean(scaled, -1, keepdims=True)
        two = jnp.mean(scaled * unit, -1, keepdims=True)
        dx1 = grad + inv * (scaled - one - unit * two)
        dx1_o[rows, :] = dx1
        low_o[rows, :] = dx1.astype(BF)


def gates_kernel(n, me, dx1, routes, pr, o, u, *refs):
    da_o, df_o, ds_o, load_o, go_o, w, go, sem = refs[n:]
    span, depth = dx1.shape
    step = pl.program_id(0)

    @pl.when(step == 0)
    def _():
        fetch(me[0], refs[:n], [(depth + 2 * LANES, depth, w)], sem)
        go[...] = jnp.zeros_like(go)
        load_o[...] = jnp.zeros_like(load_o)
        arrive(w, sem)

    lane = iota((TILE, LANES), 1)
    half = lane // 64
    low = lane < 64
    go[...] += nn(u[...].T, dx1[...])
    parts = [slice(c * TILE, (c + 1) * TILE) for c in range(span // TILE)]
    products = [nt(dx1[rows, :], w[...]) for rows in parts]
    for rows, product in zip(parts, products):
        du = product.astype(BF).astype(F32)
        probs = pr[rows, :]
        heads = o[rows, :]
        swap = pltpu.roll(heads, 64, 1)
        dprobs = jnp.zeros((TILE, LANES), F32)
        loads = jnp.zeros((TILE, LANES), F32)
        for slot in range(2):
            expert = pick(routes, rows, slot)
            own = chosen(du, expert, half)
            here = lane == expert
            gate = jnp.sum(jnp.where(here, probs, 0.0), -1, keepdims=True)
            seen = jnp.where(low, heads, swap) if slot == 0 else jnp.where(low, swap, heads)
            dgate = jnp.sum(own * seen, -1, keepdims=True)
            da = (own * gate).astype(BF)
            da_o[slot, rows, :] = da
            df_o[slot, rows, :] = three(lane, jnp.sum(da.astype(F32) * seen, -1, keepdims=True)).astype(BF)
            dprobs = jnp.where(here, dgate, dprobs)
            loads = jnp.where(here, 1.0, loads)
        load_o[0:1, :] += jnp.sum(loads, 0, keepdims=True)
        inner = jnp.sum(dprobs * probs, -1, keepdims=True)
        ds_o[rows, :] = (probs * (dprobs - inner)).astype(BF)

    @pl.when(step == pl.num_programs(0) - 1)
    def _():
        go_o[...] = go[...].astype(BF)


def attend_back_kernel(routes, qa, qf, kx, vx, da, df, *refs):
    dq_o, kv_o, dk, dv, ds, ps = refs[-6:]
    span, depth = dq_o.shape
    step = pl.program_id(0)
    lane = iota((TILE, LANES), 1)
    half = lane // 64

    for slot in range(2):
        own = slice(slot * span, (slot + 1) * span)
        probs = jnp.exp(nt(jnp.concatenate([qa[slot], qf[slot]], 1), kx[...]))
        ps[own, :] = probs.astype(BF)
        away = nt(jnp.concatenate([da[slot], df[slot]], 1), vx[...])
        ds[own, :] = (probs * away).astype(BF)
    dk_part = nn(jnp.concatenate([qa[0].T, qa[1].T], 1), ds[...])
    dv_part = nn(jnp.concatenate([da[0].T, da[1].T], 1), ps[...])
    found = nn(ds[...], kx[:, 0:LANES]) * 0.125
    for c in range(span // TILE):
        rows = slice(c * TILE, (c + 1) * TILE)
        others = slice(span + c * TILE, span + (c + 1) * TILE)
        one, two = pick(routes, rows, 0), pick(routes, rows, 1)
        for j in range(depth // LANES):
            part = jnp.where(one == 2 * j + half, found[rows, :], jnp.where(two == 2 * j + half, found[others, :], 0.0))
            dq_o[rows, j * LANES : (j + 1) * LANES] = part.astype(BF)

    @pl.when(step == 0)
    def _():
        dk[...] = dk_part
        dv[...] = dv_part

    @pl.when(step > 0)
    def _():
        dk[...] += dk_part
        dv[...] += dv_part

    @pl.when(step == pl.num_programs(0) - 1)
    def _():
        for c in range(kv_o.shape[0] // TILE):
            rows = slice(c * TILE, (c + 1) * TILE)
            both = jnp.concatenate([dk[0:64, rows] + dk[64:, rows], dv[0:64, rows] + dv[64:, rows]], 0)
            kv_o[rows, :] = both.T.astype(BF)


def sum_kernel(n, block, experts, me, hid, dq, kv, ds, sums, bias, loads, go, *refs):
    w, gq, gs, all_sums, out, sem, out_sem = refs[2 * n :]
    span, depth = hid.shape
    step = pl.program_id(0)

    @pl.when(step == 0)
    def _():
        fetch(me[0], refs[:n], [(0, depth + 2 * LANES, w)], sem)
        gq[...] = jnp.zeros_like(gq)
        gs[...] = jnp.zeros_like(gs)

    turned = jnp.concatenate([hid[...].T, jnp.ones((16, span), BF)], 0)
    gq[...] += nn(turned, dq[...])
    gs[...] += nn(turned, jnp.concatenate([kv[...], ds[...]], 1))

    @pl.when(step == pl.num_programs(0) - 1)
    def _():
        arrive(w, sem)
        all_sums[...] = jnp.zeros_like(all_sums)
        all_sums[0:32, :] = sums[...]
        all_sums[BU : BU + 4, :] = bias[0:4, :]
        wq = w[:, 0:depth].astype(F32)
        ws = w[:, depth:].astype(F32)
        wide = iota((depth, LANES), 1)
        ws_own = jnp.where(wide < experts, ws[:, LANES:], 0.0)
        around = jnp.sum(gq[0:depth, :] * wq, -1, keepdims=True)
        around += jnp.sum(gs[0:depth, 0:LANES] * ws[:, 0:LANES] + gs[0:depth, LANES:] * ws_own, -1, keepdims=True)
        shift = jnp.sum(gq[depth : depth + 1, :] * wq, -1, keepdims=True)
        shift += jnp.sum(
            gs[depth : depth + 1, 0:LANES] * ws[:, 0:LANES] + gs[depth : depth + 1, LANES:] * ws_own, -1, keepdims=True
        )
        gain = ws[:, LANES + G1 : LANES + G1 + 1]
        lift = ws[:, LANES + B1 : LANES + B1 + 1]
        stretch = (around - lift * shift) / gain
        place = lax.rem(iota((depth, LANES), 0), block)
        load = jnp.sum(jnp.where(wide == place, loads[0:1, :], 0.0), -1, keepdims=True)
        columns = jnp.where(wide < experts, gs[0:depth, LANES:], all_sums[...].T)
        columns = jnp.where(wide == G1, stretch, columns)
        columns = jnp.where(wide == B1, shift, columns)
        columns = jnp.where(wide == LOAD, load, columns)
        out[:, 0:depth] = gq[0:depth, :].astype(BF)
        out[:, depth : 2 * depth] = go[...]
        out[:, 2 * depth : 2 * depth + LANES] = gs[0:depth, 0:LANES].astype(BF)
        out[:, 2 * depth + LANES :] = columns.astype(BF)
        scatter(me[0], refs[n : 2 * n], out, out_sem)
        arrive(out, out_sem)


def result_kernel(n, me, act, x1, vec, *refs):
    res_o, wd, sem = refs[-3:]
    depth = x1.shape[1]

    @pl.when(pl.program_id(0) == 0)
    def _():
        for half in range(2):
            fetch(me[0], refs[half * n : half * n + n], ffn_parts(None, wd, half, depth, False, True), sem)
        arrive(wd, sem)

    res_o[...] = (x1[...] + vec[BD : BD + 1, :] + nn(act[...], wd[...])).astype(BF)


def close_kernel(n, me, dx1, dq, kv, ds, tok, vec, *refs):
    grad_o, w, sem = refs[n:]
    span, depth = tok.shape

    @pl.when(pl.program_id(0) == 0)
    def _():
        fetch(me[0], refs[:n], [(0, depth + 2 * LANES, w)], sem)
        arrive(w, sem)

    parts = [slice(c * TILE, (c + 1) * TILE) for c in range(span // TILE)]
    products = [
        nt(dq[rows, :], w[:, 0:depth]) + nt(jnp.concatenate([kv[rows, :], ds[rows, :]], 1), w[:, depth:]) for rows in parts
    ]
    for rows, dh in zip(parts, products):
        unit, inv = normed(tok[rows, :].astype(F32))
        scaled = dh * vec[G1 : G1 + 1, :]
        one = jnp.mean(scaled, -1, keepdims=True)
        two = jnp.mean(scaled * unit, -1, keepdims=True)
        grad_o[rows, :] = (dx1[rows, :] + inv * (scaled - one - unit * two)).astype(BF)


def finish_kernel(share_of, keep, got, gq, gk, gv, go, gr, g1, b1, g2, b2, bd, bu, load):
    share, depth = gq.shape
    head, experts = gk.shape[1], gr.shape[0]
    total = keep[...].astype(F32) + got[...].astype(F32)
    gq[...] = total[:, 0:depth]
    go[...] = total[:, depth : 2 * depth]
    gk[...] = total[:, 2 * depth : 2 * depth + head]
    gv[...] = total[:, 2 * depth + head : 2 * depth + 2 * head]
    turned = jnp.concatenate([total[:, 2 * depth + LANES :], jnp.zeros((LANES - share, LANES), F32)], 0).T
    gr[...] = turned[0:experts, 0:share]
    for at, out in zip((G1, B1, G2, B2, BD), (g1, b1, g2, b2, bd)):
        out[...] = turned[at : at + 1, 0:share].reshape(share)
    lines = [turned[BU + j : BU + j + 1, 0:share] for j in range(bu.shape[0] // share)]
    bu[...] = jnp.concatenate(lines, 1).reshape(bu.shape[0])
    load[...] = (turned[LOAD : LOAD + 1, 0:experts] * share_of).reshape(experts)


def xor_pairs(count, mask):
    return [(i, i ^ mask) for i in range(count)]


def hops(dp, fsdp):
    inner = fsdp.bit_length() - 1
    along = [1 << bit for bit in range(inner - 1, 1, -1)]
    across = [2] if inner > 1 else []
    rows = [1 << (inner + bit) for bit in range(dp.bit_length() - 1)]
    core = [1] if inner > 0 else []
    return along + across + rows + core, along + rows + across + core


def after(value, *others):
    return lax.optimization_barrier((value, *others))[0]


def move(value, mask, count):
    return lax.ppermute(value, AXES, xor_pairs(count, mask))


def spread(held, have, mask, me, count):
    axis = len([other for other in have if other > mask])
    own = jnp.expand_dims(held, axis)
    got = jnp.expand_dims(move(held, mask, count), axis)
    high = jnp.bitwise_and(me, mask) != 0
    return jnp.where(high, jnp.concatenate([got, own], axis), jnp.concatenate([own, got], axis))


def parted(value, have, mask, me):
    axis = len([other for other in have if other > mask])
    bit = (jnp.bitwise_and(me, mask) != 0).astype(jnp.int32)
    return (
        lax.dynamic_index_in_dim(value, bit, axis, keepdims=False),
        lax.dynamic_index_in_dim(value, 1 - bit, axis, keepdims=False),
    )


def joined(keep, got, dtype=BF):
    return (keep.astype(F32) + got.astype(F32)).astype(dtype)


def shrink(value, have, mask, me, count, dtype=BF):
    keep, send = parted(value, have, mask, me)
    return joined(keep, move(send, mask, count), dtype)


def cost(micros):
    return pl.CostEstimate(flops=int(micros * 1.0e9), bytes_accessed=1024, transcendentals=0)


def on_device(
    sizes, tokens, routes, lengths, ln1_gain, ln1_bias, w_query, w_key, w_value, w_out, w_router,
    ln2_gain, ln2_bias, w_up, b_up, w_down, b_down, cotangent
):
    dp, fsdp = sizes
    count = dp * fsdp
    total, depth = tokens.shape
    rows = lengths.shape[0]
    length = total // rows
    experts, head = w_router.shape[1], w_key.shape[1]
    segs = lengths.shape[1]
    share = w_query.shape[0]
    inner = w_up.shape[1]
    subs = inner // depth
    fast = share % 16 == 0 and fsdp >= 8 and dp >= 2
    first_width = 2 * depth + 2 * LANES
    me = lax.axis_index(AXES).astype(jnp.int32)
    core = (jnp.bitwise_and(me, 1) if fast else jnp.int32(0)).reshape(1)
    packed = (w_query, w_out, w_key, w_value, w_router.T, ln1_gain, ln1_bias, ln2_gain, ln2_bias, b_down, b_up, w_up, w_down)
    small, large = pl.pallas_call(
        pack_kernel,
        out_shape=[
            pltpu.VMEM((share, first_width), BF), pltpu.VMEM((share, 2 * inner), BF),
        ],
        name="pack",
    )(*packed)
    if fast:
        orders = hops(dp, fsdp)
        steps = len(orders[0])
        early = len([m for m in orders[0][:-1] if orders[0].index(m) == orders[1].index(m)])
        blocks, block, n = count // 2, share, 2
        dims = (2,) * (steps - 1)

        def grow(held, order, at):
            return spread(held, order[:at], order[at], me, count)

        def flat(value):
            return value.reshape(blocks, block, value.shape[-1])

        held = small
        for at in range(early):
            held = grow(held, orders[0], at)
            if at == 0:
                big = after(large, held)
        big = grow(big, orders[0], 0)
        parts = [held[..., : first_width // 2], held[..., first_width // 2 :]]
        for at in range(early, steps - 1):
            parts = [grow(part, order, at) for part, order in zip(parts, orders)]
            if at == early:
                for other in range(1, early):
                    big = grow(after(big, *parts), orders[0], other)
        held = flat(jnp.concatenate(parts, -1))
        w_pieces = [held, move(held, orders[0][-1], count)]
        big = [after(half, w_pieces[1]) for half in (big[..., : 4 * depth], big[..., 4 * depth :])]
        pending = list(range(early, steps - 1))
    else:
        blocks, block, n = 1, depth, 1
        w_pieces = [lax.all_gather(small, AXES, axis=0, tiled=True)[None]]
        large = lax.all_gather(large, AXES, axis=0, tiled=True)[None]
        f_pieces = [[large[..., : 4 * depth]], [large[..., 4 * depth :]]]

    smem = pl.BlockSpec(memory_space=pltpu.SMEM)
    hbm = pl.BlockSpec(memory_space=pl.ANY)
    vmem = pl.BlockSpec(memory_space=pltpu.VMEM)
    dma = pltpu.SemaphoreType.DMA

    def whole(dims):
        return pl.BlockSpec(dims, lambda *_: (0,) * len(dims))

    def shape(dims, dtype):
        return jax.ShapeDtypeStruct(dims, dtype)

    def keep_far(value):
        return pltpu.with_memory_space_constraint(value, pltpu.HBM)

    def far(dims, dtype):
        return pltpu.HBM(dims, dtype)

    def call(kernel, name, micros, grid, ins, in_specs, outs, out_specs, scratch):
        return pl.pallas_call(
            kernel, grid=grid, in_specs=in_specs, out_specs=out_specs, out_shape=outs, scratch_shapes=scratch,
            compiler_params=pltpu.CompilerParams(vmem_limit_bytes=ROOM[name] << 20), cost_estimate=cost(micros), name=name,
        )(*ins)

    span = min(STEP, length)
    tiles = total // span
    per_row = length // span

    def tile(wide):
        return pl.BlockSpec((span, wide), lambda t: (t, 0))

    def pair(wide):
        return pl.BlockSpec((2, span, wide), lambda t: (0, t, 0))

    def row_tile(wide):
        return pl.BlockSpec((span, wide), lambda r, t: (r * per_row + t, 0))

    def row_pair(wide):
        return pl.BlockSpec((2, span, wide), lambda r, t: (0, r * per_row + t, 0))

    def by_row(wide):
        return pl.BlockSpec((length, wide), lambda r, t: (r, 0))

    hid, qa, kx, vx, pr, vec = call(
        functools.partial(project_kernel, n, length, segs, experts), "project", 9.0, (tiles,),
        (core, lengths, keep_far(tokens), routes, *w_pieces),
        [smem, smem, tile(depth), tile(2)] + [hbm] * n,
        [
            far((total, depth), BF), shape((2, total, LANES), BF), far((total, 2 * LANES), BF),
            far((total, 2 * LANES), BF), shape((total, LANES), F32), shape((32, depth), F32),
        ],
        [tile(depth), pair(LANES), tile(2 * LANES), tile(2 * LANES), tile(LANES), whole((32, depth))],
        [pltpu.VMEM((depth, depth + 2 * LANES), BF), pltpu.VMEM((LANES, depth), F32), dma],
    )
    if fast:
        big = [grow(half, order, pending[0]) for half, order in zip(big, orders)]
        qa = after(qa, *big)
        big = [after(half, kx) for half in big]
    o, u, qf = call(
        functools.partial(attend_kernel, segs), "attend", 13.0, (rows, per_row),
        (lengths, routes, qa, kx, vx, pr),
        [smem, row_tile(2), row_pair(LANES), by_row(2 * LANES), by_row(2 * LANES), row_tile(LANES)],
        [shape((total, LANES), F32), shape((total, depth), BF), far((2, total, LANES), BF)],
        [row_tile(LANES), row_tile(depth), row_pair(LANES)],
        [],
    )
    if fast:
        for at in pending[1:]:
            big = [grow(half, order, at) for half, order in zip(big, orders)]
        big = [flat(half) for half in big]
        u = after(u, *big)
        big = [after(half, o) for half in big]
        f_pieces = [[half, move(half, orders[0][-1], count)] for half in big]
    x1, h2 = call(
        functools.partial(mix_kernel, n), "mix", 5.0, (tiles,),
        (core, tokens, u, vec, *w_pieces),
        [smem, tile(depth), tile(depth), whole((32, depth))] + [hbm] * n,
        [far((total, depth), F32), shape((total, depth), BF)],
        [tile(depth), tile(depth)],
        [pltpu.VMEM((depth, depth), BF), dma],
    )
    flat_f = [piece for half in f_pieces for piece in half]

    wide = 256

    column = pl.BlockSpec((total, wide), lambda s: (0, jnp.minimum(s, inner // wide - 1)))
    act, dz, bias, *f_grads = call(
        functools.partial(ffn_kernel, n), "feed", 25.0, (inner // wide + 1,),
        (core, h2, cotangent, vec, *flat_f),
        [smem, vmem, vmem, whole((32, depth))] + [hbm] * 2 * n,
        [far((total, inner), BF), far((total, inner), BF), shape((8, depth), F32)]
        + [far((blocks, block, 4 * depth), BF)] * 2 * n,
        [column, column, whole((8, depth))] + [hbm] * 2 * n,
        [
            pltpu.VMEM((2, depth, inner // 2), BF), pltpu.VMEM((inner, depth), BF), pltpu.VMEM((depth + 16, total), BF),
            pltpu.VMEM((depth, total), BF), pltpu.VMEM((2, total, wide), BF), pltpu.VMEM((2, total, wide), BF),
            pltpu.VMEM((2, depth, inner), BF), pltpu.SemaphoreType.DMA((2,)), dma,
        ],
    )
    f_grads = [f_grads[:n], f_grads[n:]]
    def turn(begin, again):
        def part(wide):
            return pl.BlockSpec((span, wide), lambda t: (t + begin, 0))

        return pl.pallas_call(
            functools.partial(turn_kernel, n, len(again) > 0), grid=(tiles // 2,),
            in_specs=[smem, part(inner), part(depth), part(depth), whole((32, depth))]
            + ([whole((32, depth)), hbm, hbm] if again else []) + [hbm] * 2 * n,
            out_specs=[part(depth), part(depth), whole((32, depth))],
            out_shape=[shape((total, depth), F32), shape((total, depth), BF), shape((32, depth), F32)],
            scratch_shapes=[pltpu.VMEM((2, depth, inner // 2), BF), dma],
            input_output_aliases={6: 0, 7: 1} if again else {},
            compiler_params=pltpu.CompilerParams(vmem_limit_bytes=ROOM["turn"] << 20), cost_estimate=cost(6.0), name="turn",
        )(core, keep_far(dz), keep_far(cotangent), keep_far(x1), vec, *again, *flat_f)

    dx1, low, sums = turn(0, ())
    if fast:
        back_orders = [list(reversed(order[:-1])) for order in orders]
        late = back_orders[0]

        def fall(value, order, at, dtype=BF):
            return shrink(value, order[at:], order[at], me, count, dtype)

        acc = [joined(half[0], move(half[1], orders[0][-1], count)).reshape(*dims, block, 4 * depth) for half in f_grads]
        sums = after(sums, *acc)
        acc = [after(a, dx1) for a in acc]
        acc = [fall(a, order, 0) for a, order in zip(acc, back_orders)]
    dx1, low, sums = turn(tiles // 2, (sums, dx1, low))
    da, df, ds, loads, go = call(
        functools.partial(gates_kernel, n), "gates", 9.0, (tiles,),
        (core, low, routes, pr, o, u, *w_pieces),
        [smem, tile(depth), tile(2), tile(LANES), tile(LANES), tile(depth)] + [hbm] * n,
        [
            shape((2, total, LANES), BF), shape((2, total, LANES), BF), shape((total, LANES), BF), shape((8, LANES), F32),
            shape((depth, depth), BF),
        ],
        [pair(LANES), pair(LANES), tile(LANES), whole((8, LANES)), whole((depth, depth))],
        [pltpu.VMEM((depth, depth), BF), pltpu.VMEM((depth, depth), F32), dma],
    )
    if fast:
        da = after(da, *acc)
        acc = [after(a, ds) for a in acc]
        acc = [fall(a, order, 1) for a, order in zip(acc, back_orders)]

    def back(row, again):
        def part(wide):
            return pl.BlockSpec((span, wide), lambda t: (row * per_row + t, 0))

        def both(wide):
            return pl.BlockSpec((2, span, wide), lambda t: (0, row * per_row + t, 0))

        def full(wide):
            return pl.BlockSpec((length, wide), lambda t: (row, 0))

        return pl.pallas_call(
            attend_back_kernel, grid=(per_row,),
            in_specs=[part(2), both(LANES), both(LANES), full(2 * LANES), full(2 * LANES), both(LANES), both(LANES)]
            + [hbm] * len(again),
            out_specs=[part(depth), full(LANES)],
            out_shape=[shape((total, depth), BF), shape((total, LANES), BF)],
            scratch_shapes=[
                pltpu.VMEM((LANES, length), F32), pltpu.VMEM((LANES, length), F32), pltpu.VMEM((2 * span, length), BF),
                pltpu.VMEM((2 * span, length), BF),
            ],
            input_output_aliases={7: 0, 8: 1} if again else {},
            compiler_params=pltpu.CompilerParams(vmem_limit_bytes=ROOM["attend_back"] << 20), cost_estimate=cost(8.0),
            name="attend_back",
        )(routes, qa, qf, kx, vx, da, df, *again)

    dq, kv = back(0, ())
    for row in range(1, rows):
        if fast and row == 1:
            dq = after(dq, *acc)
            acc = jnp.concatenate([after(a, kv) for a in acc], -1)
            acc = fall(acc, late, 2, F32 if len(late) == 3 else BF)
        dq, kv = back(row, (dq, kv))
    if fast:
        kv = after(kv, acc)
        for at in range(3, len(late)):
            acc = fall(after(acc, dq), late, at, F32 if at == len(late) - 1 else BF)
    w_grads = call(
        functools.partial(sum_kernel, n, block, experts), "sums", 6.0, (tiles,),
        (core, hid, dq, kv, ds, sums, bias, loads, go, *w_pieces),
        [
            smem, tile(depth), tile(depth), tile(LANES), tile(LANES), whole((32, depth)), whole((8, depth)),
            whole((8, LANES)), whole((depth, depth)),
        ]
        + [hbm] * n,
        [shape((blocks, block, first_width), BF)] * n,
        [hbm] * n,
        [
            pltpu.VMEM((depth, depth + 2 * LANES), BF), pltpu.VMEM((depth + 16, depth), F32),
            pltpu.VMEM((depth + 16, 2 * LANES), F32), pltpu.VMEM((LANES, depth), F32),
            pltpu.VMEM((depth, first_width), BF), dma, dma,
        ],
    )
    closing = dx1
    if fast:
        tail = joined(w_grads[0], move(w_grads[1], orders[0][-1], count)).reshape(*dims, block, first_width)
        closing = after(dx1, tail, acc)
        tails = [tail[..., : first_width // 2], tail[..., first_width // 2 :]]
        tails = [fall(part, order, 0) for part, order in zip(tails, back_orders)]
    grad_tokens = call(
        functools.partial(close_kernel, n), "close", 6.0, (tiles,),
        (core, closing, dq, kv, ds, tokens, vec, *w_pieces),
        [smem, tile(depth), tile(depth), tile(LANES), tile(LANES), tile(depth), whole((32, depth))] + [hbm] * n,
        [shape((total, depth), BF)],
        [tile(depth)],
        [pltpu.VMEM((depth, depth + 2 * LANES), BF), dma],
    )[0]
    closing = x1
    if fast:
        closing = after(x1, *tails)
        tails = [fall(after(part, grad_tokens), order, 1) for part, order in zip(tails, back_orders)]
    def results(begin, again, x1):
        def part(wide):
            return pl.BlockSpec((span, wide), lambda t: (t + begin, 0))

        return pl.pallas_call(
            functools.partial(result_kernel, n), grid=(tiles // 2,),
            in_specs=[smem, part(inner), part(depth), whole((32, depth))] + [hbm] * 2 * n + [hbm] * len(again),
            out_specs=[part(depth)],
            out_shape=[shape((total, depth), BF)],
            scratch_shapes=[pltpu.VMEM((inner, depth), BF), dma],
            input_output_aliases={4 + 2 * n: 0} if again else {},
            compiler_params=pltpu.CompilerParams(vmem_limit_bytes=ROOM["result"] << 20), cost_estimate=cost(3.5), name="result",
        )(core, act, x1, vec, *flat_f, *again)

    result = results(0, (), closing)
    if fast:
        tail = after(jnp.concatenate(tails, -1), *result)
        tail = fall(tail, late, 2, F32 if len(late) == 3 else BF)
    result = results(tiles // 2, result, closing)[0]

    def unpacked(halves):
        up = jnp.concatenate([half[:, : 2 * depth] for half in halves], 1)
        up = up.reshape(share, subs, count, share).transpose(0, 2, 1, 3).reshape(share, inner)
        down = jnp.concatenate([half[:, 2 * depth :] for half in halves], 1)
        return up, down.reshape(share, subs, depth).transpose(1, 0, 2).reshape(subs * share, depth)

    if fast:
        tail = after(tail, result)
        acc = after(acc, result)
        grad_up, grad_down = unpacked([acc[:, : 4 * depth], acc[:, 4 * depth :]])
        for at in range(3, len(late) - 1):
            tail = fall(tail, late, at)
        keep, send = parted(tail, late[-1:], late[-1], me)
        own = functools.partial(jax.ShapeDtypeStruct, dtype=F32)
        grad_query, grad_key, grad_value, grad_out, grad_router, *lines = pl.pallas_call(
            functools.partial(finish_kernel, 1.0 / (total * count)),
            out_shape=[own((share, depth)), own((share, head)), own((share, head)), own((share, depth)), own((experts, share))]
            + [own((share,))] * 5 + [own((subs * share,)), own((experts,))],
            name="finish",
        )(keep, move(send, late[-1], count))
        grad_router = grad_router.T
        grad_g1, grad_b1, grad_g2, grad_b2, grad_bd, grad_bu, load = lines
    else:
        def scattered(value):
            return lax.psum_scatter(value[0].astype(F32), AXES, scatter_dimension=0, tiled=True)

        grad_up, grad_down = unpacked([scattered(half[0]) for half in f_grads])
        own_w = scattered(w_grads[0])
        load = lax.psum(w_grads[0][0][:experts, 2 * depth + LANES + LOAD].astype(F32), AXES) / (total * count)
        extra = own_w[:, 2 * depth + LANES :]
        grad_query, grad_out = own_w[:, 0:depth], own_w[:, depth : 2 * depth]
        grad_key, grad_value = own_w[:, 2 * depth : 2 * depth + head], own_w[:, 2 * depth + head : 2 * depth + 2 * head]
        grad_router = extra[:, 0:experts]
        grad_g1, grad_b1, grad_g2, grad_b2, grad_bd = [extra[:, at] for at in (G1, B1, G2, B2, BD)]
        grad_bu = extra[:, BU : BU + subs].T.reshape(subs * share)
    return (
        result, grad_tokens, grad_g1, grad_b1, grad_query, grad_key, grad_value, grad_out, grad_router, grad_g2, grad_b2,
        grad_up, grad_bu, grad_down, grad_bd, load,
    )


def solution(mesh):
    over = P(AXES)
    flat = P(AXES, None)
    sizes = (mesh.shape["dp"], mesh.shape["fsdp"])
    return jax.shard_map(
        functools.partial(on_device, sizes),
        mesh=mesh,
        in_specs=(
            flat, flat, flat, over, over, flat, flat, flat, flat, flat, over, over, flat, over, flat, over, flat,
        ),
        out_specs=(
            flat, flat, over, over, flat, flat, flat, flat, flat, over, over, flat, over, flat, over, P(),
        ),
        check_vma=False,
    )
```

```python
import functools

import jax
import jax.numpy as jnp
from jax import lax
from jax.experimental import pallas as pl
from jax.experimental.pallas import tpu as pltpu
from jax.sharding import PartitionSpec as P

AXES = ("dp", "fsdp")
F32 = jnp.float32
BF = jnp.bfloat16
FAR = -1e30
LANES = 128
G1, B1, G2, B2, BD, BU, LOAD = 8, 9, 10, 11, 12, 13, 17
TILE = 256
STEP = 512
ROOM = {
    "project": 12, "attend": 14, "mix": 10, "feed": 25, "turn": 18, "gates": 12, "attend_back": 28, "sums": 14, "close": 14,
    "result": 18,
}


def nn(left, right):
    return jnp.dot(left, right, preferred_element_type=F32)


def nt(left, right):
    return lax.dot_general(left, right, (((1,), (1,)), ((), ())), preferred_element_type=F32)


def iota(shape, dim):
    return lax.broadcasted_iota(jnp.int32, shape, dim)


def normed(value):
    center = value - jnp.mean(value, -1, keepdims=True)
    inv = lax.rsqrt(jnp.mean(center * center, -1, keepdims=True) + 1e-05)
    return center * inv, inv


def fetch(core, pieces, parts, sem):
    for other, piece in enumerate(pieces):
        own = jnp.bitwise_xor(core, other)
        for start, wide, dst in parts:
            blocks, block, _ = piece.shape
            view = dst.reshape(blocks, len(pieces), block, wide)
            pltpu.make_async_copy(piece.at[:, :, start : start + wide], view.at[:, own], sem).start()


def arrive(dst, sem):
    pltpu.make_async_copy(dst, dst, sem).wait()


def scatter(core, pieces, src, sem):
    for other, piece in enumerate(pieces):
        own = jnp.bitwise_xor(core, other)
        blocks, block, wide = piece.shape
        view = src.reshape(blocks, len(pieces), block, wide)
        pltpu.make_async_copy(view.at[:, own], piece, sem).start()


def ffn_parts(wu, wd, half, depth, up, down):
    parts = []
    if up:
        parts.append((0, 2 * depth, wu.at[half]))
    if down:
        parts += [((2 + j) * depth, depth, wd.at[pl.ds((2 * half + j) * depth, depth), :]) for j in range(2)]
    return parts


def pack_kernel(wq, wo, wk, wv, wr, g1, b1, g2, b2, bd, bu, up, down, o, big_o):
    share, depth = wq.shape
    head, experts = wk.shape[1], wr.shape[0]
    same = iota((share, share), 0) == iota((share, share), 1)
    lane = iota((share, LANES), 1)

    def column(v):
        return jnp.sum(jnp.where(same, jnp.broadcast_to(v.astype(F32), (share, share)), 0.0), 1, keepdims=True)

    out = jnp.zeros((share, LANES), F32)
    for at, v in zip((G1, B1, G2, B2, BD), (g1, b1, g2, b2, bd)):
        out = jnp.where(lane == at, column(v[...].reshape(1, share)), out)
    flat = bu[...].reshape(1, bu.shape[0])
    for j in range(bu.shape[0] // share):
        out = jnp.where(lane == BU + j, column(flat[:, j * share : (j + 1) * share]), out)
    o[:, 0:depth] = wq[...]
    o[:, depth : depth + head] = wk[...]
    o[:, depth + head : depth + LANES] = wv[...]
    o[:, depth + LANES : depth + 2 * LANES] = out.astype(BF)
    o[:, depth + LANES : depth + LANES + experts] = nt(jnp.where(same, 1.0, 0.0).astype(BF), wr[...]).astype(BF)
    o[:, depth + 2 * LANES :] = wo[...]
    subs = bu.shape[0] // share
    wide = subs * LANES
    row, col = iota((wide, wide), 0), iota((wide, wide), 1)
    at = lax.div(lax.rem(row, subs * share), share) * LANES + lax.div(row, subs * share) * share + lax.rem(row, share)
    turn = jnp.where(at == col, 1.0, 0.0).astype(BF)
    for part in range(up.shape[1] // wide):
        moved = nn(up[:, part * wide : (part + 1) * wide], turn).astype(BF)
        for j in range(subs):
            place = (j // 2) * 4 * depth + (j % 2) * depth + part * LANES
            big_o[:, place : place + LANES] = moved[:, j * LANES : (j + 1) * LANES]
    for j in range(subs):
        place = (j // 2) * 4 * depth + (2 + j % 2) * depth
        big_o[:, place : place + depth] = down[j * share : (j + 1) * share, :]


def split3(value):
    high = value.astype(BF).astype(F32)
    rest = value - high
    mid = rest.astype(BF).astype(F32)
    return high, mid, rest - mid


def three(lane, value):
    high, mid, rest = split3(value)
    return jnp.where(lane == 4, -high, jnp.where(lane == 5, -mid, jnp.where(lane == 6, -rest, 0.0)))


def segment_of(lens, row, start, rows):
    place = iota((rows, LANES), 0) + start
    end = lens[row, 0]
    seg = (place >= end).astype(jnp.int32)
    for j in range(1, lens.shape[1]):
        end = end + lens[row, j]
        seg = seg + (place >= end).astype(jnp.int32)
    return seg


def pick(routes, rows, slot):
    return jnp.broadcast_to(routes[rows, slot : slot + 1], (TILE, LANES))


def chosen(wide, expert, half):
    out = jnp.zeros(expert.shape, F32)
    for j in range(wide.shape[1] // LANES):
        out = jnp.where(expert == 2 * j + half, wide[:, j * LANES : (j + 1) * LANES], out)
    return out


def project_kernel(n, length, segs, experts, me, lens, tok, routes, *refs):
    hid_o, qa_o, kx_o, vx_o, pr_o, vec_o, w, vec, sem = refs[n:]
    span, depth = tok.shape
    step = pl.program_id(0)
    row = lax.div(step * span, length)
    begin = lax.rem(step * span, length)

    @pl.when(step == 0)
    def _():
        fetch(me[0], refs[:n], [(0, depth + 2 * LANES, w)], sem)
        arrive(w, sem)
        vec[...] = w[:, depth + LANES :].astype(F32).T
        vec_o[...] = vec[0:32, :]

    lane = iota((TILE, LANES), 1)
    half = lane // 64
    low = lane < 64
    parts = [slice(c * TILE, (c + 1) * TILE) for c in range(span // TILE)]
    for rows in parts:
        unit, _ = normed(tok[rows, :].astype(F32))
        hid_o[rows, :] = (unit * vec[G1 : G1 + 1, :] + vec[B1 : B1 + 1, :]).astype(BF)
    products = [(nn(hid_o[rows, :], w[:, 0:depth]), nn(hid_o[rows, :], w[:, depth:])) for rows in parts]
    for c, rows in enumerate(parts):
        query, small = products[c]
        kv = small[:, :LANES].astype(BF).astype(F32)
        swap = pltpu.roll(kv, 64, 1)
        seg = segment_of(lens, row, begin + c * TILE, TILE)
        same = jnp.where(lane == seg, 1.0, 0.0)
        kx_o[rows, 0:LANES] = jnp.where(low, kv, swap).astype(BF)
        kx_o[rows, LANES:] = jnp.where(lane < segs, same, jnp.where(lane < 8, 1.0, 0.0)).astype(BF)
        vx_o[rows, 0:LANES] = jnp.where(low, swap, kv).astype(BF)
        vx_o[rows, LANES:] = jnp.ones((TILE, LANES), BF)
        logits = jnp.where(lane < experts, small[:, LANES:], FAR)
        raised = jnp.exp(logits - jnp.max(logits, -1, keepdims=True))
        pr_o[rows, :] = raised / jnp.sum(raised, -1, keepdims=True)
        for slot in range(2):
            qa_o[slot, rows, :] = (chosen(query, pick(routes, rows, slot), half) * 0.125).astype(BF)


def attend_kernel(segs, lens, routes, qa, kx, vx, pr, o_o, u_o, qf_o):
    span, depth = u_o.shape
    row, step = pl.program_id(0), pl.program_id(1)
    lane = iota((TILE, LANES), 1)
    half = lane // 64
    low = lane < 64
    for c in range(span // TILE):
        rows = slice(c * TILE, (c + 1) * TILE)
        seg = segment_of(lens, row, step * span + c * TILE, TILE)
        apart = jnp.where((lane < segs) & (lane != seg), FAR, 0.0)
        probs = pr[rows, :]
        seen, gated, experts_of = [], [], []
        for slot in range(2):
            expert = pick(routes, rows, slot)
            scores = nt(jnp.concatenate([qa[slot, rows, :], apart.astype(BF)], 1), kx[...])
            top = jnp.max(scores, -1, keepdims=True)
            raised = jnp.exp(scores - top).astype(BF)
            both = nn(raised, vx[...])
            mass = both[:, LANES:]
            out = both[:, :LANES] / mass
            qf_o[slot, rows, :] = (apart + three(lane, top + jnp.log(mass))).astype(BF)
            gate = jnp.sum(jnp.where(lane == expert, probs, 0.0), -1, keepdims=True)
            seen.append(out)
            gated.append(out * gate)
            experts_of.append(expert)
        o_o[rows, :] = jnp.where(low, seen[0], seen[1])
        for j in range(depth // LANES):
            part = jnp.where(experts_of[0] == 2 * j + half, gated[0], jnp.where(experts_of[1] == 2 * j + half, gated[1], 0.0))
            u_o[rows, j * LANES : (j + 1) * LANES] = part.astype(BF)


def mix_kernel(n, me, tok, u, vec, *refs):
    x1_o, h2_o, w, sem = refs[n:]
    span, depth = tok.shape

    @pl.when(pl.program_id(0) == 0)
    def _():
        fetch(me[0], refs[:n], [(depth + 2 * LANES, depth, w)], sem)
        arrive(w, sem)

    parts = [slice(c * TILE, (c + 1) * TILE) for c in range(span // TILE)]
    products = [nn(u[rows, :], w[...]) for rows in parts]
    for rows, product in zip(parts, products):
        after = tok[rows, :].astype(F32) + product
        x1_o[rows, :] = after
        unit, _ = normed(after)
        h2_o[rows, :] = (unit * vec[G2 : G2 + 1, :] + vec[B2 : B2 + 1, :]).astype(BF)


def ffn_kernel(n, me, h2, dy, vec, *refs):
    pieces = [refs[:n], refs[n : 2 * n]]
    act_o, dz_o, bias_o = refs[2 * n : 2 * n + 3]
    grads = [refs[2 * n + 3 : 3 * n + 3], refs[3 * n + 3 : 4 * n + 3]]
    wu, wd, ht, yt, acts, dzs, out, sem, out_sem = refs[4 * n + 3 :]
    step = pl.program_id(0)
    steps = pl.num_programs(0) - 1
    total, wide = act_o.shape
    depth = h2.shape[1]
    per = depth // wide
    some = wu.shape[2]

    @pl.when(step == 0)
    def _():
        for half in range(2):
            fetch(me[0], pieces[half], ffn_parts(wu, wd, half, depth, True, True), sem.at[half])
        for t in range(0, total, STEP):
            ht[0:depth, t : t + STEP] = h2[t : t + STEP, :].T
            yt[:, t : t + STEP] = dy[t : t + STEP, :].T
        ht[depth:, :] = jnp.ones((16, total), BF)

    for half in range(2):
        @pl.when(step == half * steps // 2)
        def _():
            arrive(wu.at[half], sem.at[half])
            arrive(wd.at[pl.ds(half * some, some), :], sem.at[half])

    one = 0.7978845608028654
    two = one * 0.044715
    cur = lax.rem(step, 2)

    def place(t):
        sub = lax.div(t, per)
        return sub, lax.rem(t, per), lax.rem(sub, 2) * depth, lax.div(sub, 2)

    def grad_up(t, slot):
        sub, part, column, half = place(t)
        up = nn(ht[...], dzs[slot])
        out[half, :, pl.ds(pl.multiple_of(column + part * wide, wide), wide)] = up[0:depth, :].astype(BF)
        bias_o[pl.ds(sub, 1), pl.ds(pl.multiple_of(part * wide, wide), wide)] = up[depth : depth + 1, :]

    def grad_down(t, slot):
        _, part, column, half = place(t)
        rows = pl.ds(pl.multiple_of(part * wide, wide), wide)
        out[half, rows, pl.ds(pl.multiple_of(column + 2 * depth, depth), depth)] = nn(yt[...], acts[slot]).T.astype(BF)

    @pl.when(step < steps)
    def _():
        before = jnp.maximum(step - 1, 0)
        sub, part, column, which = place(step)
        here = pl.ds(pl.multiple_of(step * wide, wide), wide)
        across = pl.ds(pl.multiple_of(column + part * wide, wide), wide)
        bias = vec[pl.ds(BU + sub, 1), pl.ds(pl.multiple_of(part * wide, wide), wide)]
        count = total // TILE
        for c in range(count):
            rows = slice(c * TILE, (c + 1) * TILE)
            z = nn(h2[rows, :], wu[which, :, across]) + bias
            dact = nt(dy[rows, :], wd[here, :])
            if c == 0:
                grad_up(before, 1 - cur)
            if c == count // 2:
                grad_down(before, 1 - cur)
            square = z * z
            tanh = jnp.tanh(z * (one + two * square))
            half = 0.5 * tanh + 0.5
            act = z * half
            slope = half + act * (1.0 - tanh) * (one + 3.0 * two * square)
            act = act.astype(BF)
            dz = (dact * slope).astype(BF)
            act_o[rows, :] = act
            dz_o[rows, :] = dz
            acts[cur, rows, :] = act
            dzs[cur, rows, :] = dz

    @pl.when(step == steps // 2)
    def _():
        scatter(me[0], grads[0], out.at[0], out_sem)

    @pl.when(step == steps)
    def _():
        grad_up(steps - 1, 1 - cur)
        grad_down(steps - 1, 1 - cur)
        scatter(me[0], grads[1], out.at[1], out_sem)
        arrive(out, out_sem)


def turn_kernel(n, again, me, dz, dy, x1, vec, *refs):
    if again:
        before, refs = refs[0], refs[3:]
    dx1_o, low_o, sums_o, wu, f_sem = refs[2 * n :]
    span, depth = dy.shape
    step = pl.program_id(0)

    @pl.when(step == 0)
    def _():
        for half in range(2):
            fetch(me[0], refs[half * n : half * n + n], ffn_parts(wu, None, half, depth, True, False), f_sem)
        sums_o[...] = before[...] if again else jnp.zeros_like(sums_o)
        arrive(wu, f_sem)

    parts = [slice(c * TILE, (c + 1) * TILE) for c in range(span // TILE)]
    products = [nt(dz[rows, 0 : 2 * depth], wu[0]) + nt(dz[rows, 2 * depth :], wu[1]) for rows in parts]
    for rows, dh2 in zip(parts, products):
        unit, inv = normed(x1[rows, :])
        grad = dy[rows, :].astype(F32)
        sums_o[G2 : G2 + 1, :] += jnp.sum(dh2 * unit, 0, keepdims=True)
        sums_o[B2 : B2 + 1, :] += jnp.sum(dh2, 0, keepdims=True)
        sums_o[BD : BD + 1, :] += jnp.sum(grad, 0, keepdims=True)
        scaled = dh2 * vec[G2 : G2 + 1, :]
        one = jnp.mean(scaled, -1, keepdims=True)
        two = jnp.mean(scaled * unit, -1, keepdims=True)
        dx1 = grad + inv * (scaled - one - unit * two)
        dx1_o[rows, :] = dx1
        low_o[rows, :] = dx1.astype(BF)


def gates_kernel(n, me, dx1, routes, pr, o, u, *refs):
    da_o, df_o, ds_o, load_o, go_o, w, go, sem = refs[n:]
    span, depth = dx1.shape
    step = pl.program_id(0)

    @pl.when(step == 0)
    def _():
        fetch(me[0], refs[:n], [(depth + 2 * LANES, depth, w)], sem)
        go[...] = jnp.zeros_like(go)
        load_o[...] = jnp.zeros_like(load_o)
        arrive(w, sem)

    lane = iota((TILE, LANES), 1)
    half = lane // 64
    low = lane < 64
    go[...] += nn(u[...].T, dx1[...])
    parts = [slice(c * TILE, (c + 1) * TILE) for c in range(span // TILE)]
    products = [nt(dx1[rows, :], w[...]) for rows in parts]
    for rows, product in zip(parts, products):
        du = product.astype(BF).astype(F32)
        probs = pr[rows, :]
        heads = o[rows, :]
        swap = pltpu.roll(heads, 64, 1)
        dprobs = jnp.zeros((TILE, LANES), F32)
        loads = jnp.zeros((TILE, LANES), F32)
        for slot in range(2):
            expert = pick(routes, rows, slot)
            own = chosen(du, expert, half)
            here = lane == expert
            gate = jnp.sum(jnp.where(here, probs, 0.0), -1, keepdims=True)
            seen = jnp.where(low, heads, swap) if slot == 0 else jnp.where(low, swap, heads)
            dgate = jnp.sum(own * seen, -1, keepdims=True)
            da = (own * gate).astype(BF)
            da_o[slot, rows, :] = da
            df_o[slot, rows, :] = three(lane, jnp.sum(da.astype(F32) * seen, -1, keepdims=True)).astype(BF)
            dprobs = jnp.where(here, dgate, dprobs)
            loads = jnp.where(here, 1.0, loads)
        load_o[0:1, :] += jnp.sum(loads, 0, keepdims=True)
        inner = jnp.sum(dprobs * probs, -1, keepdims=True)
        ds_o[rows, :] = (probs * (dprobs - inner)).astype(BF)

    @pl.when(step == pl.num_programs(0) - 1)
    def _():
        go_o[...] = go[...].astype(BF)


def attend_back_kernel(routes, qa, qf, kx, vx, da, df, *refs):
    dq_o, kv_o, dk, dv, ds, ps = refs[-6:]
    span, depth = dq_o.shape
    step = pl.program_id(0)
    lane = iota((TILE, LANES), 1)
    half = lane // 64

    for slot in range(2):
        own = slice(slot * span, (slot + 1) * span)
        probs = jnp.exp(nt(jnp.concatenate([qa[slot], qf[slot]], 1), kx[...]))
        ps[own, :] = probs.astype(BF)
        away = nt(jnp.concatenate([da[slot], df[slot]], 1), vx[...])
        ds[own, :] = (probs * away).astype(BF)
    dk_part = nn(jnp.concatenate([qa[0].T, qa[1].T], 1), ds[...])
    dv_part = nn(jnp.concatenate([da[0].T, da[1].T], 1), ps[...])
    found = nn(ds[...], kx[:, 0:LANES]) * 0.125
    for c in range(span // TILE):
        rows = slice(c * TILE, (c + 1) * TILE)
        others = slice(span + c * TILE, span + (c + 1) * TILE)
        one, two = pick(routes, rows, 0), pick(routes, rows, 1)
        for j in range(depth // LANES):
            part = jnp.where(one == 2 * j + half, found[rows, :], jnp.where(two == 2 * j + half, found[others, :], 0.0))
            dq_o[rows, j * LANES : (j + 1) * LANES] = part.astype(BF)

    @pl.when(step == 0)
    def _():
        dk[...] = dk_part
        dv[...] = dv_part

    @pl.when(step > 0)
    def _():
        dk[...] += dk_part
        dv[...] += dv_part

    @pl.when(step == pl.num_programs(0) - 1)
    def _():
        for c in range(kv_o.shape[0] // TILE):
            rows = slice(c * TILE, (c + 1) * TILE)
            both = jnp.concatenate([dk[0:64, rows] + dk[64:, rows], dv[0:64, rows] + dv[64:, rows]], 0)
            kv_o[rows, :] = both.T.astype(BF)


def sum_kernel(n, block, experts, me, hid, dq, kv, ds, sums, bias, loads, go, *refs):
    w, gq, gs, all_sums, out, sem, out_sem = refs[2 * n :]
    span, depth = hid.shape
    step = pl.program_id(0)

    @pl.when(step == 0)
    def _():
        fetch(me[0], refs[:n], [(0, depth + 2 * LANES, w)], sem)
        gq[...] = jnp.zeros_like(gq)
        gs[...] = jnp.zeros_like(gs)

    turned = jnp.concatenate([hid[...].T, jnp.ones((16, span), BF)], 0)
    gq[...] += nn(turned, dq[...])
    gs[...] += nn(turned, jnp.concatenate([kv[...], ds[...]], 1))

    @pl.when(step == pl.num_programs(0) - 1)
    def _():
        arrive(w, sem)
        all_sums[...] = jnp.zeros_like(all_sums)
        all_sums[0:32, :] = sums[...]
        all_sums[BU : BU + 4, :] = bias[0:4, :]
        wq = w[:, 0:depth].astype(F32)
        ws = w[:, depth:].astype(F32)
        wide = iota((depth, LANES), 1)
        ws_own = jnp.where(wide < experts, ws[:, LANES:], 0.0)
        around = jnp.sum(gq[0:depth, :] * wq, -1, keepdims=True)
        around += jnp.sum(gs[0:depth, 0:LANES] * ws[:, 0:LANES] + gs[0:depth, LANES:] * ws_own, -1, keepdims=True)
        shift = jnp.sum(gq[depth : depth + 1, :] * wq, -1, keepdims=True)
        shift += jnp.sum(
            gs[depth : depth + 1, 0:LANES] * ws[:, 0:LANES] + gs[depth : depth + 1, LANES:] * ws_own, -1, keepdims=True
        )
        gain = ws[:, LANES + G1 : LANES + G1 + 1]
        lift = ws[:, LANES + B1 : LANES + B1 + 1]
        stretch = (around - lift * shift) / gain
        place = lax.rem(iota((depth, LANES), 0), block)
        load = jnp.sum(jnp.where(wide == place, loads[0:1, :], 0.0), -1, keepdims=True)
        columns = jnp.where(wide < experts, gs[0:depth, LANES:], all_sums[...].T)
        columns = jnp.where(wide == G1, stretch, columns)
        columns = jnp.where(wide == B1, shift, columns)
        columns = jnp.where(wide == LOAD, load, columns)
        out[:, 0:depth] = gq[0:depth, :].astype(BF)
        out[:, depth : 2 * depth] = go[...]
        out[:, 2 * depth : 2 * depth + LANES] = gs[0:depth, 0:LANES].astype(BF)
        out[:, 2 * depth + LANES :] = columns.astype(BF)
        scatter(me[0], refs[n : 2 * n], out, out_sem)
        arrive(out, out_sem)


def result_kernel(n, me, act, x1, vec, *refs):
    res_o, wd, sem = refs[-3:]
    depth = x1.shape[1]

    @pl.when(pl.program_id(0) == 0)
    def _():
        for half in range(2):
            fetch(me[0], refs[half * n : half * n + n], ffn_parts(None, wd, half, depth, False, True), sem)
        arrive(wd, sem)

    res_o[...] = (x1[...] + vec[BD : BD + 1, :] + nn(act[...], wd[...])).astype(BF)


def close_kernel(n, me, dx1, dq, kv, ds, tok, vec, *refs):
    grad_o, w, sem = refs[n:]
    span, depth = tok.shape

    @pl.when(pl.program_id(0) == 0)
    def _():
        fetch(me[0], refs[:n], [(0, depth + 2 * LANES, w)], sem)
        arrive(w, sem)

    parts = [slice(c * TILE, (c + 1) * TILE) for c in range(span // TILE)]
    products = [
        nt(dq[rows, :], w[:, 0:depth]) + nt(jnp.concatenate([kv[rows, :], ds[rows, :]], 1), w[:, depth:]) for rows in parts
    ]
    for rows, dh in zip(parts, products):
        unit, inv = normed(tok[rows, :].astype(F32))
        scaled = dh * vec[G1 : G1 + 1, :]
        one = jnp.mean(scaled, -1, keepdims=True)
        two = jnp.mean(scaled * unit, -1, keepdims=True)
        grad_o[rows, :] = (dx1[rows, :] + inv * (scaled - one - unit * two)).astype(BF)


def finish_kernel(share_of, keep, got, gq, gk, gv, go, gr, g1, b1, g2, b2, bd, bu, load):
    share, depth = gq.shape
    head, experts = gk.shape[1], gr.shape[0]
    total = keep[...].astype(F32) + got[...].astype(F32)
    gq[...] = total[:, 0:depth]
    go[...] = total[:, depth : 2 * depth]
    gk[...] = total[:, 2 * depth : 2 * depth + head]
    gv[...] = total[:, 2 * depth + head : 2 * depth + 2 * head]
    turned = jnp.concatenate([total[:, 2 * depth + LANES :], jnp.zeros((LANES - share, LANES), F32)], 0).T
    gr[...] = turned[0:experts, 0:share]
    for at, out in zip((G1, B1, G2, B2, BD), (g1, b1, g2, b2, bd)):
        out[...] = turned[at : at + 1, 0:share].reshape(share)
    lines = [turned[BU + j : BU + j + 1, 0:share] for j in range(bu.shape[0] // share)]
    bu[...] = jnp.concatenate(lines, 1).reshape(bu.shape[0])
    load[...] = (turned[LOAD : LOAD + 1, 0:experts] * share_of).reshape(experts)


def xor_pairs(count, mask):
    return [(i, i ^ mask) for i in range(count)]


def hops(dp, fsdp):
    inner = fsdp.bit_length() - 1
    along = [1 << bit for bit in range(inner - 1, 1, -1)]
    across = [2] if inner > 1 else []
    rows = [1 << (inner + bit) for bit in range(dp.bit_length() - 1)]
    core = [1] if inner > 0 else []
    return along + across + rows + core, along + rows + across + core


def after(value, *others):
    return lax.optimization_barrier((value, *others))[0]


def move(value, mask, count):
    return lax.ppermute(value, AXES, xor_pairs(count, mask))


def spread(held, have, mask, me, count):
    axis = len([other for other in have if other > mask])
    own = jnp.expand_dims(held, axis)
    got = jnp.expand_dims(move(held, mask, count), axis)
    high = jnp.bitwise_and(me, mask) != 0
    return jnp.where(high, jnp.concatenate([got, own], axis), jnp.concatenate([own, got], axis))


def parted(value, have, mask, me):
    axis = len([other for other in have if other > mask])
    bit = (jnp.bitwise_and(me, mask) != 0).astype(jnp.int32)
    return (
        lax.dynamic_index_in_dim(value, bit, axis, keepdims=False),
        lax.dynamic_index_in_dim(value, 1 - bit, axis, keepdims=False),
    )


def joined(keep, got, dtype=BF):
    return (keep.astype(F32) + got.astype(F32)).astype(dtype)


def shrink(value, have, mask, me, count, dtype=BF):
    keep, send = parted(value, have, mask, me)
    return joined(keep, move(send, mask, count), dtype)


def cost(micros):
    return pl.CostEstimate(flops=int(micros * 1.0e9), bytes_accessed=1024, transcendentals=0)


def on_device(
    sizes, tokens, routes, lengths, ln1_gain, ln1_bias, w_query, w_key, w_value, w_out, w_router,
    ln2_gain, ln2_bias, w_up, b_up, w_down, b_down, cotangent
):
    dp, fsdp = sizes
    count = dp * fsdp
    total, depth = tokens.shape
    rows = lengths.shape[0]
    length = total // rows
    experts, head = w_router.shape[1], w_key.shape[1]
    segs = lengths.shape[1]
    share = w_query.shape[0]
    inner = w_up.shape[1]
    subs = inner // depth
    fast = share % 16 == 0 and fsdp >= 8 and dp >= 2
    first_width = 2 * depth + 2 * LANES
    me = lax.axis_index(AXES).astype(jnp.int32)
    core = (jnp.bitwise_and(me, 1) if fast else jnp.int32(0)).reshape(1)
    packed = (w_query, w_out, w_key, w_value, w_router.T, ln1_gain, ln1_bias, ln2_gain, ln2_bias, b_down, b_up, w_up, w_down)
    small, large = pl.pallas_call(
        pack_kernel,
        out_shape=[
            pltpu.VMEM((share, first_width), BF), pltpu.VMEM((share, 2 * inner), BF),
        ],
        name="pack",
    )(*packed)
    if fast:
        orders = hops(dp, fsdp)
        steps = len(orders[0])
        early = len([m for m in orders[0][:-1] if orders[0].index(m) == orders[1].index(m)])
        blocks, block, n = count // 2, share, 2
        dims = (2,) * (steps - 1)

        def grow(held, order, at):
            return spread(held, order[:at], order[at], me, count)

        def flat(value):
            return value.reshape(blocks, block, value.shape[-1])

        held = small
        for at in range(early):
            held = grow(held, orders[0], at)
            if at == 0:
                big = after(large, held)
        big = grow(big, orders[0], 0)
        parts = [held[..., : first_width // 2], held[..., first_width // 2 :]]
        for at in range(early, steps - 1):
            parts = [grow(part, order, at) for part, order in zip(parts, orders)]
            if at == early:
                for other in range(1, early):
                    big = grow(after(big, *parts), orders[0], other)
        held = flat(jnp.concatenate(parts, -1))
        w_pieces = [held, move(held, orders[0][-1], count)]
        big = [after(half, w_pieces[1]) for half in (big[..., : 4 * depth], big[..., 4 * depth :])]
        pending = list(range(early, steps - 1))
    else:
        blocks, block, n = 1, depth, 1
        w_pieces = [lax.all_gather(small, AXES, axis=0, tiled=True)[None]]
        large = lax.all_gather(large, AXES, axis=0, tiled=True)[None]
        f_pieces = [[large[..., : 4 * depth]], [large[..., 4 * depth :]]]

    smem = pl.BlockSpec(memory_space=pltpu.SMEM)
    hbm = pl.BlockSpec(memory_space=pl.ANY)
    vmem = pl.BlockSpec(memory_space=pltpu.VMEM)
    dma = pltpu.SemaphoreType.DMA

    def whole(dims):
        return pl.BlockSpec(dims, lambda *_: (0,) * len(dims))

    def shape(dims, dtype):
        return jax.ShapeDtypeStruct(dims, dtype)

    def keep_far(value):
        return pltpu.with_memory_space_constraint(value, pltpu.HBM)

    def far(dims, dtype):
        return pltpu.HBM(dims, dtype)

    def call(kernel, name, micros, grid, ins, in_specs, outs, out_specs, scratch):
        return pl.pallas_call(
            kernel, grid=grid, in_specs=in_specs, out_specs=out_specs, out_shape=outs, scratch_shapes=scratch,
            compiler_params=pltpu.CompilerParams(vmem_limit_bytes=ROOM[name] << 20), cost_estimate=cost(micros), name=name,
        )(*ins)

    span = min(STEP, length)
    tiles = total // span
    per_row = length // span

    def tile(wide):
        return pl.BlockSpec((span, wide), lambda t: (t, 0))

    def pair(wide):
        return pl.BlockSpec((2, span, wide), lambda t: (0, t, 0))

    def row_tile(wide):
        return pl.BlockSpec((span, wide), lambda r, t: (r * per_row + t, 0))

    def row_pair(wide):
        return pl.BlockSpec((2, span, wide), lambda r, t: (0, r * per_row + t, 0))

    def by_row(wide):
        return pl.BlockSpec((length, wide), lambda r, t: (r, 0))

    hid, qa, kx, vx, pr, vec = call(
        functools.partial(project_kernel, n, length, segs, experts), "project", 9.0, (tiles,),
        (core, lengths, keep_far(tokens), routes, *w_pieces),
        [smem, smem, tile(depth), tile(2)] + [hbm] * n,
        [
            far((total, depth), BF), shape((2, total, LANES), BF), far((total, 2 * LANES), BF),
            far((total, 2 * LANES), BF), shape((total, LANES), F32), shape((32, depth), F32),
        ],
        [tile(depth), pair(LANES), tile(2 * LANES), tile(2 * LANES), tile(LANES), whole((32, depth))],
        [pltpu.VMEM((depth, depth + 2 * LANES), BF), pltpu.VMEM((LANES, depth), F32), dma],
    )
    if fast:
        big = [grow(half, order, pending[0]) for half, order in zip(big, orders)]
        qa = after(qa, *big)
        big = [after(half, kx) for half in big]
    o, u, qf = call(
        functools.partial(attend_kernel, segs), "attend", 13.0, (rows, per_row),
        (lengths, routes, qa, kx, vx, pr),
        [smem, row_tile(2), row_pair(LANES), by_row(2 * LANES), by_row(2 * LANES), row_tile(LANES)],
        [shape((total, LANES), F32), shape((total, depth), BF), far((2, total, LANES), BF)],
        [row_tile(LANES), row_tile(depth), row_pair(LANES)],
        [],
    )
    if fast:
        for at in pending[1:]:
            big = [grow(half, order, at) for half, order in zip(big, orders)]
        big = [flat(half) for half in big]
        u = after(u, *big)
        big = [after(half, o) for half in big]
        f_pieces = [[half, move(half, orders[0][-1], count)] for half in big]
    x1, h2 = call(
        functools.partial(mix_kernel, n), "mix", 5.0, (tiles,),
        (core, tokens, u, vec, *w_pieces),
        [smem, tile(depth), tile(depth), whole((32, depth))] + [hbm] * n,
        [far((total, depth), F32), shape((total, depth), BF)],
        [tile(depth), tile(depth)],
        [pltpu.VMEM((depth, depth), BF), dma],
    )
    flat_f = [piece for half in f_pieces for piece in half]

    wide = 256

    column = pl.BlockSpec((total, wide), lambda s: (0, jnp.minimum(s, inner // wide - 1)))
    act, dz, bias, *f_grads = call(
        functools.partial(ffn_kernel, n), "feed", 25.0, (inner // wide + 1,),
        (core, h2, cotangent, vec, *flat_f),
        [smem, vmem, vmem, whole((32, depth))] + [hbm] * 2 * n,
        [far((total, inner), BF), far((total, inner), BF), shape((8, depth), F32)]
        + [far((blocks, block, 4 * depth), BF)] * 2 * n,
        [column, column, whole((8, depth))] + [hbm] * 2 * n,
        [
            pltpu.VMEM((2, depth, inner // 2), BF), pltpu.VMEM((inner, depth), BF), pltpu.VMEM((depth + 16, total), BF),
            pltpu.VMEM((depth, total), BF), pltpu.VMEM((2, total, wide), BF), pltpu.VMEM((2, total, wide), BF),
            pltpu.VMEM((2, depth, inner), BF), pltpu.SemaphoreType.DMA((2,)), dma,
        ],
    )
    f_grads = [f_grads[:n], f_grads[n:]]
    def turn(begin, again):
        def part(wide):
            return pl.BlockSpec((span, wide), lambda t: (t + begin, 0))

        return pl.pallas_call(
            functools.partial(turn_kernel, n, len(again) > 0), grid=(tiles // 2,),
            in_specs=[smem, part(inner), part(depth), part(depth), whole((32, depth))]
            + ([whole((32, depth)), hbm, hbm] if again else []) + [hbm] * 2 * n,
            out_specs=[part(depth), part(depth), whole((32, depth))],
            out_shape=[shape((total, depth), F32), shape((total, depth), BF), shape((32, depth), F32)],
            scratch_shapes=[pltpu.VMEM((2, depth, inner // 2), BF), dma],
            input_output_aliases={6: 0, 7: 1} if again else {},
            compiler_params=pltpu.CompilerParams(vmem_limit_bytes=ROOM["turn"] << 20), cost_estimate=cost(6.0), name="turn",
        )(core, keep_far(dz), keep_far(cotangent), keep_far(x1), vec, *again, *flat_f)

    dx1, low, sums = turn(0, ())
    if fast:
        back_orders = [list(reversed(order[:-1])) for order in orders]
        late = back_orders[0]

        def fall(value, order, at, dtype=BF):
            return shrink(value, order[at:], order[at], me, count, dtype)

        acc = [joined(half[0], move(half[1], orders[0][-1], count)).reshape(*dims, block, 4 * depth) for half in f_grads]
        sums = after(sums, *acc)
        acc = [after(a, dx1) for a in acc]
        acc = [fall(a, order, 0) for a, order in zip(acc, back_orders)]
    dx1, low, sums = turn(tiles // 2, (sums, dx1, low))
    da, df, ds, loads, go = call(
        functools.partial(gates_kernel, n), "gates", 9.0, (tiles,),
        (core, low, routes, pr, o, u, *w_pieces),
        [smem, tile(depth), tile(2), tile(LANES), tile(LANES), tile(depth)] + [hbm] * n,
        [
            shape((2, total, LANES), BF), shape((2, total, LANES), BF), shape((total, LANES), BF), shape((8, LANES), F32),
            shape((depth, depth), BF),
        ],
        [pair(LANES), pair(LANES), tile(LANES), whole((8, LANES)), whole((depth, depth))],
        [pltpu.VMEM((depth, depth), BF), pltpu.VMEM((depth, depth), F32), dma],
    )
    if fast:
        da = after(da, *acc)
        acc = [after(a, ds) for a in acc]
        acc = [fall(a, order, 1) for a, order in zip(acc, back_orders)]

    def back(row, again):
        def part(wide):
            return pl.BlockSpec((span, wide), lambda t: (row * per_row + t, 0))

        def both(wide):
            return pl.BlockSpec((2, span, wide), lambda t: (0, row * per_row + t, 0))

        def full(wide):
            return pl.BlockSpec((length, wide), lambda t: (row, 0))

        return pl.pallas_call(
            attend_back_kernel, grid=(per_row,),
            in_specs=[part(2), both(LANES), both(LANES), full(2 * LANES), full(2 * LANES), both(LANES), both(LANES)]
            + [hbm] * len(again),
            out_specs=[part(depth), full(LANES)],
            out_shape=[shape((total, depth), BF), shape((total, LANES), BF)],
            scratch_shapes=[
                pltpu.VMEM((LANES, length), F32), pltpu.VMEM((LANES, length), F32), pltpu.VMEM((2 * span, length), BF),
                pltpu.VMEM((2 * span, length), BF),
            ],
            input_output_aliases={7: 0, 8: 1} if again else {},
            compiler_params=pltpu.CompilerParams(vmem_limit_bytes=ROOM["attend_back"] << 20), cost_estimate=cost(8.0),
            name="attend_back",
        )(routes, qa, qf, kx, vx, da, df, *again)

    dq, kv = back(0, ())
    for row in range(1, rows):
        if fast and row == 1:
            dq = after(dq, *acc)
            acc = jnp.concatenate([after(a, kv) for a in acc], -1)
            acc = fall(acc, late, 2, F32 if len(late) == 3 else BF)
        dq, kv = back(row, (dq, kv))
    if fast:
        kv = after(kv, acc)
        for at in range(3, len(late)):
            acc = fall(after(acc, dq), late, at, F32 if at == len(late) - 1 else BF)
    w_grads = call(
        functools.partial(sum_kernel, n, block, experts), "sums", 6.0, (tiles,),
        (core, hid, dq, kv, ds, sums, bias, loads, go, *w_pieces),
        [
            smem, tile(depth), tile(depth), tile(LANES), tile(LANES), whole((32, depth)), whole((8, depth)),
            whole((8, LANES)), whole((depth, depth)),
        ]
        + [hbm] * n,
        [shape((blocks, block, first_width), BF)] * n,
        [hbm] * n,
        [
            pltpu.VMEM((depth, depth + 2 * LANES), BF), pltpu.VMEM((depth + 16, depth), F32),
            pltpu.VMEM((depth + 16, 2 * LANES), F32), pltpu.VMEM((LANES, depth), F32),
            pltpu.VMEM((depth, first_width), BF), dma, dma,
        ],
    )
    closing = dx1
    if fast:
        tail = joined(w_grads[0], move(w_grads[1], orders[0][-1], count)).reshape(*dims, block, first_width)
        closing = after(dx1, tail, acc)
        tails = [tail[..., : first_width // 2], tail[..., first_width // 2 :]]
        tails = [fall(part, order, 0) for part, order in zip(tails, back_orders)]
    grad_tokens = call(
        functools.partial(close_kernel, n), "close", 6.0, (tiles,),
        (core, closing, dq, kv, ds, tokens, vec, *w_pieces),
        [smem, tile(depth), tile(depth), tile(LANES), tile(LANES), tile(depth), whole((32, depth))] + [hbm] * n,
        [shape((total, depth), BF)],
        [tile(depth)],
        [pltpu.VMEM((depth, depth + 2 * LANES), BF), dma],
    )[0]
    closing = x1
    if fast:
        closing = after(x1, *tails)
        tails = [fall(after(part, grad_tokens), order, 1) for part, order in zip(tails, back_orders)]
    def results(begin, again, x1):
        def part(wide):
            return pl.BlockSpec((span, wide), lambda t: (t + begin, 0))

        return pl.pallas_call(
            functools.partial(result_kernel, n), grid=(tiles // 2,),
            in_specs=[smem, part(inner), part(depth), whole((32, depth))] + [hbm] * 2 * n + [hbm] * len(again),
            out_specs=[part(depth)],
            out_shape=[shape((total, depth), BF)],
            scratch_shapes=[pltpu.VMEM((inner, depth), BF), dma],
            input_output_aliases={4 + 2 * n: 0} if again else {},
            compiler_params=pltpu.CompilerParams(vmem_limit_bytes=ROOM["result"] << 20), cost_estimate=cost(3.5), name="result",
        )(core, act, x1, vec, *flat_f, *again)

    result = results(0, (), closing)
    if fast:
        tail = after(jnp.concatenate(tails, -1), *result)
        tail = fall(tail, late, 2, F32 if len(late) == 3 else BF)
    result = results(tiles // 2, result, closing)[0]

    def unpacked(halves):
        up = jnp.concatenate([half[:, : 2 * depth] for half in halves], 1)
        up = up.reshape(share, subs, count, share).transpose(0, 2, 1, 3).reshape(share, inner)
        down = jnp.concatenate([half[:, 2 * depth :] for half in halves], 1)
        return up, down.reshape(share, subs, depth).transpose(1, 0, 2).reshape(subs * share, depth)

    if fast:
        tail = after(tail, result)
        acc = after(acc, result)
        grad_up, grad_down = unpacked([acc[:, : 4 * depth], acc[:, 4 * depth :]])
        for at in range(3, len(late) - 1):
            tail = fall(tail, late, at)
        keep, send = parted(tail, late[-1:], late[-1], me)
        own = functools.partial(jax.ShapeDtypeStruct, dtype=F32)
        grad_query, grad_key, grad_value, grad_out, grad_router, *lines = pl.pallas_call(
            functools.partial(finish_kernel, 1.0 / (total * count)),
            out_shape=[own((share, depth)), own((share, head)), own((share, head)), own((share, depth)), own((experts, share))]
            + [own((share,))] * 5 + [own((subs * share,)), own((experts,))],
            compiler_params=pltpu.CompilerParams(vmem_limit_bytes=8 << 20),
            name="finish",
        )(keep, move(send, late[-1], count))
        grad_router = grad_router.T
        grad_g1, grad_b1, grad_g2, grad_b2, grad_bd, grad_bu, load = lines
    else:
        def scattered(value):
            return lax.psum_scatter(value[0].astype(F32), AXES, scatter_dimension=0, tiled=True)

        grad_up, grad_down = unpacked([scattered(half[0]) for half in f_grads])
        own_w = scattered(w_grads[0])
        load = lax.psum(w_grads[0][0][:experts, 2 * depth + LANES + LOAD].astype(F32), AXES) / (total * count)
        extra = own_w[:, 2 * depth + LANES :]
        grad_query, grad_out = own_w[:, 0:depth], own_w[:, depth : 2 * depth]
        grad_key, grad_value = own_w[:, 2 * depth : 2 * depth + head], own_w[:, 2 * depth + head : 2 * depth + 2 * head]
        grad_router = extra[:, 0:experts]
        grad_g1, grad_b1, grad_g2, grad_b2, grad_bd = [extra[:, at] for at in (G1, B1, G2, B2, BD)]
        grad_bu = extra[:, BU : BU + subs].T.reshape(subs * share)
    return (
        result, grad_tokens, grad_g1, grad_b1, grad_query, grad_key, grad_value, grad_out, grad_router, grad_g2, grad_b2,
        grad_up, grad_bu, grad_down, grad_bd, load,
    )


def solution(mesh):
    over = P(AXES)
    flat = P(AXES, None)
    sizes = (mesh.shape["dp"], mesh.shape["fsdp"])
    return jax.shard_map(
        functools.partial(on_device, sizes),
        mesh=mesh,
        in_specs=(
            flat, flat, flat, over, over, flat, flat, flat, flat, flat, over, over, flat, over, flat, over, flat,
        ),
        out_specs=(
            flat, flat, over, over, flat, flat, flat, flat, flat, over, over, flat, over, flat, over, P(),
        ),
        check_vma=False,
    )
```

```python
import functools

import jax
import jax.numpy as jnp
from jax import lax
from jax.experimental import pallas as pl
from jax.experimental.pallas import tpu as pltpu
from jax.sharding import PartitionSpec as P

AXES = ("dp", "fsdp")
F32 = jnp.float32
BF = jnp.bfloat16
FAR = -1e30
LANES = 128
G1, B1, G2, B2, BD, BU, LOAD = 8, 9, 10, 11, 12, 13, 17
TILE = 256
STEP = 512
ROOM = {
    "project": 12, "attend": 14, "mix": 10, "feed": 25, "turn": 18, "gates": 12, "attend_back": 28, "sums": 14, "close": 14,
    "result": 18,
}


def nn(left, right):
    return jnp.dot(left, right, preferred_element_type=F32)


def nt(left, right):
    return lax.dot_general(left, right, (((1,), (1,)), ((), ())), preferred_element_type=F32)


def iota(shape, dim):
    return lax.broadcasted_iota(jnp.int32, shape, dim)


def normed(value):
    center = value - jnp.mean(value, -1, keepdims=True)
    inv = lax.rsqrt(jnp.mean(center * center, -1, keepdims=True) + 1e-05)
    return center * inv, inv


def fetch(core, pieces, parts, sem):
    for other, piece in enumerate(pieces):
        own = jnp.bitwise_xor(core, other)
        for start, wide, dst in parts:
            blocks, block, _ = piece.shape
            view = dst.reshape(blocks, len(pieces), block, wide)
            pltpu.make_async_copy(piece.at[:, :, start : start + wide], view.at[:, own], sem).start()


def arrive(dst, sem):
    pltpu.make_async_copy(dst, dst, sem).wait()


def scatter(core, pieces, src, sem):
    for other, piece in enumerate(pieces):
        own = jnp.bitwise_xor(core, other)
        blocks, block, wide = piece.shape
        view = src.reshape(blocks, len(pieces), block, wide)
        pltpu.make_async_copy(view.at[:, own], piece, sem).start()


def ffn_parts(wu, wd, half, depth, up, down):
    parts = []
    if up:
        parts.append((0, 2 * depth, wu.at[half]))
    if down:
        parts += [((2 + j) * depth, depth, wd.at[pl.ds((2 * half + j) * depth, depth), :]) for j in range(2)]
    return parts


def pack_kernel(wq, wo, wk, wv, wr, g1, b1, g2, b2, bd, bu, up, down, o, big_o):
    share, depth = wq.shape
    head, experts = wk.shape[1], wr.shape[0]
    same = iota((share, share), 0) == iota((share, share), 1)
    lane = iota((share, LANES), 1)

    def column(v):
        return jnp.sum(jnp.where(same, jnp.broadcast_to(v.astype(F32), (share, share)), 0.0), 1, keepdims=True)

    out = jnp.zeros((share, LANES), F32)
    for at, v in zip((G1, B1, G2, B2, BD), (g1, b1, g2, b2, bd)):
        out = jnp.where(lane == at, column(v[...].reshape(1, share)), out)
    flat = bu[...].reshape(1, bu.shape[0])
    for j in range(bu.shape[0] // share):
        out = jnp.where(lane == BU + j, column(flat[:, j * share : (j + 1) * share]), out)
    o[:, 0:depth] = wq[...]
    o[:, depth : depth + head] = wk[...]
    o[:, depth + head : depth + LANES] = wv[...]
    o[:, depth + LANES : depth + 2 * LANES] = out.astype(BF)
    o[:, depth + LANES : depth + LANES + experts] = nt(jnp.where(same, 1.0, 0.0).astype(BF), wr[...]).astype(BF)
    o[:, depth + 2 * LANES :] = wo[...]
    subs = bu.shape[0] // share
    wide = subs * LANES
    row, col = iota((wide, wide), 0), iota((wide, wide), 1)
    at = lax.div(lax.rem(row, subs * share), share) * LANES + lax.div(row, subs * share) * share + lax.rem(row, share)
    turn = jnp.where(at == col, 1.0, 0.0).astype(BF)
    for part in range(up.shape[1] // wide):
        moved = nn(up[:, part * wide : (part + 1) * wide], turn).astype(BF)
        for j in range(subs):
            place = (j // 2) * 4 * depth + (j % 2) * depth + part * LANES
            big_o[:, place : place + LANES] = moved[:, j * LANES : (j + 1) * LANES]
    for j in range(subs):
        place = (j // 2) * 4 * depth + (2 + j % 2) * depth
        big_o[:, place : place + depth] = down[j * share : (j + 1) * share, :]


def split3(value):
    high = value.astype(BF).astype(F32)
    rest = value - high
    mid = rest.astype(BF).astype(F32)
    return high, mid, rest - mid


def three(lane, value):
    high, mid, rest = split3(value)
    return jnp.where(lane == 4, -high, jnp.where(lane == 5, -mid, jnp.where(lane == 6, -rest, 0.0)))


def segment_of(lens, row, start, rows):
    place = iota((rows, LANES), 0) + start
    end = lens[row, 0]
    seg = (place >= end).astype(jnp.int32)
    for j in range(1, lens.shape[1]):
        end = end + lens[row, j]
        seg = seg + (place >= end).astype(jnp.int32)
    return seg


def pick(routes, rows, slot):
    return jnp.broadcast_to(routes[rows, slot : slot + 1], (TILE, LANES))


def chosen(wide, expert, half):
    out = jnp.zeros(expert.shape, F32)
    for j in range(wide.shape[1] // LANES):
        out = jnp.where(expert == 2 * j + half, wide[:, j * LANES : (j + 1) * LANES], out)
    return out


def project_kernel(n, length, segs, experts, me, lens, tok, routes, *refs):
    hid_o, qa_o, kx_o, vx_o, pr_o, vec_o, w, vec, sem = refs[n:]
    span, depth = tok.shape
    step = pl.program_id(0)
    row = lax.div(step * span, length)
    begin = lax.rem(step * span, length)

    @pl.when(step == 0)
    def _():
        fetch(me[0], refs[:n], [(0, depth + 2 * LANES, w)], sem)
        arrive(w, sem)
        vec[...] = w[:, depth + LANES :].astype(F32).T
        vec_o[...] = vec[0:32, :]

    lane = iota((TILE, LANES), 1)
    half = lane // 64
    low = lane < 64
    parts = [slice(c * TILE, (c + 1) * TILE) for c in range(span // TILE)]
    for rows in parts:
        unit, _ = normed(tok[rows, :].astype(F32))
        hid_o[rows, :] = (unit * vec[G1 : G1 + 1, :] + vec[B1 : B1 + 1, :]).astype(BF)
    products = [(nn(hid_o[rows, :], w[:, 0:depth]), nn(hid_o[rows, :], w[:, depth:])) for rows in parts]
    for c, rows in enumerate(parts):
        query, small = products[c]
        kv = small[:, :LANES].astype(BF).astype(F32)
        swap = pltpu.roll(kv, 64, 1)
        seg = segment_of(lens, row, begin + c * TILE, TILE)
        same = jnp.where(lane == seg, 1.0, 0.0)
        kx_o[rows, 0:LANES] = jnp.where(low, kv, swap).astype(BF)
        kx_o[rows, LANES:] = jnp.where(lane < segs, same, jnp.where(lane < 8, 1.0, 0.0)).astype(BF)
        vx_o[rows, 0:LANES] = jnp.where(low, swap, kv).astype(BF)
        vx_o[rows, LANES:] = jnp.ones((TILE, LANES), BF)
        logits = jnp.where(lane < experts, small[:, LANES:], FAR)
        raised = jnp.exp(logits - jnp.max(logits, -1, keepdims=True))
        pr_o[rows, :] = raised / jnp.sum(raised, -1, keepdims=True)
        for slot in range(2):
            qa_o[slot, rows, :] = (chosen(query, pick(routes, rows, slot), half) * 0.125).astype(BF)


def attend_kernel(segs, lens, routes, qa, kx, vx, pr, o_o, u_o, qf_o):
    span, depth = u_o.shape
    row, step = pl.program_id(0), pl.program_id(1)
    lane = iota((TILE, LANES), 1)
    half = lane // 64
    low = lane < 64
    for c in range(span // TILE):
        rows = slice(c * TILE, (c + 1) * TILE)
        seg = segment_of(lens, row, step * span + c * TILE, TILE)
        apart = jnp.where((lane < segs) & (lane != seg), FAR, 0.0)
        probs = pr[rows, :]
        seen, gated, experts_of = [], [], []
        for slot in range(2):
            expert = pick(routes, rows, slot)
            scores = nt(jnp.concatenate([qa[slot, rows, :], apart.astype(BF)], 1), kx[...])
            top = jnp.max(scores, -1, keepdims=True)
            raised = jnp.exp(scores - top).astype(BF)
            both = nn(raised, vx[...])
            mass = both[:, LANES:]
            out = both[:, :LANES] / mass
            qf_o[slot, rows, :] = (apart + three(lane, top + jnp.log(mass))).astype(BF)
            gate = jnp.sum(jnp.where(lane == expert, probs, 0.0), -1, keepdims=True)
            seen.append(out)
            gated.append(out * gate)
            experts_of.append(expert)
        o_o[rows, :] = jnp.where(low, seen[0], seen[1])
        for j in range(depth // LANES):
            part = jnp.where(experts_of[0] == 2 * j + half, gated[0], jnp.where(experts_of[1] == 2 * j + half, gated[1], 0.0))
            u_o[rows, j * LANES : (j + 1) * LANES] = part.astype(BF)


def mix_kernel(n, me, tok, u, vec, *refs):
    x1_o, h2_o, w, sem = refs[n:]
    span, depth = tok.shape

    @pl.when(pl.program_id(0) == 0)
    def _():
        fetch(me[0], refs[:n], [(depth + 2 * LANES, depth, w)], sem)
        arrive(w, sem)

    parts = [slice(c * TILE, (c + 1) * TILE) for c in range(span // TILE)]
    products = [nn(u[rows, :], w[...]) for rows in parts]
    for rows, product in zip(parts, products):
        after = tok[rows, :].astype(F32) + product
        x1_o[rows, :] = after
        unit, _ = normed(after)
        h2_o[rows, :] = (unit * vec[G2 : G2 + 1, :] + vec[B2 : B2 + 1, :]).astype(BF)


def ffn_kernel(n, me, h2, dy, vec, *refs):
    pieces = [refs[:n], refs[n : 2 * n]]
    act_o, dz_o, bias_o = refs[2 * n : 2 * n + 3]
    grads = [refs[2 * n + 3 : 3 * n + 3], refs[3 * n + 3 : 4 * n + 3]]
    wu, wd, ht, yt, acts, dzs, out, sem, out_sem = refs[4 * n + 3 :]
    step = pl.program_id(0)
    steps = pl.num_programs(0) - 1
    total, wide = act_o.shape
    depth = h2.shape[1]
    per = depth // wide
    some = wu.shape[2]

    @pl.when(step == 0)
    def _():
        for half in range(2):
            fetch(me[0], pieces[half], ffn_parts(wu, wd, half, depth, True, True), sem.at[half])
        for t in range(0, total, STEP):
            ht[0:depth, t : t + STEP] = h2[t : t + STEP, :].T
            yt[:, t : t + STEP] = dy[t : t + STEP, :].T
        ht[depth:, :] = jnp.ones((16, total), BF)

    for half in range(2):
        @pl.when(step == half * steps // 2)
        def _():
            arrive(wu.at[half], sem.at[half])
            arrive(wd.at[pl.ds(half * some, some), :], sem.at[half])

    one = 0.7978845608028654
    two = one * 0.044715
    cur = lax.rem(step, 2)

    def place(t):
        sub = lax.div(t, per)
        return sub, lax.rem(t, per), lax.rem(sub, 2) * depth, lax.div(sub, 2)

    def grad_up(t, slot):
        sub, part, column, half = place(t)
        up = nn(ht[...], dzs[slot])
        out[half, :, pl.ds(pl.multiple_of(column + part * wide, wide), wide)] = up[0:depth, :].astype(BF)
        bias_o[pl.ds(sub, 1), pl.ds(pl.multiple_of(part * wide, wide), wide)] = up[depth : depth + 1, :]

    def grad_down(t, slot):
        _, part, column, half = place(t)
        rows = pl.ds(pl.multiple_of(part * wide, wide), wide)
        out[half, rows, pl.ds(pl.multiple_of(column + 2 * depth, depth), depth)] = nn(yt[...], acts[slot]).T.astype(BF)

    @pl.when(step < steps)
    def _():
        before = jnp.maximum(step - 1, 0)
        sub, part, column, which = place(step)
        here = pl.ds(pl.multiple_of(step * wide, wide), wide)
        across = pl.ds(pl.multiple_of(column + part * wide, wide), wide)
        bias = vec[pl.ds(BU + sub, 1), pl.ds(pl.multiple_of(part * wide, wide), wide)]
        count = total // TILE
        for c in range(count):
            rows = slice(c * TILE, (c + 1) * TILE)
            z = nn(h2[rows, :], wu[which, :, across]) + bias
            dact = nt(dy[rows, :], wd[here, :])
            if c == 0:
                grad_up(before, 1 - cur)
            if c == count // 2:
                grad_down(before, 1 - cur)
            square = z * z
            tanh = jnp.tanh(z * (one + two * square))
            half = 0.5 * tanh + 0.5
            act = z * half
            slope = half + act * (1.0 - tanh) * (one + 3.0 * two * square)
            act = act.astype(BF)
            dz = (dact * slope).astype(BF)
            act_o[rows, :] = act
            dz_o[rows, :] = dz
            acts[cur, rows, :] = act
            dzs[cur, rows, :] = dz

    @pl.when(step == steps // 2)
    def _():
        scatter(me[0], grads[0], out.at[0], out_sem)

    @pl.when(step == steps)
    def _():
        grad_up(steps - 1, 1 - cur)
        grad_down(steps - 1, 1 - cur)
        scatter(me[0], grads[1], out.at[1], out_sem)
        arrive(out, out_sem)


def turn_kernel(n, again, me, dz, dy, x1, vec, *refs):
    if again:
        before, refs = refs[0], refs[3:]
    dx1_o, low_o, sums_o, wu, f_sem = refs[2 * n :]
    span, depth = dy.shape
    step = pl.program_id(0)

    @pl.when(step == 0)
    def _():
        for half in range(2):
            fetch(me[0], refs[half * n : half * n + n], ffn_parts(wu, None, half, depth, True, False), f_sem)
        sums_o[...] = before[...] if again else jnp.zeros_like(sums_o)
        arrive(wu, f_sem)

    parts = [slice(c * TILE, (c + 1) * TILE) for c in range(span // TILE)]
    products = [nt(dz[rows, 0 : 2 * depth], wu[0]) + nt(dz[rows, 2 * depth :], wu[1]) for rows in parts]
    for rows, dh2 in zip(parts, products):
        unit, inv = normed(x1[rows, :])
        grad = dy[rows, :].astype(F32)
        sums_o[G2 : G2 + 1, :] += jnp.sum(dh2 * unit, 0, keepdims=True)
        sums_o[B2 : B2 + 1, :] += jnp.sum(dh2, 0, keepdims=True)
        sums_o[BD : BD + 1, :] += jnp.sum(grad, 0, keepdims=True)
        scaled = dh2 * vec[G2 : G2 + 1, :]
        one = jnp.mean(scaled, -1, keepdims=True)
        two = jnp.mean(scaled * unit, -1, keepdims=True)
        dx1 = grad + inv * (scaled - one - unit * two)
        dx1_o[rows, :] = dx1
        low_o[rows, :] = dx1.astype(BF)


def gates_kernel(n, me, dx1, routes, pr, o, u, *refs):
    da_o, df_o, ds_o, load_o, go_o, w, go, sem = refs[n:]
    span, depth = dx1.shape
    step = pl.program_id(0)

    @pl.when(step == 0)
    def _():
        fetch(me[0], refs[:n], [(depth + 2 * LANES, depth, w)], sem)
        go[...] = jnp.zeros_like(go)
        load_o[...] = jnp.zeros_like(load_o)
        arrive(w, sem)

    lane = iota((TILE, LANES), 1)
    half = lane // 64
    low = lane < 64
    go[...] += nn(u[...].T, dx1[...])
    parts = [slice(c * TILE, (c + 1) * TILE) for c in range(span // TILE)]
    products = [nt(dx1[rows, :], w[...]) for rows in parts]
    for rows, product in zip(parts, products):
        du = product.astype(BF).astype(F32)
        probs = pr[rows, :]
        heads = o[rows, :]
        swap = pltpu.roll(heads, 64, 1)
        dprobs = jnp.zeros((TILE, LANES), F32)
        loads = jnp.zeros((TILE, LANES), F32)
        for slot in range(2):
            expert = pick(routes, rows, slot)
            own = chosen(du, expert, half)
            here = lane == expert
            gate = jnp.sum(jnp.where(here, probs, 0.0), -1, keepdims=True)
            seen = jnp.where(low, heads, swap) if slot == 0 else jnp.where(low, swap, heads)
            dgate = jnp.sum(own * seen, -1, keepdims=True)
            da = (own * gate).astype(BF)
            da_o[slot, rows, :] = da
            df_o[slot, rows, :] = three(lane, jnp.sum(da.astype(F32) * seen, -1, keepdims=True)).astype(BF)
            dprobs = jnp.where(here, dgate, dprobs)
            loads = jnp.where(here, 1.0, loads)
        load_o[0:1, :] += jnp.sum(loads, 0, keepdims=True)
        inner = jnp.sum(dprobs * probs, -1, keepdims=True)
        ds_o[rows, :] = (probs * (dprobs - inner)).astype(BF)

    @pl.when(step == pl.num_programs(0) - 1)
    def _():
        go_o[...] = go[...].astype(BF)


def attend_back_kernel(routes, qa, qf, kx, vx, da, df, *refs):
    dq_o, kv_o, dk, dv, ds, ps = refs[-6:]
    span, depth = dq_o.shape
    step = pl.program_id(0)
    lane = iota((TILE, LANES), 1)
    half = lane // 64

    for slot in range(2):
        own = slice(slot * span, (slot + 1) * span)
        probs = jnp.exp(nt(jnp.concatenate([qa[slot], qf[slot]], 1), kx[...]))
        ps[own, :] = probs.astype(BF)
        away = nt(jnp.concatenate([da[slot], df[slot]], 1), vx[...])
        ds[own, :] = (probs * away).astype(BF)
    dk_part = nn(jnp.concatenate([qa[0].T, qa[1].T], 1), ds[...])
    dv_part = nn(jnp.concatenate([da[0].T, da[1].T], 1), ps[...])
    found = nn(ds[...], kx[:, 0:LANES]) * 0.125
    for c in range(span // TILE):
        rows = slice(c * TILE, (c + 1) * TILE)
        others = slice(span + c * TILE, span + (c + 1) * TILE)
        one, two = pick(routes, rows, 0), pick(routes, rows, 1)
        for j in range(depth // LANES):
            part = jnp.where(one == 2 * j + half, found[rows, :], jnp.where(two == 2 * j + half, found[others, :], 0.0))
            dq_o[rows, j * LANES : (j + 1) * LANES] = part.astype(BF)

    @pl.when(step == 0)
    def _():
        dk[...] = dk_part
        dv[...] = dv_part

    @pl.when(step > 0)
    def _():
        dk[...] += dk_part
        dv[...] += dv_part

    @pl.when(step == pl.num_programs(0) - 1)
    def _():
        for c in range(kv_o.shape[0] // TILE):
            rows = slice(c * TILE, (c + 1) * TILE)
            both = jnp.concatenate([dk[0:64, rows] + dk[64:, rows], dv[0:64, rows] + dv[64:, rows]], 0)
            kv_o[rows, :] = both.T.astype(BF)


def sum_kernel(n, block, experts, me, hid, dq, kv, ds, sums, bias, loads, go, *refs):
    w, gq, gs, all_sums, out, sem, out_sem = refs[2 * n :]
    span, depth = hid.shape
    step = pl.program_id(0)

    @pl.when(step == 0)
    def _():
        fetch(me[0], refs[:n], [(0, depth + 2 * LANES, w)], sem)
        gq[...] = jnp.zeros_like(gq)
        gs[...] = jnp.zeros_like(gs)

    turned = jnp.concatenate([hid[...].T, jnp.ones((16, span), BF)], 0)
    gq[...] += nn(turned, dq[...])
    gs[...] += nn(turned, jnp.concatenate([kv[...], ds[...]], 1))

    @pl.when(step == pl.num_programs(0) - 1)
    def _():
        arrive(w, sem)
        all_sums[...] = jnp.zeros_like(all_sums)
        all_sums[0:32, :] = sums[...]
        all_sums[BU : BU + 4, :] = bias[0:4, :]
        wq = w[:, 0:depth].astype(F32)
        ws = w[:, depth:].astype(F32)
        wide = iota((depth, LANES), 1)
        ws_own = jnp.where(wide < experts, ws[:, LANES:], 0.0)
        around = jnp.sum(gq[0:depth, :] * wq, -1, keepdims=True)
        around += jnp.sum(gs[0:depth, 0:LANES] * ws[:, 0:LANES] + gs[0:depth, LANES:] * ws_own, -1, keepdims=True)
        shift = jnp.sum(gq[depth : depth + 1, :] * wq, -1, keepdims=True)
        shift += jnp.sum(
            gs[depth : depth + 1, 0:LANES] * ws[:, 0:LANES] + gs[depth : depth + 1, LANES:] * ws_own, -1, keepdims=True
        )
        gain = ws[:, LANES + G1 : LANES + G1 + 1]
        lift = ws[:, LANES + B1 : LANES + B1 + 1]
        stretch = (around - lift * shift) / gain
        place = lax.rem(iota((depth, LANES), 0), block)
        load = jnp.sum(jnp.where(wide == place, loads[0:1, :], 0.0), -1, keepdims=True)
        columns = jnp.where(wide < experts, gs[0:depth, LANES:], all_sums[...].T)
        columns = jnp.where(wide == G1, stretch, columns)
        columns = jnp.where(wide == B1, shift, columns)
        columns = jnp.where(wide == LOAD, load, columns)
        out[:, 0:depth] = gq[0:depth, :].astype(BF)
        out[:, depth : 2 * depth] = go[...]
        out[:, 2 * depth : 2 * depth + LANES] = gs[0:depth, 0:LANES].astype(BF)
        out[:, 2 * depth + LANES :] = columns.astype(BF)
        scatter(me[0], refs[n : 2 * n], out, out_sem)
        arrive(out, out_sem)


def result_kernel(n, me, act, x1, vec, *refs):
    res_o, wd, sem = refs[-3:]
    depth = x1.shape[1]

    @pl.when(pl.program_id(0) == 0)
    def _():
        for half in range(2):
            fetch(me[0], refs[half * n : half * n + n], ffn_parts(None, wd, half, depth, False, True), sem)
        arrive(wd, sem)

    res_o[...] = (x1[...] + vec[BD : BD + 1, :] + nn(act[...], wd[...])).astype(BF)


def close_kernel(n, me, dx1, dq, kv, ds, tok, vec, *refs):
    grad_o, w, sem = refs[n:]
    span, depth = tok.shape

    @pl.when(pl.program_id(0) == 0)
    def _():
        fetch(me[0], refs[:n], [(0, depth + 2 * LANES, w)], sem)
        arrive(w, sem)

    parts = [slice(c * TILE, (c + 1) * TILE) for c in range(span // TILE)]
    products = [
        nt(dq[rows, :], w[:, 0:depth]) + nt(jnp.concatenate([kv[rows, :], ds[rows, :]], 1), w[:, depth:]) for rows in parts
    ]
    for rows, dh in zip(parts, products):
        unit, inv = normed(tok[rows, :].astype(F32))
        scaled = dh * vec[G1 : G1 + 1, :]
        one = jnp.mean(scaled, -1, keepdims=True)
        two = jnp.mean(scaled * unit, -1, keepdims=True)
        grad_o[rows, :] = (dx1[rows, :] + inv * (scaled - one - unit * two)).astype(BF)


def finish_kernel(share_of, keep, got, gq, gk, gv, go, gr, g1, b1, g2, b2, bd, bu, load):
    share, depth = gq.shape
    head, experts = gk.shape[1], gr.shape[0]
    total = keep[...].astype(F32) + got[...].astype(F32)
    gq[...] = total[:, 0:depth]
    go[...] = total[:, depth : 2 * depth]
    gk[...] = total[:, 2 * depth : 2 * depth + head]
    gv[...] = total[:, 2 * depth + head : 2 * depth + 2 * head]
    turned = jnp.concatenate([total[:, 2 * depth + LANES :], jnp.zeros((LANES - share, LANES), F32)], 0).T
    gr[...] = turned[0:experts, 0:share]
    for at, out in zip((G1, B1, G2, B2, BD), (g1, b1, g2, b2, bd)):
        out[...] = turned[at : at + 1, 0:share].reshape(share)
    lines = [turned[BU + j : BU + j + 1, 0:share] for j in range(bu.shape[0] // share)]
    bu[...] = jnp.concatenate(lines, 1).reshape(bu.shape[0])
    load[...] = (turned[LOAD : LOAD + 1, 0:experts] * share_of).reshape(experts)


def xor_pairs(count, mask):
    return [(i, i ^ mask) for i in range(count)]


def hops(dp, fsdp):
    inner = fsdp.bit_length() - 1
    along = [1 << bit for bit in range(inner - 1, 1, -1)]
    across = [2] if inner > 1 else []
    rows = [1 << (inner + bit) for bit in range(dp.bit_length() - 1)]
    core = [1] if inner > 0 else []
    return along + across + rows + core, along + rows + across + core


def after(value, *others):
    return lax.optimization_barrier((value, *others))[0]


def move(value, mask, count):
    return lax.ppermute(value, AXES, xor_pairs(count, mask))


def spread(held, have, mask, me, count):
    axis = len([other for other in have if other > mask])
    own = jnp.expand_dims(held, axis)
    got = jnp.expand_dims(move(held, mask, count), axis)
    high = jnp.bitwise_and(me, mask) != 0
    return jnp.where(high, jnp.concatenate([got, own], axis), jnp.concatenate([own, got], axis))


def parted(value, have, mask, me):
    axis = len([other for other in have if other > mask])
    bit = (jnp.bitwise_and(me, mask) != 0).astype(jnp.int32)
    return (
        lax.dynamic_index_in_dim(value, bit, axis, keepdims=False),
        lax.dynamic_index_in_dim(value, 1 - bit, axis, keepdims=False),
    )


def joined(keep, got, dtype=BF):
    return (keep.astype(F32) + got.astype(F32)).astype(dtype)


def shrink(value, have, mask, me, count, dtype=BF):
    keep, send = parted(value, have, mask, me)
    return joined(keep, move(send, mask, count), dtype)


def cost(micros):
    return pl.CostEstimate(flops=int(micros * 1.0e9), bytes_accessed=1024, transcendentals=0)


def on_device(
    sizes, tokens, routes, lengths, ln1_gain, ln1_bias, w_query, w_key, w_value, w_out, w_router,
    ln2_gain, ln2_bias, w_up, b_up, w_down, b_down, cotangent
):
    dp, fsdp = sizes
    count = dp * fsdp
    total, depth = tokens.shape
    rows = lengths.shape[0]
    length = total // rows
    experts, head = w_router.shape[1], w_key.shape[1]
    segs = lengths.shape[1]
    share = w_query.shape[0]
    inner = w_up.shape[1]
    subs = inner // depth
    fast = share % 16 == 0 and fsdp >= 8 and dp >= 2
    first_width = 2 * depth + 2 * LANES
    me = lax.axis_index(AXES).astype(jnp.int32)
    core = (jnp.bitwise_and(me, 1) if fast else jnp.int32(0)).reshape(1)
    packed = (w_query, w_out, w_key, w_value, w_router.T, ln1_gain, ln1_bias, ln2_gain, ln2_bias, b_down, b_up, w_up, w_down)
    small, large = pl.pallas_call(
        pack_kernel,
        out_shape=[
            pltpu.VMEM((share, first_width), BF), pltpu.VMEM((share, 2 * inner), BF),
        ],
        name="pack",
    )(*packed)
    if fast:
        orders = hops(dp, fsdp)
        steps = len(orders[0])
        early = len([m for m in orders[0][:-1] if orders[0].index(m) == orders[1].index(m)])
        blocks, block, n = count // 2, share, 2
        dims = (2,) * (steps - 1)

        def grow(held, order, at):
            return spread(held, order[:at], order[at], me, count)

        def flat(value):
            return value.reshape(blocks, block, value.shape[-1])

        held = small
        for at in range(early):
            held = grow(held, orders[0], at)
            if at == 0:
                big = after(large, held)
        big = grow(big, orders[0], 0)
        parts = [held[..., : first_width // 2], held[..., first_width // 2 :]]
        for at in range(early, steps - 1):
            parts = [grow(part, order, at) for part, order in zip(parts, orders)]
            if at == early:
                for other in range(1, early):
                    big = grow(after(big, *parts), orders[0], other)
        held = flat(jnp.concatenate(parts, -1))
        w_pieces = [held, move(held, orders[0][-1], count)]
        big = [after(half, w_pieces[1]) for half in (big[..., : 4 * depth], big[..., 4 * depth :])]
        pending = list(range(early, steps - 1))
    else:
        blocks, block, n = 1, depth, 1
        w_pieces = [lax.all_gather(small, AXES, axis=0, tiled=True)[None]]
        large = lax.all_gather(large, AXES, axis=0, tiled=True)[None]
        f_pieces = [[large[..., : 4 * depth]], [large[..., 4 * depth :]]]

    smem = pl.BlockSpec(memory_space=pltpu.SMEM)
    hbm = pl.BlockSpec(memory_space=pl.ANY)
    vmem = pl.BlockSpec(memory_space=pltpu.VMEM)
    dma = pltpu.SemaphoreType.DMA

    def whole(dims):
        return pl.BlockSpec(dims, lambda *_: (0,) * len(dims))

    def shape(dims, dtype):
        return jax.ShapeDtypeStruct(dims, dtype)

    def keep_far(value):
        return pltpu.with_memory_space_constraint(value, pltpu.HBM)

    def far(dims, dtype):
        return pltpu.HBM(dims, dtype)

    def call(kernel, name, micros, grid, ins, in_specs, outs, out_specs, scratch):
        return pl.pallas_call(
            kernel, grid=grid, in_specs=in_specs, out_specs=out_specs, out_shape=outs, scratch_shapes=scratch,
            compiler_params=pltpu.CompilerParams(vmem_limit_bytes=ROOM[name] << 20), cost_estimate=cost(micros), name=name,
        )(*ins)

    span = min(STEP, length)
    tiles = total // span
    per_row = length // span

    def tile(wide):
        return pl.BlockSpec((span, wide), lambda t: (t, 0))

    def pair(wide):
        return pl.BlockSpec((2, span, wide), lambda t: (0, t, 0))

    def row_tile(wide):
        return pl.BlockSpec((span, wide), lambda r, t: (r * per_row + t, 0))

    def row_pair(wide):
        return pl.BlockSpec((2, span, wide), lambda r, t: (0, r * per_row + t, 0))

    def by_row(wide):
        return pl.BlockSpec((length, wide), lambda r, t: (r, 0))

    hid, qa, kx, vx, pr, vec = call(
        functools.partial(project_kernel, n, length, segs, experts), "project", 9.0, (tiles,),
        (core, lengths, keep_far(tokens), routes, *w_pieces),
        [smem, smem, tile(depth), tile(2)] + [hbm] * n,
        [
            far((total, depth), BF), shape((2, total, LANES), BF), far((total, 2 * LANES), BF),
            far((total, 2 * LANES), BF), shape((total, LANES), F32), shape((32, depth), F32),
        ],
        [tile(depth), pair(LANES), tile(2 * LANES), tile(2 * LANES), tile(LANES), whole((32, depth))],
        [pltpu.VMEM((depth, depth + 2 * LANES), BF), pltpu.VMEM((LANES, depth), F32), dma],
    )
    if fast:
        big = [grow(half, order, pending[0]) for half, order in zip(big, orders)]
        qa = after(qa, *big)
        big = [after(half, kx) for half in big]
    o, u, qf = call(
        functools.partial(attend_kernel, segs), "attend", 13.0, (rows, per_row),
        (lengths, routes, qa, kx, vx, pr),
        [smem, row_tile(2), row_pair(LANES), by_row(2 * LANES), by_row(2 * LANES), row_tile(LANES)],
        [shape((total, LANES), F32), shape((total, depth), BF), far((2, total, LANES), BF)],
        [row_tile(LANES), row_tile(depth), row_pair(LANES)],
        [],
    )
    if fast:
        for at in pending[1:]:
            big = [grow(half, order, at) for half, order in zip(big, orders)]
        big = [flat(half) for half in big]
        u = after(u, *big)
        big = [after(half, o) for half in big]
        f_pieces = [[half, move(half, orders[0][-1], count)] for half in big]
    x1, h2 = call(
        functools.partial(mix_kernel, n), "mix", 5.0, (tiles,),
        (core, tokens, u, vec, *w_pieces),
        [smem, tile(depth), tile(depth), whole((32, depth))] + [hbm] * n,
        [far((total, depth), F32), shape((total, depth), BF)],
        [tile(depth), tile(depth)],
        [pltpu.VMEM((depth, depth), BF), dma],
    )
    flat_f = [piece for half in f_pieces for piece in half]

    wide = 256

    column = pl.BlockSpec((total, wide), lambda s: (0, jnp.minimum(s, inner // wide - 1)))
    act, dz, bias, *f_grads = call(
        functools.partial(ffn_kernel, n), "feed", 25.0, (inner // wide + 1,),
        (core, h2, cotangent, vec, *flat_f),
        [smem, vmem, vmem, whole((32, depth))] + [hbm] * 2 * n,
        [far((total, inner), BF), far((total, inner), BF), shape((8, depth), F32)]
        + [far((blocks, block, 4 * depth), BF)] * 2 * n,
        [column, column, whole((8, depth))] + [hbm] * 2 * n,
        [
            pltpu.VMEM((2, depth, inner // 2), BF), pltpu.VMEM((inner, depth), BF), pltpu.VMEM((depth + 16, total), BF),
            pltpu.VMEM((depth, total), BF), pltpu.VMEM((2, total, wide), BF), pltpu.VMEM((2, total, wide), BF),
            pltpu.VMEM((2, depth, inner), BF), pltpu.SemaphoreType.DMA((2,)), dma,
        ],
    )
    f_grads = [f_grads[:n], f_grads[n:]]
    def turn(begin, again):
        def part(wide):
            return pl.BlockSpec((span, wide), lambda t: (t + begin, 0))

        return pl.pallas_call(
            functools.partial(turn_kernel, n, len(again) > 0), grid=(tiles // 2,),
            in_specs=[smem, part(inner), part(depth), part(depth), whole((32, depth))]
            + ([whole((32, depth)), hbm, hbm] if again else []) + [hbm] * 2 * n,
            out_specs=[part(depth), part(depth), whole((32, depth))],
            out_shape=[shape((total, depth), F32), shape((total, depth), BF), shape((32, depth), F32)],
            scratch_shapes=[pltpu.VMEM((2, depth, inner // 2), BF), dma],
            input_output_aliases={6: 0, 7: 1} if again else {},
            compiler_params=pltpu.CompilerParams(vmem_limit_bytes=ROOM["turn"] << 20), cost_estimate=cost(6.0), name="turn",
        )(core, keep_far(dz), keep_far(cotangent), keep_far(x1), vec, *again, *flat_f)

    dx1, low, sums = turn(0, ())
    if fast:
        back_orders = [list(reversed(order[:-1])) for order in orders]
        late = back_orders[0]

        def fall(value, order, at, dtype=BF):
            return shrink(value, order[at:], order[at], me, count, dtype)

        acc = [joined(half[0], move(half[1], orders[0][-1], count)).reshape(*dims, block, 4 * depth) for half in f_grads]
        sums = after(sums, *acc)
        acc = [after(a, dx1) for a in acc]
        acc = [fall(a, order, 0) for a, order in zip(acc, back_orders)]
    dx1, low, sums = turn(tiles // 2, (sums, dx1, low))
    da, df, ds, loads, go = call(
        functools.partial(gates_kernel, n), "gates", 9.0, (tiles,),
        (core, low, routes, pr, o, u, *w_pieces),
        [smem, tile(depth), tile(2), tile(LANES), tile(LANES), tile(depth)] + [hbm] * n,
        [
            shape((2, total, LANES), BF), shape((2, total, LANES), BF), shape((total, LANES), BF), shape((8, LANES), F32),
            shape((depth, depth), BF),
        ],
        [pair(LANES), pair(LANES), tile(LANES), whole((8, LANES)), whole((depth, depth))],
        [pltpu.VMEM((depth, depth), BF), pltpu.VMEM((depth, depth), F32), dma],
    )
    if fast:
        da = after(da, *acc)
        acc = [after(a, ds) for a in acc]
        acc = [fall(a, order, 1) for a, order in zip(acc, back_orders)]

    def back(row, again):
        def part(wide):
            return pl.BlockSpec((span, wide), lambda t: (row * per_row + t, 0))

        def both(wide):
            return pl.BlockSpec((2, span, wide), lambda t: (0, row * per_row + t, 0))

        def full(wide):
            return pl.BlockSpec((length, wide), lambda t: (row, 0))

        return pl.pallas_call(
            attend_back_kernel, grid=(per_row,),
            in_specs=[part(2), both(LANES), both(LANES), full(2 * LANES), full(2 * LANES), both(LANES), both(LANES)]
            + [hbm] * len(again),
            out_specs=[part(depth), full(LANES)],
            out_shape=[shape((total, depth), BF), shape((total, LANES), BF)],
            scratch_shapes=[
                pltpu.VMEM((LANES, length), F32), pltpu.VMEM((LANES, length), F32), pltpu.VMEM((2 * span, length), BF),
                pltpu.VMEM((2 * span, length), BF),
            ],
            input_output_aliases={7: 0, 8: 1} if again else {},
            compiler_params=pltpu.CompilerParams(vmem_limit_bytes=ROOM["attend_back"] << 20), cost_estimate=cost(8.0),
            name="attend_back",
        )(routes, qa, qf, kx, vx, da, df, *again)

    dq, kv = back(0, ())
    for row in range(1, rows):
        if fast and row == 1:
            dq = after(dq, *acc)
            acc = jnp.concatenate([after(a, kv) for a in acc], -1)
            acc = fall(acc, late, 2, F32 if len(late) == 3 else BF)
        dq, kv = back(row, (dq, kv))
    if fast:
        kv = after(kv, acc)
        for at in range(3, len(late)):
            acc = fall(after(acc, dq), late, at, F32 if at == len(late) - 1 else BF)
    w_grads = call(
        functools.partial(sum_kernel, n, block, experts), "sums", 6.0, (tiles,),
        (core, hid, dq, kv, ds, sums, bias, loads, go, *w_pieces),
        [
            smem, tile(depth), tile(depth), tile(LANES), tile(LANES), whole((32, depth)), whole((8, depth)),
            whole((8, LANES)), whole((depth, depth)),
        ]
        + [hbm] * n,
        [shape((blocks, block, first_width), BF)] * n,
        [hbm] * n,
        [
            pltpu.VMEM((depth, depth + 2 * LANES), BF), pltpu.VMEM((depth + 16, depth), F32),
            pltpu.VMEM((depth + 16, 2 * LANES), F32), pltpu.VMEM((LANES, depth), F32),
            pltpu.VMEM((depth, first_width), BF), dma, dma,
        ],
    )
    closing = dx1
    if fast:
        tail = joined(w_grads[0], move(w_grads[1], orders[0][-1], count)).reshape(*dims, block, first_width)
        closing = after(dx1, tail)
        tails = [tail[..., : first_width // 2], tail[..., first_width // 2 :]]
        tails = [fall(part, order, 0) for part, order in zip(tails, back_orders)]
    grad_tokens = call(
        functools.partial(close_kernel, n), "close", 6.0, (tiles,),
        (core, closing, dq, kv, ds, tokens, vec, *w_pieces),
        [smem, tile(depth), tile(depth), tile(LANES), tile(LANES), tile(depth), whole((32, depth))] + [hbm] * n,
        [shape((total, depth), BF)],
        [tile(depth)],
        [pltpu.VMEM((depth, depth + 2 * LANES), BF), dma],
    )[0]
    closing = x1
    if fast:
        closing = after(x1, *tails)
        tails = [fall(after(part, grad_tokens), order, 1) for part, order in zip(tails, back_orders)]
    def results(begin, again, x1):
        def part(wide):
            return pl.BlockSpec((span, wide), lambda t: (t + begin, 0))

        return pl.pallas_call(
            functools.partial(result_kernel, n), grid=(tiles // 2,),
            in_specs=[smem, part(inner), part(depth), whole((32, depth))] + [hbm] * 2 * n + [hbm] * len(again),
            out_specs=[part(depth)],
            out_shape=[shape((total, depth), BF)],
            scratch_shapes=[pltpu.VMEM((inner, depth), BF), dma],
            input_output_aliases={4 + 2 * n: 0} if again else {},
            compiler_params=pltpu.CompilerParams(vmem_limit_bytes=ROOM["result"] << 20), cost_estimate=cost(3.5), name="result",
        )(core, act, x1, vec, *flat_f, *again)

    result = results(0, (), closing)
    if fast:
        tail = after(jnp.concatenate(tails, -1), *result)
        tail = fall(tail, late, 2, F32 if len(late) == 3 else BF)
    result = results(tiles // 2, result, closing)[0]

    def unpacked(halves):
        up = jnp.concatenate([half[:, : 2 * depth] for half in halves], 1)
        up = up.reshape(share, subs, count, share).transpose(0, 2, 1, 3).reshape(share, inner)
        down = jnp.concatenate([half[:, 2 * depth :] for half in halves], 1)
        return up, down.reshape(share, subs, depth).transpose(1, 0, 2).reshape(subs * share, depth)

    if fast:
        tail = after(tail, result)
        acc = after(acc, result)
        grad_up, grad_down = unpacked([acc[:, : 4 * depth], acc[:, 4 * depth :]])
        for at in range(3, len(late) - 1):
            tail = fall(tail, late, at)
        keep, send = parted(tail, late[-1:], late[-1], me)
        own = functools.partial(jax.ShapeDtypeStruct, dtype=F32)
        grad_query, grad_key, grad_value, grad_out, grad_router, *lines = pl.pallas_call(
            functools.partial(finish_kernel, 1.0 / (total * count)),
            out_shape=[own((share, depth)), own((share, head)), own((share, head)), own((share, depth)), own((experts, share))]
            + [own((share,))] * 5 + [own((subs * share,)), own((experts,))],
            compiler_params=pltpu.CompilerParams(vmem_limit_bytes=8 << 20),
            name="finish",
        )(keep, move(send, late[-1], count))
        grad_router = grad_router.T
        grad_g1, grad_b1, grad_g2, grad_b2, grad_bd, grad_bu, load = lines
    else:
        def scattered(value):
            return lax.psum_scatter(value[0].astype(F32), AXES, scatter_dimension=0, tiled=True)

        grad_up, grad_down = unpacked([scattered(half[0]) for half in f_grads])
        own_w = scattered(w_grads[0])
        load = lax.psum(w_grads[0][0][:experts, 2 * depth + LANES + LOAD].astype(F32), AXES) / (total * count)
        extra = own_w[:, 2 * depth + LANES :]
        grad_query, grad_out = own_w[:, 0:depth], own_w[:, depth : 2 * depth]
        grad_key, grad_value = own_w[:, 2 * depth : 2 * depth + head], own_w[:, 2 * depth + head : 2 * depth + 2 * head]
        grad_router = extra[:, 0:experts]
        grad_g1, grad_b1, grad_g2, grad_b2, grad_bd = [extra[:, at] for at in (G1, B1, G2, B2, BD)]
        grad_bu = extra[:, BU : BU + subs].T.reshape(subs * share)
    return (
        result, grad_tokens, grad_g1, grad_b1, grad_query, grad_key, grad_value, grad_out, grad_router, grad_g2, grad_b2,
        grad_up, grad_bu, grad_down, grad_bd, load,
    )


def solution(mesh):
    over = P(AXES)
    flat = P(AXES, None)
    sizes = (mesh.shape["dp"], mesh.shape["fsdp"])
    return jax.shard_map(
        functools.partial(on_device, sizes),
        mesh=mesh,
        in_specs=(
            flat, flat, flat, over, over, flat, flat, flat, flat, flat, over, over, flat, over, flat, over, flat,
        ),
        out_specs=(
            flat, flat, over, over, flat, flat, flat, flat, flat, over, over, flat, over, flat, over, P(),
        ),
        check_vma=False,
    )
```
